256 devices in a mesh: orient: 64 (over x, y_hi, z), dom: 4 (over y_lo, core).
Axes of the slice: x: 4, y: 4 (y_hi: 2, y_lo: 2; y = y_hi * 2 + y_lo), z: 8, core: 2. Of those that a mesh axis runs over, the one named last changes fastest.
Arguments:
- images: bfloat16 [256, 2, 4096], P(('orient', 'dom')), may hold values from -6 to 6
- offsets: int32 [256, 9, 2], P(('orient', 'dom')), may hold values from -5 to 5, as said below
- groups: int32 [256], P(('orient', 'dom')), may hold values from 0 to 7
- defocus: int32 [256], P(('orient', 'dom')), may hold values from 0 to 63
- refs: bfloat16 [8192, 2, 4096], P('orient'), may hold values from -2 to 2
- log_prior: float32 [8192], P('orient'), may hold values from -4 to 4
- noise_inv: float32 [8, 4096], replicated, may hold values from 0.030029297 to 0.12011719
- ctf_table: float32 [64, 4096], replicated, may hold values from 0.05 to 1
Outputs:
- data_sum: float32 [8192, 2, 4096], P('orient', None, 'dom')
- weight_sum: float32 [8192, 4096], P('orient', 'dom')
- evidence: float32 [256], P(('orient', 'dom'))
The draws below stay inside these ranges and needn't reach their ends.
Inputs may be any that keep to these rules, and one draw needn't show every extreme that they name: offsets[i, t] = centre[i] + (2 (t mod 3) - 2, 2 (t // 3) - 2) for one centre of each particle.
All inputs are finite; a program needn't handle non-finite values.
Results may differ from the reference program's by a relative error of at most 0.025.
Values may be sent and summed in bfloat16 or wider, within the bound.
No kernel may reach another device: no remote copies, remote signals or barrier semaphores. Data moves between devices by JAX's collectives and lax.ppermute only.
A program may use at most 64 MiB of HBM per device.

```python
import math
import jax
import jax.numpy as jnp
from jax import lax

SIDE = 64
PIX = 4096
REFS = 8192
TRANS = 9
NGROUPS = 8
NDEF = 64
PARTICLES = 256


def draw_centres(key):
    centre = jax.random.randint(jax.random.fold_in(key, 11), (PARTICLES, 2), -3, 4).astype(jnp.int32)
    centre = centre.at[0].set(jnp.array([-3, -3], jnp.int32))
    return centre.at[1].set(jnp.array([3, 3], jnp.int32))


def ref_base(key):
    shape = (REFS, 2, PIX)
    base = 0.5 * jnp.clip(jax.random.normal(jax.random.fold_in(key, 21), shape, jnp.float32), -4.0, 4.0)
    return base


def draw_offsets(key, part):
    centre = draw_centres(key)
    step = jnp.arange(TRANS, dtype=jnp.int32)
    grid_x = 2 * (step % 3) - 2
    grid_y = 2 * (step // 3) - 2
    return jnp.stack([centre[:, 0:1] + grid_x[None, :], centre[:, 1:2] + grid_y[None, :]], axis=2).astype(jnp.int32)


def draw_refs(key, part):
    return ref_base(key).astype(jnp.bfloat16)


def draw_images(key, part):
    shape = (PARTICLES, 2, PIX)
    base = jnp.clip(jax.random.normal(jax.random.fold_in(key, 31), shape, jnp.float32), -6.0, 6.0)
    return base.astype(jnp.bfloat16)


def touch_ends(result, own_key, low, top_value):
    longest = result.shape.index(max(result.shape))
    spots = []
    for shift in (0, 1):
        where = [jax.random.randint(jax.random.fold_in(own_key, axis), (), 0, length) for axis, length in enumerate(result.shape)]
        where[longest] = (where[longest] + shift) % result.shape[longest]
        spots.append(tuple(where))
    return result.at[spots[0]].set(low).at[spots[1]].set(top_value)


def shard_levels(key, extent, pieces, low, largest):
    def one(position, parts):
        heights = jax.random.uniform(jax.random.fold_in(jax.random.fold_in(key, 6), position), (parts,), jnp.float32, low / len(pieces), largest / len(pieces))
        return jnp.repeat(jnp.exp(heights), extent[position] // parts).reshape((-1,) + (1,) * (len(extent) - position - 1))

    loudness = one(*pieces[0])
    for cut in pieces[1:]:
        loudness = loudness * one(*cut)
    return loudness


def centred(stream_key, shape, deviation, bound, shards=(), kind=jnp.bfloat16):
    loudness = shard_levels(stream_key, shape, shards, -0.22, 0.18) if shards else 1.0
    values = jax.random.normal(stream_key, shape, jnp.float32) * deviation * loudness
    return jnp.minimum(jnp.maximum(values, -bound), bound).astype(kind)


def setup_inputs(seed: int = 0) -> dict:
    key_list = jax.random.split(jax.random.key(seed), 9)
    return {
        "images": draw_images(jax.random.fold_in(key_list[8], 71), 0),
        "offsets": draw_offsets(jax.random.fold_in(key_list[8], 71), 0),
        "groups": touch_ends(jax.random.randint(key_list[2], (PARTICLES,), 0, NGROUPS), jax.random.fold_in(key_list[2], 1), 0, NGROUPS - 1).astype(jnp.int32),
        "defocus": touch_ends(jax.random.randint(key_list[3], (PARTICLES,), 0, NDEF), jax.random.fold_in(key_list[3], 1), 0, NDEF - 1).astype(jnp.int32),
        "refs": draw_refs(jax.random.fold_in(key_list[8], 71), 0),
        "log_prior": centred(key_list[5], (REFS,), 1.0, 4.0, ((0, 64),), jnp.float32),
        "noise_inv": jnp.clip(jnp.exp(jax.random.uniform(key_list[6], (NGROUPS, PIX), jnp.float32, math.log(0.030029297), math.log(0.12011719))), 0.030029297, 0.12011719),
        "ctf_table": jnp.clip(jax.random.uniform(key_list[7], (NDEF, PIX), jnp.float32, 0.05, 1.0), 0.05, 1.0),
    }


TWO_PI = 2.0 * math.pi
TRANS_VAR = 8.0


def frequencies(first, count):
    pixel = first + jnp.arange(count, dtype=jnp.int32)
    half = SIDE // 2
    return (pixel % SIDE + half) % SIDE - half, (pixel // SIDE + half) % SIDE - half


def shifted(weighted, shift_x, shift_y, freq_x, freq_y):
    turns = (shift_x[:, None] * freq_x[None, :] + shift_y[:, None] * freq_y[None, :]) % SIDE
    angle = turns.astype(jnp.float32) * (TWO_PI / SIDE)
    cosine = jnp.cos(angle)
    sine = jnp.sin(angle)
    real_part = weighted[:, 0].astype(jnp.float32)
    imag_part = weighted[:, 1].astype(jnp.float32)
    new_real = real_part * cosine + imag_part * sine
    new_imag = imag_part * cosine - real_part * sine
    return jnp.concatenate([new_real, new_imag], axis=1).astype(jnp.bfloat16)


def reference(images, offsets, groups, defocus, refs, log_prior, noise_inv, ctf_table):
    block_rows = 32
    freq_x, freq_y = frequencies(0, PIX)
    ref_wide = refs.reshape(REFS, 2 * PIX).astype(jnp.float32)
    real_ref = refs[:, 0].astype(jnp.float32)
    imag_ref = refs[:, 1].astype(jnp.float32)
    power = (real_ref * real_ref + imag_ref * imag_ref).astype(jnp.bfloat16).astype(jnp.float32)
    scale = 25.0 * REFS / PARTICLES

    def one_block(carry, index):
        data_total, weight_total = carry
        start = (index * block_rows).astype(jnp.int32)
        image = lax.dynamic_slice_in_dim(images, start, block_rows, 0)
        shift = lax.dynamic_slice_in_dim(offsets, start, block_rows, 0)
        group = lax.dynamic_slice_in_dim(groups, start, block_rows, 0)
        focus = lax.dynamic_slice_in_dim(defocus, start, block_rows, 0)
        noise_row = noise_inv[group]
        ctf_row = ctf_table[focus]
        product = noise_row * ctf_row
        weighted = (image.astype(jnp.float32) * product[:, None, :]).astype(jnp.bfloat16)
        ctf_power = (product * ctf_row).astype(jnp.bfloat16).astype(jnp.float32)
        self_term = jnp.dot(ctf_power, power.T)
        moved = jnp.stack([shifted(weighted, shift[:, t, 0], shift[:, t, 1], freq_x, freq_y) for t in range(TRANS)])
        moved_wide = moved.astype(jnp.float32)
        cross = jnp.einsum("tbk,rk->tbr", moved_wide, ref_wide)
        shift_x = shift[:, :, 0]
        shift_y = shift[:, :, 1]
        prior = -((shift_x * shift_x + shift_y * shift_y).astype(jnp.float32) / (2.0 * TRANS_VAR))
        score = cross - 0.5 * self_term[None, :, :] + prior.T[:, :, None] + log_prior[None, None, :]
        top = jnp.max(score, axis=(0, 2))
        total = jnp.sum(jnp.exp(score - top[None, :, None]), axis=(0, 2))
        evidence = top + jnp.log(total)
        post = jnp.exp(score - evidence[None, :, None]).astype(jnp.bfloat16)
        post_wide = post.astype(jnp.float32)
        post_sum = jnp.sum(post_wide, axis=0).astype(jnp.bfloat16).astype(jnp.float32)
        data_total = data_total + jnp.einsum("tbr,tbk->rk", post_wide, moved_wide)
        weight_total = weight_total + jnp.dot(post_sum.T, ctf_power)
        return (data_total, weight_total), evidence

    start_carry = (jnp.zeros((REFS, 2 * PIX), jnp.float32), jnp.zeros((REFS, PIX), jnp.float32))
    (data_total, weight_total), evidence = lax.scan(one_block, start_carry, jnp.arange(PARTICLES // block_rows, dtype=jnp.int32))
    data_sum = (data_total * scale).reshape(REFS, 2, PIX)
    weight_sum = weight_total * scale
    return data_sum, weight_sum, evidence.reshape(PARTICLES)
```

```python
import functools
import math

import jax
import jax.numpy as jnp
import numpy as np
from jax import lax
from jax.experimental import pallas as pl
from jax.experimental.pallas import tpu as pltpu
from jax.sharding import Mesh
from jax.sharding import PartitionSpec as P

SIDE = 64
PIX = SIDE * SIDE
QUART = PIX // 4
META = 128
WIDE = QUART + META
DEFS = 64
GROUPS = 8
TWO_PI = 2.0 * math.pi
TRANS_VAR = 8.0
F32 = jnp.float32
BF16 = jnp.bfloat16
NT = (((1,), (1,)), ((), ()))
NN = (((1,), (0,)), ((), ()))
VMEM_LIMIT = 48 * 1024 * 1024


def phase_rows():
    pixel = np.arange(PIX)
    freq_x = (pixel % SIDE + 32) % SIDE - 32
    freq_y = (pixel // SIDE + 32) % SIDE - 32
    turn_x = (2 * freq_x) % SIDE * (TWO_PI / SIDE)
    turn_y = (2 * freq_y) % SIDE * (TWO_PI / SIDE)
    rows = [np.cos(turn_x), np.sin(turn_x), np.cos(turn_y), np.sin(turn_y)]
    return np.concatenate([np.stack(rows), np.zeros((4, PIX))]).astype(np.float32)


def params():
    return pltpu.CompilerParams(vmem_limit_bytes=VMEM_LIMIT)


def prep_kernel(codes, image_ref, noise_ref, ctf_ref, out_ref):
    group, focus, centre_x, centre_y = codes[0], codes[1], codes[2], codes[3]
    rows = lax.broadcasted_iota(jnp.int32, (8, PIX), 0)
    noise = jnp.sum(jnp.where(rows == group, noise_ref[...], 0.0), axis=0, keepdims=True)
    ctf = jnp.sum(jnp.where(rows == focus % 8, ctf_ref[...], 0.0), axis=0, keepdims=True)
    weighted = (image_ref[0].astype(F32) * (noise * ctf)).astype(BF16).astype(F32)
    real = jnp.concatenate([weighted[0:1, j * QUART : (j + 1) * QUART] for j in range(4)], axis=0)
    imag = jnp.concatenate([weighted[1:2, j * QUART : (j + 1) * QUART] for j in range(4)], axis=0)
    lane = lax.broadcasted_iota(jnp.int32, (4, QUART), 1)
    row = lax.broadcasted_iota(jnp.int32, (4, QUART), 0)
    freq_x = ((lane & 63) + 32 & 63) - 32
    freq_y = ((row * (QUART // SIDE) + (lane >> 6)) + 32 & 63) - 32
    angle = ((freq_x * centre_x + freq_y * centre_y) & 63).astype(F32) * (TWO_PI / SIDE)
    cosine = jnp.cos(angle)
    sine = jnp.sin(angle)
    body = jnp.concatenate([real * cosine + imag * sine, imag * cosine - real * sine], axis=0)
    spot = lax.broadcasted_iota(jnp.int32, (8, META), 1)
    meta = jnp.where(
        spot == 0,
        group,
        jnp.where(spot == 1, focus, jnp.where(spot == 2, centre_x, jnp.where(spot == 3, centre_y, 0))),
    ).astype(F32)
    one = jnp.concatenate([body, meta], axis=1)
    pair = jnp.concatenate([one, one], axis=0).astype(BF16)
    for k in range(out_ref.shape[0] // 16):
        out_ref[16 * k : 16 * (k + 1), :] = pair


def refs_kernel(real_ref, imag_ref, trig_ref, ctf_ref, noise_ref, turned_ref, power_ref, ctf3_ref, noise3_ref):
    real = real_ref[...].astype(F32)
    imag = imag_ref[...].astype(F32)
    count = real.shape[0]
    cosine = trig_ref[2:3, :]
    sine = trig_ref[3:4, :]
    rc, rs, ic, si = real * cosine, real * sine, imag * cosine, imag * sine
    turned_ref[0, 0:count, :] = (rc + si).astype(BF16)
    turned_ref[1, 0:count, :] = (ic - rs).astype(BF16)
    turned_ref[0, count : 2 * count, :] = real_ref[...]
    turned_ref[1, count : 2 * count, :] = imag_ref[...]
    turned_ref[0, 2 * count : 3 * count, :] = (rc - si).astype(BF16)
    turned_ref[1, 2 * count : 3 * count, :] = (ic + rs).astype(BF16)
    power_ref[...] = (real * real + imag * imag).astype(BF16)

    def split(table):
        first = table.astype(BF16)
        rest = table - first.astype(F32)
        second = rest.astype(BF16)
        third = (rest - second.astype(F32)).astype(BF16)
        return first, second, third

    ctf3_ref[...] = jnp.concatenate(split(ctf_ref[...]), axis=0)
    parts = [part.astype(F32) for part in split(noise_ref[...])]
    noise3_ref[...] = jnp.concatenate(parts + [jnp.zeros_like(parts[0])], axis=0).astype(BF16)


def ctf_power_rows(meta, ctf3, noise3):
    count = meta.shape[0]
    spot = lax.broadcasted_iota(jnp.int32, (count, 3 * DEFS), 1) % DEFS
    pick_ctf = (spot == meta[:, 1:2].astype(jnp.int32)).astype(BF16)
    spot = lax.broadcasted_iota(jnp.int32, (count, 4 * GROUPS), 1) % GROUPS
    pick_noise = (spot == meta[:, 0:1].astype(jnp.int32)).astype(BF16)
    ctf = lax.dot_general(pick_ctf, ctf3, NN, preferred_element_type=F32)
    noise = lax.dot_general(pick_noise, noise3, NN, preferred_element_type=F32)
    return (noise * ctf * ctf).astype(BF16)


def shift_x(real, imag, cosine, sine):
    rc, rs, ic, si = real * cosine, real * sine, imag * cosine, imag * sine
    new_real = jnp.concatenate([rc - si, real, rc + si], axis=0).astype(BF16)
    new_imag = jnp.concatenate([ic + rs, imag, ic - rs], axis=0).astype(BF16)
    return new_real, new_imag


def score_kernel(
    place, near_ref, far_ref, turned_ref, power_ref, ctf3_ref, noise3_ref, trig_ref, prior_ref,
    q0_ref, q1_ref, q2_ref, q3_ref, stats_ref, wide_ref, cross_ref, self_ref,
):
    step = pl.program_id(0)
    y_hi = place[0]
    dom = place[1]
    half = near_ref.shape[0]
    count = 2 * half // 8
    refs = power_ref.shape[0]

    @pl.when(step == 0)
    def _():
        for part, spot in ((near_ref, y_hi), (far_ref, 1 - y_hi)):
            for tile in range(WIDE // 128):
                start = pl.multiple_of(2 * half * tile + spot * half, half)
                wide_ref[pl.ds(start, half), :] = part[:, 128 * tile : 128 * (tile + 1)].astype(F32)
        cross_ref[...] = jnp.zeros_like(cross_ref)
        self_ref[...] = jnp.zeros_like(self_ref)

    def pick(row, tile):
        return wide_ref[pl.ds(2 * half * tile + row, count, stride=8), :]

    meta = pick(0, QUART // 128)
    real = jnp.concatenate([pick(step, tile) for tile in range(QUART // 128)], axis=1)
    imag = jnp.concatenate([pick(step + 4, tile) for tile in range(QUART // 128)], axis=1)
    both = jnp.concatenate([meta, meta], axis=0).astype(BF16)
    quarter = jnp.concatenate([real, imag], axis=0).astype(BF16)
    outs = (q0_ref, q1_ref, q2_ref, q3_ref)
    for k in range(4):

        @pl.when((step ^ dom) == k)
        def _(k=k):
            outs[k][:, 0:QUART] = quarter
            outs[k][:, QUART:WIDE] = both

    new_real, new_imag = shift_x(real, imag, trig_ref[0:1, :], trig_ref[1:2, :])
    cross_ref[...] += lax.dot_general(
        new_real, turned_ref[0], NT, preferred_element_type=F32
    ) + lax.dot_general(new_imag, turned_ref[1], NT, preferred_element_type=F32)
    ctf_power = ctf_power_rows(meta, ctf3_ref[...], noise3_ref[...])
    self_ref[...] += lax.dot_general(ctf_power, power_ref[...], NT, preferred_element_type=F32)

    @pl.when(step == 3)
    def _():
        base = prior_ref[...] - 0.5 * self_ref[...]
        centre_x = meta[:, 2:3]
        centre_y = meta[:, 3:4]
        scores = {}
        top = None
        for a in range(3):
            for b in range(3):
                off_x = centre_x + (2.0 * a - 2.0)
                off_y = centre_y + (2.0 * b - 2.0)
                value = (
                    cross_ref[a * count : (a + 1) * count, b * refs : (b + 1) * refs]
                    + base
                    - (off_x * off_x + off_y * off_y) / (2.0 * TRANS_VAR)
                )
                scores[a, b] = value
                top = value if top is None else jnp.maximum(top, value)
        top = jnp.max(top, axis=1, keepdims=True)
        mass = jnp.zeros((count, refs), F32)
        probs = []
        for a in range(3):
            row = []
            for b in range(3):
                value = jnp.exp(scores[a, b] - top)
                mass = mass + value
                row.append(value)
            probs.append(jnp.concatenate(row, axis=1).astype(BF16))
        total = top + jnp.log(jnp.sum(mass, axis=1, keepdims=True))
        first = jnp.concatenate(probs[0:2], axis=0)
        empty = jnp.zeros((count, 2 * refs), BF16)
        low = jnp.concatenate([probs[2][:, 0 : 2 * refs], jnp.concatenate([probs[2][:, 2 * refs :], empty[:, 0:refs]], axis=1)], axis=0)
        for k in range(4):
            outs[k][:, WIDE : WIDE + 3 * refs] = first
            outs[k][:, WIDE + 3 * refs : WIDE + 5 * refs] = low
        lane = lax.broadcasted_iota(jnp.int32, (count, 2 * count), 1)
        line = lax.broadcasted_iota(jnp.int32, (count, 2 * count), 0)
        spread = jnp.where(lane == line, total, 0.0) + jnp.where(lane == line + count, top, 0.0)
        stats_ref[...] = jnp.broadcast_to(jnp.sum(spread, axis=0, keepdims=True), stats_ref.shape)


def final_kernel(
    place, q0_ref, q1_ref, q2_ref, q3_ref, stats_ref, ctf3_ref, noise3_ref, trig_ref,
    data_ref, weight_ref, evidence_ref, post_ref, sum_ref, meta_ref, *, scale,
):
    step = pl.program_id(0)
    dom = place[1]
    orient = place[2]
    mine = place[3]
    quarters = (q0_ref, q1_ref, q2_ref, q3_ref)
    count = q0_ref.shape[0] // 2
    refs = sum_ref.shape[0]
    doms = 4

    @pl.when(step == 0)
    def _():
        lane = lax.broadcasted_iota(jnp.int32, (count, 2 * count), 1)
        line = lax.broadcasted_iota(jnp.int32, (count, 2 * count), 0)
        for k in range(doms):
            group = dom ^ k
            table = stats_ref[pl.ds(group, stats_ref.shape[0] // doms, stride=doms), :]
            top = jnp.max(table, axis=0, keepdims=True)
            evidence = top + jnp.log(jnp.sum(jnp.exp(table - top), axis=0, keepdims=True))
            own = stats_ref[pl.ds(orient * doms + group, 1), :]
            evidence_col = jnp.sum(jnp.where(lane == line, evidence, 0.0), axis=1, keepdims=True)
            top_col = jnp.sum(jnp.where(lane == line + count, own, 0.0), axis=1, keepdims=True)
            factor = jnp.exp(top_col - evidence_col)
            if k == 0:
                spot = lax.broadcasted_iota(jnp.int32, evidence.shape, 1)
                value = jnp.sum(jnp.where(spot == mine, evidence, 0.0), axis=1, keepdims=True)
                evidence_ref[...] = jnp.broadcast_to(value, evidence_ref.shape)
            meta_ref[k * count : (k + 1) * count, :] = quarters[k][0:count, QUART:WIDE].astype(F32)
            first = quarters[k][:, WIDE : WIDE + 3 * refs].astype(F32)
            low = quarters[k][:, WIDE + 3 * refs : WIDE + 5 * refs].astype(F32)
            rows = [
                first[0:count],
                first[count : 2 * count],
                jnp.concatenate([low[0:count], low[count : 2 * count, 0:refs]], axis=1),
            ]
            total = jnp.zeros((count, refs), F32)
            for a in range(3):
                post = (rows[a] * factor).astype(BF16).astype(F32)
                spot = (a * doms + k) * count
                for b in range(3):
                    part = post[:, b * refs : (b + 1) * refs]
                    total = total + part
                    post_ref[b * refs : (b + 1) * refs, spot : spot + count] = part.T.astype(BF16)
            sum_ref[:, k * count : (k + 1) * count] = total.T.astype(BF16)

    cos_x, sin_x = trig_ref[0:1, :], trig_ref[1:2, :]
    real = jnp.concatenate([quarters[k][0:count, pl.ds(pl.multiple_of(step * cos_x.shape[1], 128), cos_x.shape[1])] for k in range(doms)], axis=0)
    imag = jnp.concatenate([quarters[k][count : 2 * count, pl.ds(pl.multiple_of(step * cos_x.shape[1], 128), cos_x.shape[1])] for k in range(doms)], axis=0)
    new_real, new_imag = shift_x(real.astype(F32), imag.astype(F32), cos_x, sin_x)
    sums_real = lax.dot_general(post_ref[...], new_real, NN, preferred_element_type=F32)
    sums_imag = lax.dot_general(post_ref[...], new_imag, NN, preferred_element_type=F32)
    r0, r1, r2 = (sums_real[b * refs : (b + 1) * refs] for b in range(3))
    i0, i1, i2 = (sums_imag[b * refs : (b + 1) * refs] for b in range(3))
    cos_y, sin_y = trig_ref[2:3, :] * scale, trig_ref[3:4, :] * scale
    data_ref[0] = r1 * scale + (r0 + r2) * cos_y + (i2 - i0) * sin_y
    data_ref[1] = i1 * scale + (i0 + i2) * cos_y + (r0 - r2) * sin_y
    ctf_power = ctf_power_rows(meta_ref[...], ctf3_ref[...], noise3_ref[...])
    weight_ref[...] = lax.dot_general(sum_ref[...], ctf_power, NN, preferred_element_type=F32) * scale


def on_device(images, offsets, groups, defocus, refs, log_prior, noise_inv, ctf_table):
    count_refs = refs.shape[0]
    size = {name: lax.axis_size(name) for name in ("x", "yh", "z", "yl", "c")}
    orients = size["x"] * size["yh"] * size["z"]
    devices = orients * size["yl"] * size["c"]
    spread = size["x"] * size["z"]
    group = orients
    scale = 25.0 * (count_refs * orients) / devices
    trig = jnp.asarray(phase_rows())
    pos_x, pos_yh, pos_z = lax.axis_index("x"), lax.axis_index("yh"), lax.axis_index("z")
    dom = lax.axis_index("yl") * size["c"] + lax.axis_index("c")
    orient = (pos_x * size["yh"] + pos_yh) * size["z"] + pos_z
    mine = (pos_yh * size["x"] + pos_x) * size["z"] + pos_z
    place = jnp.stack([pos_yh, dom, orient, mine]).astype(jnp.int32)
    codes = jnp.concatenate([groups, defocus, offsets[0, 4]])

    whole = lambda shape: pl.BlockSpec(shape, lambda *_: (0,) * len(shape))
    payload = pl.pallas_call(
        prep_kernel,
        grid_spec=pltpu.PrefetchScalarGridSpec(
            num_scalar_prefetch=1,
            grid=(1,),
            in_specs=[
                whole((1, 2, PIX)),
                whole((GROUPS, PIX)),
                pl.BlockSpec((8, PIX), lambda s, c: (c[1] // 8, 0)),
            ],
            out_specs=whole((8 * spread, WIDE)),
        ),
        out_shape=jax.ShapeDtypeStruct((8 * spread, WIDE), BF16),
        compiler_params=params(),
        name="prep",
    )(codes, images, noise_inv, ctf_table)
    near = lax.all_to_all(payload, ("x", "z"), 0, 0, tiled=True)
    far = lax.ppermute(near, "yh", [(0, 1), (1, 0)])

    flat = refs.reshape(count_refs, 2 * PIX)
    turned, power, ctf3, noise3 = pl.pallas_call(
        refs_kernel,
        grid=(4,),
        in_specs=[
            pl.BlockSpec((count_refs, QUART), lambda j: (0, j)),
            pl.BlockSpec((count_refs, QUART), lambda j: (0, j + 4)),
            pl.BlockSpec((8, QUART), lambda j: (0, j)),
            pl.BlockSpec((DEFS, QUART), lambda j: (0, j)),
            pl.BlockSpec((GROUPS, QUART), lambda j: (0, j)),
        ],
        out_specs=[
            pl.BlockSpec((2, 3 * count_refs, QUART), lambda j: (0, 0, j)),
            pl.BlockSpec((count_refs, QUART), lambda j: (0, j)),
            pl.BlockSpec((3 * DEFS, QUART), lambda j: (0, j)),
            pl.BlockSpec((4 * GROUPS, QUART), lambda j: (0, j)),
        ],
        out_shape=[
            jax.ShapeDtypeStruct((2, 3 * count_refs, PIX), BF16),
            jax.ShapeDtypeStruct((count_refs, PIX), BF16),
            jax.ShapeDtypeStruct((3 * DEFS, PIX), BF16),
            jax.ShapeDtypeStruct((4 * GROUPS, PIX), BF16),
        ],
        compiler_params=params(),
        name="turn_refs",
    )(flat, flat, trig, ctf_table, noise_inv)

    box = (2 * group, WIDE + 5 * count_refs)
    *quarters, stats = pl.pallas_call(
        score_kernel,
        grid_spec=pltpu.PrefetchScalarGridSpec(
            num_scalar_prefetch=1,
            grid=(4,),
            in_specs=[
                whole((8 * spread, WIDE)),
                whole((8 * spread, WIDE)),
                pl.BlockSpec((2, 3 * count_refs, QUART), lambda j, s: (0, 0, j)),
                pl.BlockSpec((count_refs, QUART), lambda j, s: (0, j)),
                pl.BlockSpec((3 * DEFS, QUART), lambda j, s: (0, j)),
                pl.BlockSpec((4 * GROUPS, QUART), lambda j, s: (0, j)),
                pl.BlockSpec((8, QUART), lambda j, s: (0, j)),
                whole((1, count_refs)),
            ],
            out_specs=[whole(box)] * 4 + [whole((devices, 2 * group))],
            scratch_shapes=[
                pltpu.VMEM((16 * spread * (WIDE // 128), 128), F32),
                pltpu.VMEM((3 * group, 3 * count_refs), F32),
                pltpu.VMEM((group, count_refs), F32),
            ],
        ),
        out_shape=[jax.ShapeDtypeStruct(box, BF16)] * 4
        + [jax.ShapeDtypeStruct((devices, 2 * group), F32)],
        compiler_params=params(),
        name="score",
    )(place, near, far, turned, power, ctf3, noise3, trig, log_prior[None, :])

    moved = [quarters[0]]
    for k in range(1, 4):
        moved.append(lax.ppermute(quarters[k], ("yl", "c"), [(d, d ^ k) for d in range(4)]))
    stats_all = lax.all_to_all(stats, ("x", "yh", "z", "yl", "c"), 0, 0, tiled=True)

    chunk = QUART // 4
    data, weight, evidence = pl.pallas_call(
        functools.partial(final_kernel, scale=scale),
        grid_spec=pltpu.PrefetchScalarGridSpec(
            num_scalar_prefetch=1,
            grid=(4,),
            in_specs=[whole(box)] * 4
            + [
                whole((devices, 2 * group)),
                pl.BlockSpec((3 * DEFS, chunk), lambda n, s: (0, s[1] * 4 + n)),
                pl.BlockSpec((4 * GROUPS, chunk), lambda n, s: (0, s[1] * 4 + n)),
                pl.BlockSpec((8, chunk), lambda n, s: (0, s[1] * 4 + n)),
            ],
            out_specs=[
                pl.BlockSpec((2, count_refs, chunk), lambda n, s: (0, 0, n)),
                pl.BlockSpec((count_refs, chunk), lambda n, s: (0, n)),
                whole((8, 128)),
            ],
            scratch_shapes=[
                pltpu.VMEM((3 * count_refs, 12 * group), BF16),
                pltpu.VMEM((count_refs, 4 * group), BF16),
                pltpu.VMEM((4 * group, META), F32),
            ],
        ),
        out_shape=[
            jax.ShapeDtypeStruct((2, count_refs, QUART), F32),
            jax.ShapeDtypeStruct((count_refs, QUART), F32),
            jax.ShapeDtypeStruct((8, 128), F32),
        ],
        compiler_params=params(),
        name="insert",
    )(place, *moved, stats_all, ctf3, noise3, trig)
    return jnp.transpose(data, (1, 0, 2)), weight, evidence[0, 0:1]


def solution(mesh):
    fine = Mesh(mesh.devices.reshape(4, 2, 8, 2, 2), ("x", "yh", "z", "yl", "c"))
    orient = ("x", "yh", "z")
    dom = ("yl", "c")
    every = orient + dom
    return jax.shard_map(
        on_device,
        mesh=fine,
        in_specs=(
            P(every, None, None),
            P(every, None, None),
            P(every),
            P(every),
            P(orient, None, None),
            P(orient),
            P(),
            P(),
        ),
        out_specs=(P(orient, None, dom), P(orient, dom), P(every)),
        check_vma=False,
    )
```

```python
import functools
import math

import jax
import jax.numpy as jnp
import numpy as np
from jax import lax
from jax.experimental import pallas as pl
from jax.experimental.pallas import tpu as pltpu
from jax.sharding import Mesh
from jax.sharding import PartitionSpec as P

SIDE = 64
PIX = SIDE * SIDE
QUART = PIX // 4
META = 128
WIDE = QUART + META
DEFS = 64
GROUPS = 8
TWO_PI = 2.0 * math.pi
TRANS_VAR = 8.0
F32 = jnp.float32
BF16 = jnp.bfloat16
NT = (((1,), (1,)), ((), ()))
NN = (((1,), (0,)), ((), ()))
AXES = ("x", "yh", "zh", "zl", "yl", "c")
VMEM_LIMIT = 24 * 1024 * 1024
VMEM_ALL = 61 * 1024 * 1024


def phase_rows():
    pixel = np.arange(PIX)
    freq_x = (pixel % SIDE + 32) % SIDE - 32
    freq_y = (pixel // SIDE + 32) % SIDE - 32
    turn_x = (2 * freq_x) % SIDE * (TWO_PI / SIDE)
    turn_y = (2 * freq_y) % SIDE * (TWO_PI / SIDE)
    rows = [np.cos(turn_x), np.sin(turn_x), np.cos(turn_y), np.sin(turn_y)]
    return np.concatenate([np.stack(rows), np.zeros((4, PIX))]).astype(np.float32)


def params(limit=VMEM_LIMIT):
    return pltpu.CompilerParams(vmem_limit_bytes=limit)


def prep_kernel(
    offsets, groups, defocus, image_hbm, noise_hbm, ctf_hbm, out_ref, image_ref, noise_ref, ctf_ref, sems
):
    group, focus, centre_x, centre_y = groups[0], defocus[0], offsets[0, 4], offsets[1, 4]
    start = pl.multiple_of(focus // 8 * 8, 8)
    copies = [
        pltpu.make_async_copy(ctf_hbm.at[pl.ds(start, 8)], ctf_ref, sems.at[0]),
        pltpu.make_async_copy(noise_hbm, noise_ref, sems.at[1]),
        pltpu.make_async_copy(image_hbm, image_ref, sems.at[2]),
    ]
    for copy in copies:
        copy.start()
    lane = lax.broadcasted_iota(jnp.int32, (4, QUART), 1)
    row = lax.broadcasted_iota(jnp.int32, (4, QUART), 0)
    freq_x = ((lane & 63) + 32 & 63) - 32
    freq_y = ((row * (QUART // SIDE) + (lane >> 6)) + 32 & 63) - 32
    angle = ((freq_x * centre_x + freq_y * centre_y) & 63).astype(F32) * (TWO_PI / SIDE)
    cosine = jnp.cos(angle)
    sine = jnp.sin(angle)
    spot = lax.broadcasted_iota(jnp.int32, (8, META), 1)
    meta = jnp.where(
        spot == 0,
        group,
        jnp.where(spot == 1, focus, jnp.where(spot == 2, centre_x, jnp.where(spot == 3, centre_y, 0))),
    ).astype(F32)
    for copy in copies:
        copy.wait()
    rows = lax.broadcasted_iota(jnp.int32, (8, PIX), 0)
    noise = jnp.sum(jnp.where(rows == group, noise_ref[...], 0.0), axis=0, keepdims=True)
    ctf = jnp.sum(jnp.where(rows == focus % 8, ctf_ref[...], 0.0), axis=0, keepdims=True)
    weighted = (image_ref[0].astype(F32) * (noise * ctf)).astype(BF16).astype(F32)
    real = jnp.concatenate([weighted[0:1, j * QUART : (j + 1) * QUART] for j in range(4)], axis=0)
    imag = jnp.concatenate([weighted[1:2, j * QUART : (j + 1) * QUART] for j in range(4)], axis=0)
    body = jnp.concatenate([real * cosine + imag * sine, imag * cosine - real * sine], axis=0)
    one = jnp.concatenate([body, meta], axis=1)
    pair = jnp.concatenate([one, one], axis=0).astype(BF16)
    for k in range(out_ref.shape[0] // 16):
        out_ref[16 * k : 16 * (k + 1), :] = pair


def refs_kernel(
    flat_ref, trig_ref, ctf_ref, noise_ref, prior_ref, turned_ref, power_ref, ctf3_ref, noise3_ref, column_ref
):
    count = flat_ref.shape[0]
    width = 256

    def split(table):
        first = table.astype(BF16)
        rest = table - first.astype(F32)
        second = rest.astype(BF16)
        third = (rest - second.astype(F32)).astype(BF16)
        return first, second, third

    def body(step, carry):
        at = pl.ds(pl.multiple_of(step * width, width), width)
        low = flat_ref[:, at]
        high = flat_ref[:, pl.ds(pl.multiple_of(PIX + step * width, width), width)]
        real = low.astype(F32)
        imag = high.astype(F32)
        cosine = trig_ref[2:3, at]
        sine = trig_ref[3:4, at]
        rc, rs, ic, si = real * cosine, real * sine, imag * cosine, imag * sine
        turned_ref[0, 0:count, at] = (rc + si).astype(BF16)
        turned_ref[1, 0:count, at] = (ic - rs).astype(BF16)
        turned_ref[0, count : 2 * count, at] = low
        turned_ref[1, count : 2 * count, at] = high
        turned_ref[0, 2 * count : 3 * count, at] = (rc - si).astype(BF16)
        turned_ref[1, 2 * count : 3 * count, at] = (ic + rs).astype(BF16)
        power_ref[:, at] = (real * real + imag * imag).astype(BF16)
        ctf3_ref[:, at] = jnp.concatenate(split(ctf_ref[:, at]), axis=0)
        parts = [part.astype(F32) for part in split(noise_ref[:, at])]
        noise3_ref[:, at] = jnp.concatenate(parts + [jnp.zeros_like(parts[0])], axis=0).astype(BF16)
        return carry

    lax.fori_loop(0, PIX // width, body, 0)
    line = lax.broadcasted_iota(jnp.int32, (count, count), 0)
    lane = lax.broadcasted_iota(jnp.int32, (count, count), 1)
    column = jnp.sum(jnp.where(lane == line, prior_ref[...], 0.0), axis=1, keepdims=True)
    column_ref[...] = jnp.broadcast_to(column, column_ref.shape)


def ctf_power_rows(group, focus, ctf3, noise3):
    count = group.shape[0]
    spot = lax.broadcasted_iota(jnp.int32, (count, 3 * DEFS), 1) % DEFS
    pick_ctf = (spot == focus.astype(jnp.int32)).astype(BF16)
    spot = lax.broadcasted_iota(jnp.int32, (count, 4 * GROUPS), 1) % GROUPS
    pick_noise = (spot == group.astype(jnp.int32)).astype(BF16)
    ctf = lax.dot_general(pick_ctf, ctf3, NN, preferred_element_type=F32)
    noise = lax.dot_general(pick_noise, noise3, NN, preferred_element_type=F32)
    return (noise * ctf * ctf).astype(BF16)


def shift_x(real, imag, cosine, sine):
    rc, rs, ic, si = real * cosine, real * sine, imag * cosine, imag * sine
    return (rc - si, real, rc + si), (ic + rs, imag, ic - rs)


def unpack(parts, wide_ref):
    size = parts[0].shape[0]
    whole = size * len(parts)
    for spot, part in enumerate(parts):
        for tile in range(WIDE // 128):
            start = whole * tile + size * spot
            wide_ref[start : start + size, :] = part[:, 128 * tile : 128 * (tile + 1)].astype(F32)

    def chunk(row, first, count):
        tiles = [
            wide_ref[pl.ds(whole * tile + 8 * first + row, count, stride=8), :] for tile in range(QUART // 128)
        ]
        return jnp.concatenate(tiles, axis=1)

    def codes(first, count):
        return wide_ref[pl.ds(whole * (QUART // 128) + 8 * first, count, stride=8), :]

    return chunk, codes


def swap_lanes(row, step, flag):
    lane = lax.broadcasted_iota(jnp.int32, row.shape, 1)
    width = row.shape[1]
    other = jnp.where((lane & step) == 0, pltpu.roll(row, width - step, 1), pltpu.roll(row, step, 1))
    return jnp.where(flag == 1, other, row)


def quarter_kernel(place, own_ref, side_ref, q0_ref, q1_ref, q2_ref, q3_ref, wide_ref):
    outs = (q0_ref, q1_ref, q2_ref, q3_ref)
    count = 2 * own_ref.shape[0] // 8
    chunk, codes = unpack((own_ref, side_ref), wide_ref)
    meta = codes(0, count)
    both = jnp.concatenate([meta, meta], axis=0).astype(BF16)
    for k in range(4):
        part = place[0] ^ k
        outs[k][:, 0:QUART] = jnp.concatenate([chunk(part, 0, count), chunk(part + 4, 0, count)], axis=0).astype(BF16)
        outs[k][:, QUART:WIDE] = both


def score_kernel(
    place, own_ref, side_ref, far_ref, corner_ref, turned_ref, power_ref, ctf3_ref, noise3_ref, trig_ref, column_ref,
    q0_ref, q1_ref, q2_ref, q3_ref, stats_ref, wide_ref,
):
    outs = (q0_ref, q1_ref, q2_ref, q3_ref)
    count = 4 * own_ref.shape[0] // 8
    half = count // 2
    refs = power_ref.shape[0]
    chunk, codes = unpack((own_ref, side_ref, far_ref, corner_ref), wide_ref)
    meta = codes(0, count)
    cross = jnp.zeros((3 * refs, 3 * count), F32)
    self_term = jnp.zeros((refs, count), F32)
    for j in range(4):
        at = slice(j * QUART, (j + 1) * QUART)
        cos_x, sin_x = trig_ref[0:1, at], trig_ref[1:2, at]
        for c, parts in enumerate(shift_x(chunk(j, 0, count), chunk(j + 4, 0, count), cos_x, sin_x)):
            new = jnp.concatenate(parts, axis=0).astype(BF16)
            cross += lax.dot_general(turned_ref[c, :, at], new, NT, preferred_element_type=F32)
        ctf_power = ctf_power_rows(meta[:, 0:1], meta[:, 1:2], ctf3_ref[:, at], noise3_ref[:, at])
        self_term += lax.dot_general(power_ref[:, at], ctf_power, NT, preferred_element_type=F32)
        part = place[0] ^ j
        late = jnp.concatenate([chunk(part, half, half), chunk(part + 4, half, half)], axis=0).astype(BF16)
        for side in range(2):
            outs[j][side * count : (side + 1) * count, 5 * refs : 5 * refs + QUART // 2] = late[
                :, side * QUART // 2 : (side + 1) * QUART // 2
            ]

    base = column_ref[:, 0:count] - 0.5 * self_term
    base_pair = jnp.concatenate([base, base], axis=1)
    turned_codes = meta.T
    centre_x, centre_y = turned_codes[2:3, :], turned_codes[3:4, :]

    def offset_term(a, b):
        off_x = centre_x + (2.0 * a - 2.0)
        off_y = centre_y + (2.0 * b - 2.0)
        return (off_x * off_x + off_y * off_y) / (2.0 * TRANS_VAR)

    pairs, singles = [], []
    for b in range(3):
        value = cross[b * refs : (b + 1) * refs]
        pairs.append(
            value[:, 0 : 2 * count] + base_pair - jnp.concatenate([offset_term(0, b), offset_term(1, b)], axis=1)
        )
        singles.append(value[:, 2 * count :] + base - offset_term(2, b))
    top_pair = jnp.max(jnp.maximum(jnp.maximum(pairs[0], pairs[1]), pairs[2]), axis=0, keepdims=True)
    top = jnp.max(jnp.maximum(jnp.maximum(singles[0], singles[1]), singles[2]), axis=0, keepdims=True)
    top = jnp.maximum(top, jnp.maximum(top_pair[:, 0:count], top_pair[:, count:]))
    top_pair = jnp.concatenate([top, top], axis=1)
    pairs = [jnp.exp(value - top_pair) for value in pairs]
    singles = [jnp.exp(value - top) for value in singles]
    mass_pair = jnp.sum(pairs[0] + pairs[1] + pairs[2], axis=0, keepdims=True)
    mass = jnp.sum(singles[0] + singles[1] + singles[2], axis=0, keepdims=True)
    mass = mass + mass_pair[:, 0:count] + mass_pair[:, count:]
    total = top + jnp.log(mass)
    row = jnp.concatenate([total, top], axis=1)
    row = swap_lanes(swap_lanes(row, half, place[2]), half // 2, place[3])
    stats_ref[...] = jnp.broadcast_to(row, stats_ref.shape)
    last = jnp.concatenate(singles[0:2], axis=1)
    notes = jnp.concatenate([meta[half:, 0:count], jnp.zeros((refs - half, count), F32)], axis=0)
    ends = jnp.concatenate([singles[2], notes], axis=1), jnp.concatenate([notes, singles[2]], axis=1)
    for k in range(4):
        for b in range(3):
            outs[k][:, b * refs : (b + 1) * refs] = pairs[b].astype(BF16)
        outs[k][:, 3 * refs : 4 * refs] = last.astype(BF16)
        outs[k][:, 4 * refs : 5 * refs] = ends[k % 2].astype(BF16)


def final_kernel(
    place, e0_ref, e1_ref, e2_ref, e3_ref, q0_ref, q1_ref, q2_ref, q3_ref, stats_ref, ctf3_ref, noise3_ref, trig_ref,
    data_ref, weight_ref, evidence_ref, post_ref, sum_ref, *, scale,
):
    dom, orient, y_hi, z_lo, mine = place[0], place[1], place[2], place[3], place[4]
    early = (e0_ref, e1_ref, e2_ref, e3_ref)
    boxes = (q0_ref, q1_ref, q2_ref, q3_ref)
    doms = 4
    count = q0_ref.shape[0] // 2
    half = count // 2
    refs = sum_ref.shape[0]
    pair = 2 * count
    orients = stats_ref.shape[0] // doms
    lane = lax.broadcasted_iota(jnp.int32, (1, pair), 1)
    left = lane < count
    upper = (lax.broadcasted_iota(jnp.int32, (orients, pair), 0) & 8) != 0
    factors, groups, foci = [], [], []
    for k in range(doms):
        start = dom ^ k ^ (2 * y_hi)
        table = jnp.where(
            upper,
            stats_ref[pl.ds(start ^ 2, orients, stride=doms), :],
            stats_ref[pl.ds(start, orients, stride=doms), :],
        )
        top = jnp.max(table, axis=0, keepdims=True)
        evidence = top + jnp.log(jnp.sum(jnp.exp(table - top), axis=0, keepdims=True))
        own = stats_ref[pl.ds(orient * doms + (dom ^ k), 1), :]
        factor = jnp.exp(pltpu.roll(own, count, 1) - evidence)
        factor = swap_lanes(swap_lanes(factor, half, y_hi), half // 2, z_lo)
        factors.append(jnp.where(left, factor, pltpu.roll(factor, count, 1)))
        if k == 0:
            evidence_ref[0] = jnp.sum(jnp.where(lane == mine, evidence, 0.0))
        notes = boxes[k][0:half, 4 * refs : 5 * refs].astype(F32)
        first = early[k][0:half, QUART:WIDE].astype(F32)
        spot = count if k % 2 == 0 else 0
        groups += [first[:, 0:1], notes[:, spot : spot + 1]]
        foci += [first[:, 1:2], notes[:, spot + 1 : spot + 2]]

    def fill(pieces, spot):
        total = jnp.zeros((refs, pair), F32)
        for b in range(3):
            post = pieces[b].astype(BF16)
            post_ref[b * refs : (b + 1) * refs, spot : spot + pair] = post
            total = total + post.astype(F32)
        sum_ref[:, spot : spot + pair] = total.astype(BF16)

    def block(k, number):
        return boxes[k][:, number * refs : (number + 1) * refs].astype(F32) * factors[k]

    for k in range(doms):
        fill([block(k, b) for b in range(3)], k * pair)
    for k in range(0, doms, 2):
        even, odd = block(k, 3), block(k + 1, 3)
        pieces = [
            jnp.where(left, even, pltpu.roll(odd, count, 1)),
            jnp.where(left, pltpu.roll(even, count, 1), odd),
            jnp.where(left, block(k, 4), block(k + 1, 4)),
        ]
        fill(pieces, (doms + k // 2) * pair)

    width = 256
    group = jnp.concatenate(groups, axis=0)
    focus = jnp.concatenate(foci, axis=0)
    for n in range(QUART // width):
        at = slice(n * width, (n + 1) * width)
        wide_at = pl.ds(pl.multiple_of(dom * QUART + n * width, width), width)
        cos_x, sin_x = trig_ref[0:1, wide_at], trig_ref[1:2, wide_at]
        reals, imags = [], []
        side = 2 * n * width // QUART
        late_at = slice(5 * refs + n * width - side * QUART // 2, 5 * refs + (n + 1) * width - side * QUART // 2)
        for k in range(doms):
            late = boxes[k][side * count : (side + 1) * count, late_at].astype(F32)
            soon = early[k][:, at].astype(F32)
            real = jnp.concatenate([soon[0:half], late[0:half]], axis=0)
            imag = jnp.concatenate([soon[half:], late[half:]], axis=0)
            new_real, new_imag = shift_x(real, imag, cos_x, sin_x)
            reals.append([part.astype(BF16) for part in new_real])
            imags.append([part.astype(BF16) for part in new_imag])

        def stack(parts):
            first = [parts[k][a] for k in range(doms) for a in range(2)]
            return jnp.concatenate(first + [parts[k][2] for k in range(doms)], axis=0)

        sums_real = lax.dot_general(post_ref[...], stack(reals), NN, preferred_element_type=F32)
        sums_imag = lax.dot_general(post_ref[...], stack(imags), NN, preferred_element_type=F32)
        r0, r1, r2 = (sums_real[b * refs : (b + 1) * refs] for b in range(3))
        i0, i1, i2 = (sums_imag[b * refs : (b + 1) * refs] for b in range(3))
        cos_y, sin_y = trig_ref[2:3, wide_at] * scale, trig_ref[3:4, wide_at] * scale
        both = (
            r1 * scale + (r0 + r2) * cos_y + (i2 - i0) * sin_y,
            i1 * scale + (i0 + i2) * cos_y + (r0 - r2) * sin_y,
        )
        for tile in range(width // 128):
            for c in range(2):
                first = 2 * (n * (width // 128) + tile) + c
                data_ref[pl.ds(first, refs, stride=2 * (QUART // 128)), :] = both[c][:, 128 * tile : 128 * (tile + 1)]
        ctf_power = ctf_power_rows(group, focus, ctf3_ref[:, wide_at], noise3_ref[:, wide_at])
        owns = [ctf_power[k * count : (k + 1) * count] for k in range(doms)]
        spread = jnp.concatenate([own for own in owns for _ in range(2)] + owns, axis=0)
        weight_ref[:, at] = lax.dot_general(sum_ref[...], spread, NN, preferred_element_type=F32) * scale


def on_device(images, offsets, groups, defocus, refs, log_prior, noise_inv, ctf_table):
    count_refs = refs.shape[0]
    size = {name: lax.axis_size(name) for name in AXES}
    orients = size["x"] * size["yh"] * size["zh"] * size["zl"]
    devices = orients * size["yl"] * size["c"]
    scale = 25.0 * (count_refs * orients) / devices
    trig = jnp.asarray(phase_rows())
    at = {name: lax.axis_index(name) for name in AXES}
    dom = at["yl"] * size["c"] + at["c"]
    orient = ((at["x"] * size["yh"] + at["yh"]) * size["zh"] + at["zh"]) * size["zl"] + at["zl"]
    mine = ((at["yh"] * size["zl"] + at["zl"]) * size["x"] + at["x"]) * size["zh"] + at["zh"]
    place = jnp.stack([dom, orient, at["yh"], at["zl"], mine]).astype(jnp.int32)

    smem = pl.BlockSpec(memory_space=pltpu.SMEM)
    vmem = pl.BlockSpec(memory_space=pltpu.VMEM)
    hbm = pl.BlockSpec(memory_space=pltpu.HBM)
    shape = jax.ShapeDtypeStruct
    line = 8 * size["x"] * size["zh"]
    payload = pl.pallas_call(
        prep_kernel,
        in_specs=[smem] * 3 + [hbm] * 3,
        out_specs=vmem,
        out_shape=shape((line, WIDE), BF16),
        scratch_shapes=[
            pltpu.VMEM((1, 2, PIX), BF16),
            pltpu.VMEM((GROUPS, PIX), F32),
            pltpu.VMEM((8, PIX), F32),
            pltpu.SemaphoreType.DMA((3,)),
        ],
        compiler_params=params(VMEM_ALL),
        name="prep",
    )(jnp.transpose(offsets, (0, 2, 1))[0], groups, defocus, images, noise_inv, ctf_table)
    flip = [(i, 3 - i) for i in range(4)]
    own = lax.all_to_all(payload, ("x", "zh"), 0, 0, tiled=True)
    side = lax.ppermute(own, "zl", [(0, 1), (1, 0)])
    far = lax.ppermute(own, ("yh", "yl"), flip)

    flat = refs.reshape(count_refs, 2 * PIX)
    side, flat = lax.optimization_barrier((side, flat))
    corner = lax.ppermute(side, ("yh", "yl"), flip)

    early = pl.pallas_call(
        quarter_kernel,
        in_specs=[smem] + [vmem] * 2,
        out_specs=[vmem] * 4,
        out_shape=[shape((orients, WIDE), BF16)] * 4,
        scratch_shapes=[pltpu.VMEM((4 * orients * (WIDE // 128), 128), F32)],
        compiler_params=params(),
        name="quarters",
    )(place, own, side)

    def share(parts):
        moves = [[(d, d ^ k) for d in range(4)] for k in range(4)]
        return parts[0:1] + [lax.ppermute(parts[k], ("yl", "c"), moves[k]) for k in range(1, 4)]

    early = list(early)
    flat, early[0] = lax.optimization_barrier((flat, early[0]))
    turned, power, ctf3, noise3, column = pl.pallas_call(
        refs_kernel,
        in_specs=[vmem] * 5,
        out_specs=[vmem] * 5,
        out_shape=[
            shape((2, 3 * count_refs, PIX), BF16),
            shape((count_refs, PIX), BF16),
            shape((3 * DEFS, PIX), BF16),
            shape((4 * GROUPS, PIX), BF16),
            shape((count_refs, 128), F32),
        ],
        compiler_params=params(),
        cost_estimate=pl.CostEstimate(flops=8 * count_refs * PIX, bytes_accessed=10 << 20, transcendentals=0),
        name="turn_refs",
    )(flat, trig, ctf_table, noise_inv, log_prior[None, :])

    early = share(early)
    early, far, corner = lax.optimization_barrier((early, far, corner))

    box = (2 * orients, 5 * count_refs + QUART // 2)
    *boxes, stats = pl.pallas_call(
        score_kernel,
        in_specs=[smem] + [vmem] * 10,
        out_specs=[vmem] * 5,
        out_shape=[shape(box, BF16)] * 4 + [shape((devices, 2 * orients), F32)],
        scratch_shapes=[pltpu.VMEM((8 * orients * (WIDE // 128), 128), F32)],
        compiler_params=params(),
        cost_estimate=pl.CostEstimate(
            flops=18 * orients * count_refs * 2 * PIX, bytes_accessed=10 << 20, transcendentals=0
        ),
        name="score",
    )(place, own, side, far, corner, turned, power, ctf3, noise3, trig, column)

    boxes = share(list(boxes))
    stats_all = lax.all_to_all(stats, AXES, 0, 0, tiled=True)

    data, weight, evidence = pl.pallas_call(
        functools.partial(final_kernel, scale=scale),
        in_specs=[smem] + [vmem] * 12,
        out_specs=[vmem, vmem, smem],
        scratch_shapes=[
            pltpu.VMEM((3 * count_refs, 12 * orients), BF16),
            pltpu.VMEM((count_refs, 12 * orients), BF16),
        ],
        out_shape=[
            shape((2 * count_refs * (QUART // 128), 128), F32),
            shape((count_refs, QUART), F32),
            shape((1,), F32),
        ],
        compiler_params=params(),
        name="insert",
    )(place, *early, *boxes, stats_all, ctf3, noise3, trig)
    data = jnp.transpose(data.reshape(count_refs, QUART // 128, 2, 128), (0, 2, 1, 3))
    return data.reshape(count_refs, 2, QUART), weight, evidence


def solution(mesh):
    fine = Mesh(mesh.devices.reshape(4, 2, 4, 2, 2, 2), AXES)
    orient = AXES[0:4]
    dom = AXES[4:6]
    return jax.shard_map(
        on_device,
        mesh=fine,
        in_specs=(
            P(AXES, None, None),
            P(AXES, None, None),
            P(AXES),
            P(AXES),
            P(orient, None, None),
            P(orient),
            P(),
            P(),
        ),
        out_specs=(P(orient, None, dom), P(orient, dom), P(AXES)),
        check_vma=False,
    )
```

```python
import functools
import math

import jax
import jax.numpy as jnp
from jax import lax
from jax.experimental import pallas as pl
from jax.experimental.pallas import tpu as pltpu
from jax.sharding import Mesh
from jax.sharding import PartitionSpec as P

SIDE = 64
PIX = SIDE * SIDE
QUART = PIX // 4
META = 128
WIDE = QUART + META
DEFS = 64
GROUPS = 8
TWO_PI = 2.0 * math.pi
TRANS_VAR = 8.0
F32 = jnp.float32
BF16 = jnp.bfloat16
NT = (((1,), (1,)), ((), ()))
NN = (((1,), (0,)), ((), ()))
AXES = ("x", "yh", "zh", "zl", "yl", "c")
VMEM_LIMIT = 24 * 1024 * 1024
VMEM_ALL = 61 * 1024 * 1024


def phases(step):
    freq = (step + SIDE // 2 & SIDE - 1) - SIDE // 2
    angle = (2 * freq & SIDE - 1).astype(F32) * (TWO_PI / SIDE)
    return jnp.cos(angle), jnp.sin(angle)


def phases_x(width):
    cosine, sine = phases(lax.broadcasted_iota(jnp.int32, (8, 128), 1) & SIDE - 1)
    many = width // 128
    return jnp.concatenate([cosine[0:1]] * many, axis=1), jnp.concatenate([sine[0:1]] * many, axis=1)


def phases_y(first, width):
    pixel = lax.broadcasted_iota(jnp.int32, (8, width), 1) + first
    cosine, sine = phases(pixel // SIDE)
    return cosine[0:1], sine[0:1]


def params(limit=VMEM_LIMIT):
    return pltpu.CompilerParams(vmem_limit_bytes=limit)


def prep_kernel(
    offsets, groups, defocus, image_hbm, noise_hbm, ctf_hbm, out_ref, image_ref, noise_ref, ctf_ref, sems
):
    group, focus, centre_x, centre_y = groups[0], defocus[0], offsets[0, 4], offsets[1, 4]
    start = pl.multiple_of(focus // 8 * 8, 8)
    copies = [
        pltpu.make_async_copy(ctf_hbm.at[pl.ds(start, 8)], ctf_ref, sems.at[0]),
        pltpu.make_async_copy(noise_hbm, noise_ref, sems.at[1]),
        pltpu.make_async_copy(image_hbm, image_ref, sems.at[2]),
    ]
    for copy in copies:
        copy.start()
    lane = lax.broadcasted_iota(jnp.int32, (4, QUART), 1)
    row = lax.broadcasted_iota(jnp.int32, (4, QUART), 0)
    freq_x = ((lane & 63) + 32 & 63) - 32
    freq_y = ((row * (QUART // SIDE) + (lane >> 6)) + 32 & 63) - 32
    angle = ((freq_x * centre_x + freq_y * centre_y) & 63).astype(F32) * (TWO_PI / SIDE)
    cosine = jnp.cos(angle)
    sine = jnp.sin(angle)
    spot = lax.broadcasted_iota(jnp.int32, (8, META), 1)
    meta = jnp.where(
        spot == 0,
        group,
        jnp.where(spot == 1, focus, jnp.where(spot == 2, centre_x, jnp.where(spot == 3, centre_y, 0))),
    ).astype(F32)
    for copy in copies:
        copy.wait()
    rows = lax.broadcasted_iota(jnp.int32, (8, PIX), 0)
    noise = jnp.sum(jnp.where(rows == group, noise_ref[...], 0.0), axis=0, keepdims=True)
    ctf = jnp.sum(jnp.where(rows == focus % 8, ctf_ref[...], 0.0), axis=0, keepdims=True)
    weighted = (image_ref[0].astype(F32) * (noise * ctf)).astype(BF16).astype(F32)
    real = jnp.concatenate([weighted[0:1, j * QUART : (j + 1) * QUART] for j in range(4)], axis=0)
    imag = jnp.concatenate([weighted[1:2, j * QUART : (j + 1) * QUART] for j in range(4)], axis=0)
    body = jnp.concatenate([real * cosine + imag * sine, imag * cosine - real * sine], axis=0)
    one = jnp.concatenate([body, meta], axis=1)
    pair = jnp.concatenate([one, one], axis=0).astype(BF16)
    for k in range(out_ref.shape[0] // 16):
        out_ref[16 * k : 16 * (k + 1), :] = pair


def refs_kernel(
    flat_ref, ctf_ref, noise_ref, prior_ref, turned_ref, power_ref, ctf3_ref, noise3_ref, column_ref
):
    count = flat_ref.shape[0]
    width = 256

    def split(table):
        first = table.astype(BF16)
        rest = table - first.astype(F32)
        second = rest.astype(BF16)
        third = (rest - second.astype(F32)).astype(BF16)
        return first, second, third

    def body(step, carry):
        at = pl.ds(pl.multiple_of(step * width, width), width)
        low = flat_ref[:, at]
        high = flat_ref[:, pl.ds(pl.multiple_of(PIX + step * width, width), width)]
        real = low.astype(F32)
        imag = high.astype(F32)
        cosine, sine = phases_y(step * width, width)
        rc, rs, ic, si = real * cosine, real * sine, imag * cosine, imag * sine
        turned_ref[0, 0:count, at] = (rc + si).astype(BF16)
        turned_ref[1, 0:count, at] = (ic - rs).astype(BF16)
        turned_ref[0, count : 2 * count, at] = low
        turned_ref[1, count : 2 * count, at] = high
        turned_ref[0, 2 * count : 3 * count, at] = (rc - si).astype(BF16)
        turned_ref[1, 2 * count : 3 * count, at] = (ic + rs).astype(BF16)
        power_ref[:, at] = (real * real + imag * imag).astype(BF16)
        ctf3_ref[:, at] = jnp.concatenate(split(ctf_ref[:, at]), axis=0)
        parts = [part.astype(F32) for part in split(noise_ref[:, at])]
        noise3_ref[:, at] = jnp.concatenate(parts + [jnp.zeros_like(parts[0])], axis=0).astype(BF16)
        return carry

    lax.fori_loop(0, PIX // width, body, 0)
    line = lax.broadcasted_iota(jnp.int32, (count, count), 0)
    lane = lax.broadcasted_iota(jnp.int32, (count, count), 1)
    column = jnp.sum(jnp.where(lane == line, prior_ref[...], 0.0), axis=1, keepdims=True)
    column_ref[...] = jnp.broadcast_to(column, column_ref.shape)


def ctf_power_rows(group, focus, ctf3, noise3):
    count = group.shape[0]
    spot = lax.broadcasted_iota(jnp.int32, (count, 3 * DEFS), 1) % DEFS
    pick_ctf = (spot == focus.astype(jnp.int32)).astype(BF16)
    spot = lax.broadcasted_iota(jnp.int32, (count, 4 * GROUPS), 1) % GROUPS
    pick_noise = (spot == group.astype(jnp.int32)).astype(BF16)
    ctf = lax.dot_general(pick_ctf, ctf3, NN, preferred_element_type=F32)
    noise = lax.dot_general(pick_noise, noise3, NN, preferred_element_type=F32)
    return (noise * ctf * ctf).astype(BF16)


def shift_x(real, imag, cosine, sine):
    rc, rs, ic, si = real * cosine, real * sine, imag * cosine, imag * sine
    return (rc - si, real, rc + si), (ic + rs, imag, ic - rs)


def unpack(parts, wide_ref):
    size = parts[0].shape[0]
    whole = size * len(parts)
    for spot, part in enumerate(parts):
        for tile in range(WIDE // 128):
            start = whole * tile + size * spot
            wide_ref[start : start + size, :] = part[:, 128 * tile : 128 * (tile + 1)].astype(F32)

    def chunk(row, first, count):
        tiles = [
            wide_ref[pl.ds(whole * tile + 8 * first + row, count, stride=8), :] for tile in range(QUART // 128)
        ]
        return jnp.concatenate(tiles, axis=1)

    def codes(first, count):
        return wide_ref[pl.ds(whole * (QUART // 128) + 8 * first, count, stride=8), :]

    return chunk, codes


def swap_lanes(row, step, flag):
    lane = lax.broadcasted_iota(jnp.int32, row.shape, 1)
    width = row.shape[1]
    other = jnp.where((lane & step) == 0, pltpu.roll(row, width - step, 1), pltpu.roll(row, step, 1))
    return jnp.where(flag == 1, other, row)


def quarter_kernel(place, own_ref, side_ref, q0_ref, q1_ref, q2_ref, q3_ref, wide_ref):
    outs = (q0_ref, q1_ref, q2_ref, q3_ref)
    count = 2 * own_ref.shape[0] // 8
    chunk, codes = unpack((own_ref, side_ref), wide_ref)
    meta = codes(0, count)
    both = jnp.concatenate([meta, meta], axis=0).astype(BF16)
    for k in range(4):
        part = place[0] ^ k
        outs[k][:, 0:QUART] = jnp.concatenate([chunk(part, 0, count), chunk(part + 4, 0, count)], axis=0).astype(BF16)
        outs[k][:, QUART:WIDE] = both


def score_kernel(
    place, own_ref, side_ref, far_ref, corner_ref, turned_ref, power_ref, ctf3_ref, noise3_ref, column_ref,
    q0_ref, q1_ref, q2_ref, q3_ref, stats_ref, wide_ref,
):
    outs = (q0_ref, q1_ref, q2_ref, q3_ref)
    count = 4 * own_ref.shape[0] // 8
    half = count // 2
    refs = power_ref.shape[0]
    chunk, codes = unpack((own_ref, side_ref, far_ref, corner_ref), wide_ref)
    meta = codes(0, count)
    cos_x, sin_x = phases_x(QUART)
    cross = jnp.zeros((3 * refs, 3 * count), F32)
    self_term = jnp.zeros((refs, count), F32)
    for j in range(4):
        at = slice(j * QUART, (j + 1) * QUART)
        for c, parts in enumerate(shift_x(chunk(j, 0, count), chunk(j + 4, 0, count), cos_x, sin_x)):
            new = jnp.concatenate(parts, axis=0).astype(BF16)
            cross += lax.dot_general(turned_ref[c, :, at], new, NT, preferred_element_type=F32)
        ctf_power = ctf_power_rows(meta[:, 0:1], meta[:, 1:2], ctf3_ref[:, at], noise3_ref[:, at])
        self_term += lax.dot_general(power_ref[:, at], ctf_power, NT, preferred_element_type=F32)
        part = place[0] ^ j
        late = jnp.concatenate([chunk(part, half, half), chunk(part + 4, half, half)], axis=0).astype(BF16)
        for side in range(2):
            outs[j][side * count : (side + 1) * count, 5 * refs : 5 * refs + QUART // 2] = late[
                :, side * QUART // 2 : (side + 1) * QUART // 2
            ]

    base = column_ref[:, 0:count] - 0.5 * self_term
    base_pair = jnp.concatenate([base, base], axis=1)
    turned_codes = meta.T
    centre_x, centre_y = turned_codes[2:3, :], turned_codes[3:4, :]

    def offset_term(a, b):
        off_x = centre_x + (2.0 * a - 2.0)
        off_y = centre_y + (2.0 * b - 2.0)
        return (off_x * off_x + off_y * off_y) / (2.0 * TRANS_VAR)

    pairs, singles = [], []
    for b in range(3):
        value = cross[b * refs : (b + 1) * refs]
        pairs.append(
            value[:, 0 : 2 * count] + base_pair - jnp.concatenate([offset_term(0, b), offset_term(1, b)], axis=1)
        )
        singles.append(value[:, 2 * count :] + base - offset_term(2, b))
    top_pair = jnp.max(jnp.maximum(jnp.maximum(pairs[0], pairs[1]), pairs[2]), axis=0, keepdims=True)
    top = jnp.max(jnp.maximum(jnp.maximum(singles[0], singles[1]), singles[2]), axis=0, keepdims=True)
    top = jnp.maximum(top, jnp.maximum(top_pair[:, 0:count], top_pair[:, count:]))
    top_pair = jnp.concatenate([top, top], axis=1)
    pairs = [jnp.exp(value - top_pair) for value in pairs]
    singles = [jnp.exp(value - top) for value in singles]
    mass_pair = jnp.sum(pairs[0] + pairs[1] + pairs[2], axis=0, keepdims=True)
    mass = jnp.sum(singles[0] + singles[1] + singles[2], axis=0, keepdims=True)
    mass = mass + mass_pair[:, 0:count] + mass_pair[:, count:]
    total = top + jnp.log(mass)
    row = jnp.concatenate([total, top], axis=1)
    row = swap_lanes(swap_lanes(row, half, place[2]), half // 2, place[3])
    stats_ref[...] = jnp.broadcast_to(row, stats_ref.shape)
    last = jnp.concatenate(singles[0:2], axis=1)
    notes = jnp.concatenate([meta[half:, 0:count], jnp.zeros((refs - half, count), F32)], axis=0)
    ends = jnp.concatenate([singles[2], notes], axis=1), jnp.concatenate([notes, singles[2]], axis=1)
    for k in range(4):
        for b in range(3):
            outs[k][:, b * refs : (b + 1) * refs] = pairs[b].astype(BF16)
        outs[k][:, 3 * refs : 4 * refs] = last.astype(BF16)
        outs[k][:, 4 * refs : 5 * refs] = ends[k % 2].astype(BF16)


def final_kernel(
    place, e0_ref, e1_ref, e2_ref, e3_ref, q0_ref, q1_ref, q2_ref, q3_ref, stats_ref, ctf3_ref, noise3_ref,
    data_ref, weight_ref, evidence_ref, post_ref, sum_ref, *, scale,
):
    dom, orient, y_hi, z_lo, mine = place[0], place[1], place[2], place[3], place[4]
    early = (e0_ref, e1_ref, e2_ref, e3_ref)
    boxes = (q0_ref, q1_ref, q2_ref, q3_ref)
    doms = 4
    count = q0_ref.shape[0] // 2
    half = count // 2
    refs = sum_ref.shape[0]
    pair = 2 * count
    orients = stats_ref.shape[0] // doms
    lane = lax.broadcasted_iota(jnp.int32, (1, pair), 1)
    left = lane < count
    upper = (lax.broadcasted_iota(jnp.int32, (orients, pair), 0) & 8) != 0
    factors, groups, foci = [], [], []
    for k in range(doms):
        start = dom ^ k ^ (2 * y_hi)
        table = jnp.where(
            upper,
            stats_ref[pl.ds(start ^ 2, orients, stride=doms), :],
            stats_ref[pl.ds(start, orients, stride=doms), :],
        )
        top = jnp.max(table, axis=0, keepdims=True)
        evidence = top + jnp.log(jnp.sum(jnp.exp(table - top), axis=0, keepdims=True))
        own = stats_ref[pl.ds(orient * doms + (dom ^ k), 1), :]
        factor = jnp.exp(pltpu.roll(own, count, 1) - evidence)
        factor = swap_lanes(swap_lanes(factor, half, y_hi), half // 2, z_lo)
        factors.append(jnp.where(left, factor, pltpu.roll(factor, count, 1)))
        if k == 0:
            evidence_ref[0] = jnp.sum(jnp.where(lane == mine, evidence, 0.0))
        notes = boxes[k][0:half, 4 * refs : 5 * refs].astype(F32)
        first = early[k][0:half, QUART:WIDE].astype(F32)
        spot = count if k % 2 == 0 else 0
        groups += [first[:, 0:1], notes[:, spot : spot + 1]]
        foci += [first[:, 1:2], notes[:, spot + 1 : spot + 2]]

    def fill(pieces, spot):
        total = jnp.zeros((refs, pair), F32)
        for b in range(3):
            post = pieces[b].astype(BF16)
            post_ref[b * refs : (b + 1) * refs, spot : spot + pair] = post
            total = total + post.astype(F32)
        sum_ref[:, spot : spot + pair] = total.astype(BF16)

    def block(k, number):
        return boxes[k][:, number * refs : (number + 1) * refs].astype(F32) * factors[k]

    for k in range(doms):
        fill([block(k, b) for b in range(3)], k * pair)
    for k in range(0, doms, 2):
        even, odd = block(k, 3), block(k + 1, 3)
        pieces = [
            jnp.where(left, even, pltpu.roll(odd, count, 1)),
            jnp.where(left, pltpu.roll(even, count, 1), odd),
            jnp.where(left, block(k, 4), block(k + 1, 4)),
        ]
        fill(pieces, (doms + k // 2) * pair)

    width = 256
    cos_x, sin_x = phases_x(width)
    group = jnp.concatenate(groups, axis=0)
    focus = jnp.concatenate(foci, axis=0)
    for n in range(QUART // width):
        at = slice(n * width, (n + 1) * width)
        wide_at = pl.ds(pl.multiple_of(dom * QUART + n * width, width), width)
        reals, imags = [], []
        side = 2 * n * width // QUART
        late_at = slice(5 * refs + n * width - side * QUART // 2, 5 * refs + (n + 1) * width - side * QUART // 2)
        for k in range(doms):
            late = boxes[k][side * count : (side + 1) * count, late_at].astype(F32)
            soon = early[k][:, at].astype(F32)
            real = jnp.concatenate([soon[0:half], late[0:half]], axis=0)
            imag = jnp.concatenate([soon[half:], late[half:]], axis=0)
            new_real, new_imag = shift_x(real, imag, cos_x, sin_x)
            reals.append([part.astype(BF16) for part in new_real])
            imags.append([part.astype(BF16) for part in new_imag])

        def stack(parts):
            first = [parts[k][a] for k in range(doms) for a in range(2)]
            return jnp.concatenate(first + [parts[k][2] for k in range(doms)], axis=0)

        sums_real = lax.dot_general(post_ref[...], stack(reals), NN, preferred_element_type=F32)
        sums_imag = lax.dot_general(post_ref[...], stack(imags), NN, preferred_element_type=F32)
        r0, r1, r2 = (sums_real[b * refs : (b + 1) * refs] for b in range(3))
        i0, i1, i2 = (sums_imag[b * refs : (b + 1) * refs] for b in range(3))
        cos_y, sin_y = phases_y(dom * QUART + n * width, width)
        cos_y, sin_y = cos_y * scale, sin_y * scale
        both = (
            r1 * scale + (r0 + r2) * cos_y + (i2 - i0) * sin_y,
            i1 * scale + (i0 + i2) * cos_y + (r0 - r2) * sin_y,
        )
        for tile in range(width // 128):
            for c in range(2):
                first = 2 * (n * (width // 128) + tile) + c
                data_ref[pl.ds(first, refs, stride=2 * (QUART // 128)), :] = both[c][:, 128 * tile : 128 * (tile + 1)]
        ctf_power = ctf_power_rows(group, focus, ctf3_ref[:, wide_at], noise3_ref[:, wide_at])
        owns = [ctf_power[k * count : (k + 1) * count] for k in range(doms)]
        spread = jnp.concatenate([own for own in owns for _ in range(2)] + owns, axis=0)
        weight_ref[:, at] = lax.dot_general(sum_ref[...], spread, NN, preferred_element_type=F32) * scale


def on_device(images, offsets, groups, defocus, refs, log_prior, noise_inv, ctf_table):
    count_refs = refs.shape[0]
    size = {name: lax.axis_size(name) for name in AXES}
    orients = size["x"] * size["yh"] * size["zh"] * size["zl"]
    devices = orients * size["yl"] * size["c"]
    scale = 25.0 * (count_refs * orients) / devices
    at = {name: lax.axis_index(name) for name in AXES}
    dom = at["yl"] * size["c"] + at["c"]
    orient = ((at["x"] * size["yh"] + at["yh"]) * size["zh"] + at["zh"]) * size["zl"] + at["zl"]
    mine = ((at["yh"] * size["zl"] + at["zl"]) * size["x"] + at["x"]) * size["zh"] + at["zh"]
    place = jnp.stack([dom, orient, at["yh"], at["zl"], mine]).astype(jnp.int32)

    smem = pl.BlockSpec(memory_space=pltpu.SMEM)
    vmem = pl.BlockSpec(memory_space=pltpu.VMEM)
    hbm = pl.BlockSpec(memory_space=pltpu.HBM)
    shape = jax.ShapeDtypeStruct
    line = 8 * size["x"] * size["zh"]
    payload = pl.pallas_call(
        prep_kernel,
        in_specs=[smem] * 3 + [hbm] * 3,
        out_specs=vmem,
        out_shape=shape((line, WIDE), BF16),
        scratch_shapes=[
            pltpu.VMEM((1, 2, PIX), BF16),
            pltpu.VMEM((GROUPS, PIX), F32),
            pltpu.VMEM((8, PIX), F32),
            pltpu.SemaphoreType.DMA((3,)),
        ],
        compiler_params=params(VMEM_ALL),
        name="prep",
    )(jnp.transpose(offsets, (0, 2, 1))[0], groups, defocus, images, noise_inv, ctf_table)
    flip = [(i, 3 - i) for i in range(4)]
    own = lax.all_to_all(payload, ("x", "zh"), 0, 0, tiled=True)
    side = lax.ppermute(own, "zl", [(0, 1), (1, 0)])
    far = lax.ppermute(own, ("yh", "yl"), flip)

    flat = refs.reshape(count_refs, 2 * PIX)
    side, flat = lax.optimization_barrier((side, flat))
    corner = lax.ppermute(side, ("yh", "yl"), flip)

    early = pl.pallas_call(
        quarter_kernel,
        in_specs=[smem] + [vmem] * 2,
        out_specs=[vmem] * 4,
        out_shape=[shape((orients, WIDE), BF16)] * 4,
        scratch_shapes=[pltpu.VMEM((4 * orients * (WIDE // 128), 128), F32)],
        compiler_params=params(),
        name="quarters",
    )(place, own, side)

    def share(parts):
        moves = [[(d, d ^ k) for d in range(4)] for k in range(4)]
        return parts[0:1] + [lax.ppermute(parts[k], ("yl", "c"), moves[k]) for k in range(1, 4)]

    early = list(early)
    flat, early[0] = lax.optimization_barrier((flat, early[0]))
    turned, power, ctf3, noise3, column = pl.pallas_call(
        refs_kernel,
        in_specs=[vmem] * 4,
        out_specs=[vmem] * 5,
        out_shape=[
            shape((2, 3 * count_refs, PIX), BF16),
            shape((count_refs, PIX), BF16),
            shape((3 * DEFS, PIX), BF16),
            shape((4 * GROUPS, PIX), BF16),
            shape((count_refs, 128), F32),
        ],
        compiler_params=params(),
        cost_estimate=pl.CostEstimate(flops=8 * count_refs * PIX, bytes_accessed=10 << 20, transcendentals=0),
        name="turn_refs",
    )(flat, ctf_table, noise_inv, log_prior[None, :])

    early = share(early)

    box = (2 * orients, 5 * count_refs + QUART // 2)
    *boxes, stats = pl.pallas_call(
        score_kernel,
        in_specs=[smem] + [vmem] * 9,
        out_specs=[vmem] * 5,
        out_shape=[shape(box, BF16)] * 4 + [shape((devices, 2 * orients), F32)],
        scratch_shapes=[pltpu.VMEM((8 * orients * (WIDE // 128), 128), F32)],
        compiler_params=params(),
        cost_estimate=pl.CostEstimate(
            flops=18 * orients * count_refs * 2 * PIX, bytes_accessed=10 << 20, transcendentals=0
        ),
        name="score",
    )(place, own, side, far, corner, turned, power, ctf3, noise3, column)

    early, boxes, stats = lax.optimization_barrier((early, list(boxes), stats))
    boxes = share(boxes)
    stats_all = lax.all_to_all(stats, AXES, 0, 0, tiled=True)

    data, weight, evidence = pl.pallas_call(
        functools.partial(final_kernel, scale=scale),
        in_specs=[smem] + [vmem] * 11,
        out_specs=[vmem, vmem, smem],
        scratch_shapes=[
            pltpu.VMEM((3 * count_refs, 12 * orients), BF16),
            pltpu.VMEM((count_refs, 12 * orients), BF16),
        ],
        out_shape=[
            shape((2 * count_refs * (QUART // 128), 128), F32),
            shape((count_refs, QUART), F32),
            shape((1,), F32),
        ],
        compiler_params=params(),
        name="insert",
    )(place, *early, *boxes, stats_all, ctf3, noise3)
    data = jnp.transpose(data.reshape(count_refs, QUART // 128, 2, 128), (0, 2, 1, 3))
    return data.reshape(count_refs, 2, QUART), weight, evidence


def solution(mesh):
    fine = Mesh(mesh.devices.reshape(4, 2, 4, 2, 2, 2), AXES)
    orient = AXES[0:4]
    dom = AXES[4:6]
    return jax.shard_map(
        on_device,
        mesh=fine,
        in_specs=(
            P(AXES, None, None),
            P(AXES, None, None),
            P(AXES),
            P(AXES),
            P(orient, None, None),
            P(orient),
            P(),
            P(),
        ),
        out_specs=(P(orient, None, dom), P(orient, dom), P(AXES)),
        check_vma=False,
    )
```

```python
import functools
import math

import jax
import jax.numpy as jnp
from jax import lax
from jax.experimental import pallas as pl
from jax.experimental.pallas import tpu as pltpu
from jax.sharding import Mesh
from jax.sharding import PartitionSpec as P

SIDE = 64
PIX = SIDE * SIDE
QUART = PIX // 4
META = 128
WIDE = QUART + META
DEFS = 64
GROUPS = 8
TWO_PI = 2.0 * math.pi
TRANS_VAR = 8.0
F32 = jnp.float32
BF16 = jnp.bfloat16
NT = (((1,), (1,)), ((), ()))
NN = (((1,), (0,)), ((), ()))
AXES = ("x", "yh", "zh", "zl", "yl", "c")
TABLE_ROWS = 3 * DEFS + 4 * GROUPS
VMEM_LIMIT = 24 * 1024 * 1024
VMEM_ALL = 61 * 1024 * 1024


def phases(step):
    freq = (step + SIDE // 2 & SIDE - 1) - SIDE // 2
    angle = (2 * freq & SIDE - 1).astype(F32) * (TWO_PI / SIDE)
    return jnp.cos(angle), jnp.sin(angle)


def phases_x(width):
    cosine, sine = phases(lax.broadcasted_iota(jnp.int32, (8, 128), 1) & SIDE - 1)
    many = width // 128
    return jnp.concatenate([cosine[0:1]] * many, axis=1), jnp.concatenate([sine[0:1]] * many, axis=1)


def phases_y(first, rows):
    line = lax.broadcasted_iota(jnp.int32, (rows, 128), 0)
    lane = lax.broadcasted_iota(jnp.int32, (rows, 128), 1)
    return phases((first + 128 * line + lane) // SIDE)


def params(limit=VMEM_LIMIT):
    return pltpu.CompilerParams(vmem_limit_bytes=limit)


def prep_kernel(
    offsets, groups, defocus, image_hbm, noise_hbm, ctf_hbm, out_ref, image_ref, noise_ref, ctf_ref, sems
):
    group, focus, centre_x, centre_y = groups[0], defocus[0], offsets[0, 4], offsets[1, 4]
    start = pl.multiple_of(focus // 8 * 8, 8)
    copies = [
        pltpu.make_async_copy(ctf_hbm.at[pl.ds(start, 8)], ctf_ref, sems.at[0]),
        pltpu.make_async_copy(noise_hbm, noise_ref, sems.at[1]),
        pltpu.make_async_copy(image_hbm, image_ref, sems.at[2]),
    ]
    for copy in copies:
        copy.start()
    lane = lax.broadcasted_iota(jnp.int32, (4, QUART), 1)
    row = lax.broadcasted_iota(jnp.int32, (4, QUART), 0)
    freq_x = ((lane & 63) + 32 & 63) - 32
    freq_y = ((row * (QUART // SIDE) + (lane >> 6)) + 32 & 63) - 32
    angle = ((freq_x * centre_x + freq_y * centre_y) & 63).astype(F32) * (TWO_PI / SIDE)
    cosine = jnp.cos(angle)
    sine = jnp.sin(angle)
    spot = lax.broadcasted_iota(jnp.int32, (8, META), 1)
    meta = jnp.where(
        spot == 0,
        group,
        jnp.where(spot == 1, focus, jnp.where(spot == 2, centre_x, jnp.where(spot == 3, centre_y, 0))),
    ).astype(F32)
    for copy in copies:
        copy.wait()
    rows = lax.broadcasted_iota(jnp.int32, (8, PIX), 0)
    noise = jnp.sum(jnp.where(rows == group, noise_ref[...], 0.0), axis=0, keepdims=True)
    ctf = jnp.sum(jnp.where(rows == focus % 8, ctf_ref[...], 0.0), axis=0, keepdims=True)
    weighted = (image_ref[0].astype(F32) * (noise * ctf)).astype(BF16).astype(F32)
    real = jnp.concatenate([weighted[0:1, j * QUART : (j + 1) * QUART] for j in range(4)], axis=0)
    imag = jnp.concatenate([weighted[1:2, j * QUART : (j + 1) * QUART] for j in range(4)], axis=0)
    body = jnp.concatenate([real * cosine + imag * sine, imag * cosine - real * sine], axis=0)
    one = jnp.concatenate([body, meta], axis=1)
    pair = jnp.concatenate([one, one], axis=0).astype(BF16)
    for k in range(out_ref.shape[0] // 16):
        out_ref[16 * k : 16 * (k + 1), :] = pair


def tables_kernel(ctf_ref, noise_ref, tables_ref):
    def split(table):
        first = table.astype(BF16).astype(F32)
        second = (table - first).astype(BF16).astype(F32)
        return [first, second, table - first - second]

    noise = split(noise_ref[...])
    rows = split(ctf_ref[...]) + noise + [jnp.zeros_like(noise[0])]
    tables_ref[...] = jnp.concatenate(rows, axis=0).astype(BF16)


def refs_kernel(flat_ref, prior_ref, turned_ref, power_ref, column_ref, cos_ref, sin_ref):
    count = flat_ref.shape[0]
    width = 256
    cos_ref[...], sin_ref[...] = phases_y(0, PIX // 128)

    def body(step, carry):
        at = pl.ds(pl.multiple_of(step * width, width), width)
        low = flat_ref[:, at]
        high = flat_ref[:, pl.ds(pl.multiple_of(PIX + step * width, width), width)]
        real = low.astype(F32)
        imag = high.astype(F32)
        lines = [pl.ds(step * (width // 128) + k, 1) for k in range(width // 128)]
        cosine = jnp.concatenate([cos_ref[line, :] for line in lines], axis=1)
        sine = jnp.concatenate([sin_ref[line, :] for line in lines], axis=1)
        rc, rs, ic, si = real * cosine, real * sine, imag * cosine, imag * sine
        turned_ref[0, 0:count, at] = (rc + si).astype(BF16)
        turned_ref[1, 0:count, at] = (ic - rs).astype(BF16)
        turned_ref[0, count : 2 * count, at] = low
        turned_ref[1, count : 2 * count, at] = high
        turned_ref[0, 2 * count : 3 * count, at] = (rc - si).astype(BF16)
        turned_ref[1, 2 * count : 3 * count, at] = (ic + rs).astype(BF16)
        power_ref[:, at] = (real * real + imag * imag).astype(BF16)
        return carry

    lax.fori_loop(0, PIX // width, body, 0)
    line = lax.broadcasted_iota(jnp.int32, (count, count), 0)
    lane = lax.broadcasted_iota(jnp.int32, (count, count), 1)
    column = jnp.sum(jnp.where(lane == line, prior_ref[...], 0.0), axis=1, keepdims=True)
    column_ref[...] = jnp.broadcast_to(column, column_ref.shape)


def table_picks(group, focus):
    spot = lax.broadcasted_iota(jnp.int32, (group.shape[0], TABLE_ROWS), 1)
    ctf = (spot < 3 * DEFS) & (spot % DEFS == focus.astype(jnp.int32))
    noise = (spot >= 3 * DEFS) & (spot < 3 * (DEFS + GROUPS)) & (spot % GROUPS == group.astype(jnp.int32))
    return jnp.concatenate([ctf.astype(F32), noise.astype(F32)], axis=0).astype(BF16)


def ctf_power_rows(picks, tables):
    rows = lax.dot_general(picks, tables, NN, preferred_element_type=F32)
    count = rows.shape[0] // 2
    ctf, noise = rows[0:count], rows[count:]
    return (noise * ctf * ctf).astype(BF16)


def shift_x(real, imag, cosine, sine):
    rc, rs, ic, si = real * cosine, real * sine, imag * cosine, imag * sine
    return (rc - si, real, rc + si), (ic + rs, imag, ic - rs)


def unpack(parts, wide_ref):
    size = parts[0].shape[0]
    whole = size * len(parts)
    for spot, part in enumerate(parts):
        for tile in range(WIDE // 128):
            start = whole * tile + size * spot
            wide_ref[start : start + size, :] = part[:, 128 * tile : 128 * (tile + 1)].astype(F32)

    def chunk(row, first, count):
        tiles = [
            wide_ref[pl.ds(whole * tile + 8 * first + row, count, stride=8), :] for tile in range(QUART // 128)
        ]
        return jnp.concatenate(tiles, axis=1)

    def codes(first, count):
        return wide_ref[pl.ds(whole * (QUART // 128) + 8 * first, count, stride=8), :]

    return chunk, codes


def swap_lanes(row, step, flag):
    lane = lax.broadcasted_iota(jnp.int32, row.shape, 1)
    width = row.shape[1]
    other = jnp.where((lane & step) == 0, pltpu.roll(row, width - step, 1), pltpu.roll(row, step, 1))
    return jnp.where(flag == 1, other, row)


def quarter_kernel(place, own_ref, side_ref, q0_ref, q1_ref, q2_ref, q3_ref, wide_ref):
    outs = (q0_ref, q1_ref, q2_ref, q3_ref)
    count = 2 * own_ref.shape[0] // 8
    chunk, codes = unpack((own_ref, side_ref), wide_ref)
    meta = codes(0, count)
    both = jnp.concatenate([meta, meta], axis=0).astype(BF16)
    for k in range(4):
        part = place[0] ^ k
        outs[k][:, 0:QUART] = jnp.concatenate([chunk(part, 0, count), chunk(part + 4, 0, count)], axis=0).astype(BF16)
        outs[k][:, QUART:WIDE] = both


def score_kernel(
    place, own_ref, side_ref, far_ref, corner_ref, turned_ref, power_ref, tables_ref, column_ref,
    q0_ref, q1_ref, q2_ref, q3_ref, stats_ref, wide_ref,
):
    outs = (q0_ref, q1_ref, q2_ref, q3_ref)
    count = 4 * own_ref.shape[0] // 8
    half = count // 2
    refs = power_ref.shape[0]
    chunk, codes = unpack((own_ref, side_ref, far_ref, corner_ref), wide_ref)
    meta = codes(0, count)
    picks = table_picks(meta[:, 0:1], meta[:, 1:2])
    cos_x, sin_x = phases_x(QUART)
    cross = jnp.zeros((3 * refs, 3 * count), F32)
    self_term = jnp.zeros((refs, count), F32)
    for j in range(4):
        at = slice(j * QUART, (j + 1) * QUART)
        for c, parts in enumerate(shift_x(chunk(j, 0, count), chunk(j + 4, 0, count), cos_x, sin_x)):
            new = jnp.concatenate(parts, axis=0).astype(BF16)
            cross += lax.dot_general(turned_ref[c, :, at], new, NT, preferred_element_type=F32)
        ctf_power = ctf_power_rows(picks, tables_ref[:, at])
        self_term += lax.dot_general(power_ref[:, at], ctf_power, NT, preferred_element_type=F32)
        part = place[0] ^ j
        late = jnp.concatenate([chunk(part, half, half), chunk(part + 4, half, half)], axis=0).astype(BF16)
        for side in range(2):
            outs[j][side * count : (side + 1) * count, 5 * refs : 5 * refs + QUART // 2] = late[
                :, side * QUART // 2 : (side + 1) * QUART // 2
            ]

    base = column_ref[:, 0:count] - 0.5 * self_term
    base_pair = jnp.concatenate([base, base], axis=1)
    turned_codes = meta.T
    centre_x, centre_y = turned_codes[2:3, :], turned_codes[3:4, :]

    def offset_term(a, b):
        off_x = centre_x + (2.0 * a - 2.0)
        off_y = centre_y + (2.0 * b - 2.0)
        return (off_x * off_x + off_y * off_y) / (2.0 * TRANS_VAR)

    pairs, singles = [], []
    for b in range(3):
        value = cross[b * refs : (b + 1) * refs]
        pairs.append(
            value[:, 0 : 2 * count] + base_pair - jnp.concatenate([offset_term(0, b), offset_term(1, b)], axis=1)
        )
        singles.append(value[:, 2 * count :] + base - offset_term(2, b))
    top_pair = jnp.max(jnp.maximum(jnp.maximum(pairs[0], pairs[1]), pairs[2]), axis=0, keepdims=True)
    top = jnp.max(jnp.maximum(jnp.maximum(singles[0], singles[1]), singles[2]), axis=0, keepdims=True)
    top = jnp.maximum(top, jnp.maximum(top_pair[:, 0:count], top_pair[:, count:]))
    top_pair = jnp.concatenate([top, top], axis=1)
    pairs = [jnp.exp(value - top_pair) for value in pairs]
    singles = [jnp.exp(value - top) for value in singles]
    mass_pair = jnp.sum(pairs[0] + pairs[1] + pairs[2], axis=0, keepdims=True)
    mass = jnp.sum(singles[0] + singles[1] + singles[2], axis=0, keepdims=True)
    mass = mass + mass_pair[:, 0:count] + mass_pair[:, count:]
    total = top + jnp.log(mass)
    row = jnp.concatenate([total, top], axis=1)
    row = swap_lanes(swap_lanes(row, half, place[2]), half // 2, place[3])
    stats_ref[...] = jnp.broadcast_to(row, stats_ref.shape)
    last = jnp.concatenate(singles[0:2], axis=1)
    notes = jnp.concatenate([meta[half:, 0:count], jnp.zeros((refs - half, count), F32)], axis=0)
    ends = jnp.concatenate([singles[2], notes], axis=1), jnp.concatenate([notes, singles[2]], axis=1)
    for k in range(4):
        for b in range(3):
            outs[k][:, b * refs : (b + 1) * refs] = pairs[b].astype(BF16)
        outs[k][:, 3 * refs : 4 * refs] = last.astype(BF16)
        outs[k][:, 4 * refs : 5 * refs] = ends[k % 2].astype(BF16)


def final_kernel(
    place, e0_ref, e1_ref, e2_ref, e3_ref, q0_ref, q1_ref, q2_ref, q3_ref, stats_ref, tables_ref,
    data_ref, weight_ref, evidence_ref, post_ref, sum_ref, *, scale,
):
    dom, orient, y_hi, z_lo, mine = place[0], place[1], place[2], place[3], place[4]
    early = (e0_ref, e1_ref, e2_ref, e3_ref)
    boxes = (q0_ref, q1_ref, q2_ref, q3_ref)
    doms = 4
    count = q0_ref.shape[0] // 2
    half = count // 2
    refs = sum_ref.shape[0]
    pair = 2 * count
    orients = stats_ref.shape[0] // doms
    lane = lax.broadcasted_iota(jnp.int32, (1, pair), 1)
    left = lane < count
    upper = (lax.broadcasted_iota(jnp.int32, (orients, pair), 0) & 8) != 0
    factors, groups, foci = [], [], []
    for k in range(doms):
        start = dom ^ k ^ (2 * y_hi)
        table = jnp.where(
            upper,
            stats_ref[pl.ds(start ^ 2, orients, stride=doms), :],
            stats_ref[pl.ds(start, orients, stride=doms), :],
        )
        top = jnp.max(table, axis=0, keepdims=True)
        evidence = top + jnp.log(jnp.sum(jnp.exp(table - top), axis=0, keepdims=True))
        own = stats_ref[pl.ds(orient * doms + (dom ^ k), 1), :]
        factor = jnp.exp(pltpu.roll(own, count, 1) - evidence)
        factor = swap_lanes(swap_lanes(factor, half, y_hi), half // 2, z_lo)
        factors.append(jnp.where(left, factor, pltpu.roll(factor, count, 1)))
        if k == 0:
            evidence_ref[0] = jnp.sum(jnp.where(lane == mine, evidence, 0.0))
        notes = boxes[k][0:half, 4 * refs : 5 * refs].astype(F32)
        first = early[k][0:half, QUART:WIDE].astype(F32)
        spot = count if k % 2 == 0 else 0
        groups += [first[:, 0:1], notes[:, spot : spot + 1]]
        foci += [first[:, 1:2], notes[:, spot + 1 : spot + 2]]

    def fill(pieces, spot):
        total = jnp.zeros((refs, pair), F32)
        for b in range(3):
            post = pieces[b].astype(BF16)
            post_ref[b * refs : (b + 1) * refs, spot : spot + pair] = post
            total = total + post.astype(F32)
        return total

    def block(k, number):
        return boxes[k][:, number * refs : (number + 1) * refs].astype(F32) * factors[k]

    totals = []
    for k in range(doms):
        total = fill([block(k, b) for b in range(3)], k * pair)
        totals.append(total + pltpu.roll(total, count, 1))
    for k in range(0, doms, 2):
        even, odd = block(k, 3), block(k + 1, 3)
        pieces = [
            jnp.where(left, even, pltpu.roll(odd, count, 1)),
            jnp.where(left, pltpu.roll(even, count, 1), odd),
            jnp.where(left, block(k, 4), block(k + 1, 4)),
        ]
        total = fill(pieces, (doms + k // 2) * pair) + jnp.where(left, totals[k], totals[k + 1])
        sum_ref[:, k * count : (k + 2) * count] = total.astype(BF16)

    width = 256
    cos_x, sin_x = phases_x(width)
    picks = table_picks(jnp.concatenate(groups, axis=0), jnp.concatenate(foci, axis=0))
    cos_rows, sin_rows = phases_y(dom * QUART, QUART // 128)
    cos_rows, sin_rows = cos_rows * scale, sin_rows * scale
    for n in range(QUART // width):
        at = slice(n * width, (n + 1) * width)
        wide_at = pl.ds(pl.multiple_of(dom * QUART + n * width, width), width)
        reals, imags = [], []
        side = 2 * n * width // QUART
        late_at = slice(5 * refs + n * width - side * QUART // 2, 5 * refs + (n + 1) * width - side * QUART // 2)
        for k in range(doms):
            late = boxes[k][side * count : (side + 1) * count, late_at].astype(F32)
            soon = early[k][:, at].astype(F32)
            real = jnp.concatenate([soon[0:half], late[0:half]], axis=0)
            imag = jnp.concatenate([soon[half:], late[half:]], axis=0)
            new_real, new_imag = shift_x(real, imag, cos_x, sin_x)
            reals.append([part.astype(BF16) for part in new_real])
            imags.append([part.astype(BF16) for part in new_imag])

        def stack(parts):
            first = [parts[k][a] for k in range(doms) for a in range(2)]
            return jnp.concatenate(first + [parts[k][2] for k in range(doms)], axis=0)

        sums_real = lax.dot_general(post_ref[...], stack(reals), NN, preferred_element_type=F32)
        sums_imag = lax.dot_general(post_ref[...], stack(imags), NN, preferred_element_type=F32)
        r0, r1, r2 = (sums_real[b * refs : (b + 1) * refs] for b in range(3))
        i0, i1, i2 = (sums_imag[b * refs : (b + 1) * refs] for b in range(3))
        lines = [n * (width // 128) + tile for tile in range(width // 128)]
        cos_y = jnp.concatenate([cos_rows[line : line + 1] for line in lines], axis=1)
        sin_y = jnp.concatenate([sin_rows[line : line + 1] for line in lines], axis=1)
        both = (
            r1 * scale + (r0 + r2) * cos_y + (i2 - i0) * sin_y,
            i1 * scale + (i0 + i2) * cos_y + (r0 - r2) * sin_y,
        )
        for tile in range(width // 128):
            for c in range(2):
                first = 2 * (n * (width // 128) + tile) + c
                data_ref[pl.ds(first, refs, stride=2 * (QUART // 128)), :] = both[c][:, 128 * tile : 128 * (tile + 1)]
        ctf_power = ctf_power_rows(picks, tables_ref[:, wide_at])
        weight_ref[:, at] = lax.dot_general(sum_ref[...], ctf_power, NN, preferred_element_type=F32) * scale


def on_device(images, offsets, groups, defocus, refs, log_prior, noise_inv, ctf_table):
    count_refs = refs.shape[0]
    size = {name: lax.axis_size(name) for name in AXES}
    orients = size["x"] * size["yh"] * size["zh"] * size["zl"]
    devices = orients * size["yl"] * size["c"]
    scale = 25.0 * (count_refs * orients) / devices
    at = {name: lax.axis_index(name) for name in AXES}
    dom = at["yl"] * size["c"] + at["c"]
    orient = ((at["x"] * size["yh"] + at["yh"]) * size["zh"] + at["zh"]) * size["zl"] + at["zl"]
    mine = ((at["yh"] * size["zl"] + at["zl"]) * size["x"] + at["x"]) * size["zh"] + at["zh"]
    place = jnp.stack([dom, orient, at["yh"], at["zl"], mine]).astype(jnp.int32)

    smem = pl.BlockSpec(memory_space=pltpu.SMEM)
    vmem = pl.BlockSpec(memory_space=pltpu.VMEM)
    hbm = pl.BlockSpec(memory_space=pltpu.HBM)
    shape = jax.ShapeDtypeStruct
    line = 8 * size["x"] * size["zh"]
    payload = pl.pallas_call(
        prep_kernel,
        in_specs=[smem] * 3 + [hbm] * 3,
        out_specs=vmem,
        out_shape=shape((line, WIDE), BF16),
        scratch_shapes=[
            pltpu.VMEM((1, 2, PIX), BF16),
            pltpu.VMEM((GROUPS, PIX), F32),
            pltpu.VMEM((8, PIX), F32),
            pltpu.SemaphoreType.DMA((3,)),
        ],
        compiler_params=params(VMEM_ALL),
        name="prep",
    )(jnp.transpose(offsets, (0, 2, 1))[0], groups, defocus, images, noise_inv, ctf_table)
    flip = [(i, 3 - i) for i in range(4)]
    own = lax.all_to_all(payload, ("x", "zh"), 0, 0, tiled=True)
    side = lax.ppermute(own, "zl", [(0, 1), (1, 0)])
    far = lax.ppermute(own, ("yh", "yl"), flip)

    flat = refs.reshape(count_refs, 2 * PIX)
    flat, ctf_late, noise_late = lax.optimization_barrier((flat, ctf_table, noise_inv))
    tables = pl.pallas_call(
        tables_kernel,
        in_specs=[vmem] * 2,
        out_specs=vmem,
        out_shape=shape((TABLE_ROWS, PIX), BF16),
        compiler_params=params(VMEM_LIMIT // 3),
        name="tables",
    )(ctf_late, noise_late)
    side, _, flat, tables = lax.optimization_barrier((side, far, flat, tables))
    corner = lax.ppermute(side, ("yh", "yl"), flip)

    early = pl.pallas_call(
        quarter_kernel,
        in_specs=[smem] + [vmem] * 2,
        out_specs=[vmem] * 4,
        out_shape=[shape((orients, WIDE), BF16)] * 4,
        scratch_shapes=[pltpu.VMEM((4 * orients * (WIDE // 128), 128), F32)],
        compiler_params=params(VMEM_LIMIT // 3),
        name="quarters",
    )(place, own, side)

    def share(parts):
        moves = [[(d, d ^ k) for d in range(4)] for k in range(4)]
        return parts[0:1] + [lax.ppermute(parts[k], ("yl", "c"), moves[k]) for k in range(1, 4)]

    early = list(early)
    flat, early[0] = lax.optimization_barrier((flat, early[0]))
    turned, power, column = pl.pallas_call(
        refs_kernel,
        in_specs=[vmem] * 2,
        out_specs=[vmem] * 3,
        out_shape=[
            shape((2, 3 * count_refs, PIX), BF16),
            shape((count_refs, PIX), BF16),
            shape((count_refs, 128), F32),
        ],
        scratch_shapes=[pltpu.VMEM((PIX // 128, 128), F32)] * 2,
        compiler_params=params(),
        cost_estimate=pl.CostEstimate(flops=8 * count_refs * PIX, bytes_accessed=10 << 20, transcendentals=0),
        name="turn_refs",
    )(flat, log_prior[None, :])
    early = share(early)

    box = (2 * orients, 5 * count_refs + QUART // 2)
    *boxes, stats = pl.pallas_call(
        score_kernel,
        in_specs=[smem] + [vmem] * 8,
        out_specs=[vmem] * 5,
        out_shape=[shape(box, BF16)] * 4 + [shape((devices, 2 * orients), F32)],
        scratch_shapes=[pltpu.VMEM((8 * orients * (WIDE // 128), 128), F32)],
        compiler_params=params(),
        cost_estimate=pl.CostEstimate(
            flops=18 * orients * count_refs * 2 * PIX, bytes_accessed=10 << 20, transcendentals=0
        ),
        name="score",
    )(place, own, side, far, corner, turned, power, tables, column)

    early, boxes, stats = lax.optimization_barrier((early, list(boxes), stats))
    boxes = share(boxes)
    stats_all = lax.all_to_all(stats, AXES, 0, 0, tiled=True)

    data, weight, evidence = pl.pallas_call(
        functools.partial(final_kernel, scale=scale),
        in_specs=[smem] + [vmem] * 10,
        out_specs=[vmem, vmem, smem],
        scratch_shapes=[
            pltpu.VMEM((3 * count_refs, 12 * orients), BF16),
            pltpu.VMEM((count_refs, 4 * orients), BF16),
        ],
        out_shape=[
            shape((2 * count_refs * (QUART // 128), 128), F32),
            shape((count_refs, QUART), F32),
            shape((1,), F32),
        ],
        compiler_params=params(),
        name="insert",
    )(place, *early, *boxes, stats_all, tables)
    data = jnp.transpose(data.reshape(count_refs, QUART // 128, 2, 128), (0, 2, 1, 3))
    return data.reshape(count_refs, 2, QUART), weight, evidence


def solution(mesh):
    fine = Mesh(mesh.devices.reshape(4, 2, 4, 2, 2, 2), AXES)
    orient = AXES[0:4]
    dom = AXES[4:6]
    return jax.shard_map(
        on_device,
        mesh=fine,
        in_specs=(
            P(AXES, None, None),
            P(AXES, None, None),
            P(AXES),
            P(AXES),
            P(orient, None, None),
            P(orient),
            P(),
            P(),
        ),
        out_specs=(P(orient, None, dom), P(orient, dom), P(AXES)),
        check_vma=False,
    )
```

```python
import functools
import math

import jax
import jax.numpy as jnp
from jax import lax
from jax.experimental import pallas as pl
from jax.experimental.pallas import tpu as pltpu
from jax.sharding import Mesh
from jax.sharding import PartitionSpec as P

SIDE = 64
PIX = SIDE * SIDE
QUART = PIX // 4
META = 128
WIDE = QUART + META
DEFS = 64
GROUPS = 8
TWO_PI = 2.0 * math.pi
TRANS_VAR = 8.0
F32 = jnp.float32
BF16 = jnp.bfloat16
NT = (((1,), (1,)), ((), ()))
NN = (((1,), (0,)), ((), ()))
AXES = ("x", "yh", "zh", "zl", "yl", "c")
TABLE_ROWS = 3 * DEFS + 4 * GROUPS
VMEM_LIMIT = 24 * 1024 * 1024
VMEM_ALL = 61 * 1024 * 1024


def phases(step):
    freq = (step + SIDE // 2 & SIDE - 1) - SIDE // 2
    angle = (2 * freq & SIDE - 1).astype(F32) * (TWO_PI / SIDE)
    return jnp.cos(angle), jnp.sin(angle)


def phases_x(width):
    cosine, sine = phases(lax.broadcasted_iota(jnp.int32, (8, 128), 1) & SIDE - 1)
    many = width // 128
    return jnp.concatenate([cosine[0:1]] * many, axis=1), jnp.concatenate([sine[0:1]] * many, axis=1)


def phases_y(first, rows):
    line = lax.broadcasted_iota(jnp.int32, (rows, 128), 0)
    lane = lax.broadcasted_iota(jnp.int32, (rows, 128), 1)
    return phases((first + 128 * line + lane) // SIDE)


def params(limit=VMEM_LIMIT):
    return pltpu.CompilerParams(vmem_limit_bytes=limit)


def prep_kernel(
    offsets, groups, defocus, image_hbm, noise_hbm, ctf_hbm, out_ref, image_ref, noise_ref, ctf_ref, sems
):
    group, focus, centre_x, centre_y = groups[0], defocus[0], offsets[0, 4], offsets[1, 4]
    start = pl.multiple_of(focus // 8 * 8, 8)
    copies = [
        pltpu.make_async_copy(ctf_hbm.at[pl.ds(start, 8)], ctf_ref, sems.at[0]),
        pltpu.make_async_copy(noise_hbm, noise_ref, sems.at[1]),
        pltpu.make_async_copy(image_hbm, image_ref, sems.at[2]),
    ]
    for copy in copies:
        copy.start()
    lane = lax.broadcasted_iota(jnp.int32, (4, QUART), 1)
    row = lax.broadcasted_iota(jnp.int32, (4, QUART), 0)
    freq_x = ((lane & 63) + 32 & 63) - 32
    freq_y = ((row * (QUART // SIDE) + (lane >> 6)) + 32 & 63) - 32
    angle = ((freq_x * centre_x + freq_y * centre_y) & 63).astype(F32) * (TWO_PI / SIDE)
    cosine = jnp.cos(angle)
    sine = jnp.sin(angle)
    spot = lax.broadcasted_iota(jnp.int32, (8, META), 1)
    meta = jnp.where(
        spot == 0,
        group,
        jnp.where(spot == 1, focus, jnp.where(spot == 2, centre_x, jnp.where(spot == 3, centre_y, 0))),
    ).astype(F32)
    for copy in copies:
        copy.wait()
    rows = lax.broadcasted_iota(jnp.int32, (8, PIX), 0)
    noise = jnp.sum(jnp.where(rows == group, noise_ref[...], 0.0), axis=0, keepdims=True)
    ctf = jnp.sum(jnp.where(rows == focus % 8, ctf_ref[...], 0.0), axis=0, keepdims=True)
    weighted = (image_ref[0].astype(F32) * (noise * ctf)).astype(BF16).astype(F32)
    real = jnp.concatenate([weighted[0:1, j * QUART : (j + 1) * QUART] for j in range(4)], axis=0)
    imag = jnp.concatenate([weighted[1:2, j * QUART : (j + 1) * QUART] for j in range(4)], axis=0)
    body = jnp.concatenate([real * cosine + imag * sine, imag * cosine - real * sine], axis=0)
    one = jnp.concatenate([body, meta], axis=1)
    pair = jnp.concatenate([one, one], axis=0).astype(BF16)
    for k in range(out_ref.shape[0] // 16):
        out_ref[16 * k : 16 * (k + 1), :] = pair


def tables_kernel(ctf_ref, noise_ref, tables_ref):
    def split(table):
        first = table.astype(BF16).astype(F32)
        second = (table - first).astype(BF16).astype(F32)
        return [first, second, table - first - second]

    noise = split(noise_ref[...])
    rows = split(ctf_ref[...]) + noise + [jnp.zeros_like(noise[0])]
    tables_ref[...] = jnp.concatenate(rows, axis=0).astype(BF16)


def refs_kernel(flat_ref, prior_ref, turned_ref, power_ref, column_ref, cos_ref, sin_ref):
    count = flat_ref.shape[0]
    width = 256
    cos_ref[...], sin_ref[...] = phases_y(0, PIX // 128)

    def body(step, carry):
        at = pl.ds(pl.multiple_of(step * width, width), width)
        low = flat_ref[:, at]
        high = flat_ref[:, pl.ds(pl.multiple_of(PIX + step * width, width), width)]
        real = low.astype(F32)
        imag = high.astype(F32)
        lines = [pl.ds(step * (width // 128) + k, 1) for k in range(width // 128)]
        cosine = jnp.concatenate([cos_ref[line, :] for line in lines], axis=1)
        sine = jnp.concatenate([sin_ref[line, :] for line in lines], axis=1)
        rc, rs, ic, si = real * cosine, real * sine, imag * cosine, imag * sine
        turned_ref[0, 0:count, at] = (rc + si).astype(BF16)
        turned_ref[1, 0:count, at] = (ic - rs).astype(BF16)
        turned_ref[0, count : 2 * count, at] = low
        turned_ref[1, count : 2 * count, at] = high
        turned_ref[0, 2 * count : 3 * count, at] = (rc - si).astype(BF16)
        turned_ref[1, 2 * count : 3 * count, at] = (ic + rs).astype(BF16)
        power_ref[:, at] = (real * real + imag * imag).astype(BF16)
        return carry

    lax.fori_loop(0, PIX // width, body, 0)
    line = lax.broadcasted_iota(jnp.int32, (count, count), 0)
    lane = lax.broadcasted_iota(jnp.int32, (count, count), 1)
    column = jnp.sum(jnp.where(lane == line, prior_ref[...], 0.0), axis=1, keepdims=True)
    column_ref[...] = jnp.broadcast_to(column, column_ref.shape)


def table_picks(group, focus):
    spot = lax.broadcasted_iota(jnp.int32, (group.shape[0], TABLE_ROWS), 1)
    ctf = (spot < 3 * DEFS) & (spot % DEFS == focus.astype(jnp.int32))
    noise = (spot >= 3 * DEFS) & (spot < 3 * (DEFS + GROUPS)) & (spot % GROUPS == group.astype(jnp.int32))
    return jnp.concatenate([ctf.astype(F32), noise.astype(F32)], axis=0).astype(BF16)


def ctf_power_rows(picks, tables):
    rows = lax.dot_general(picks, tables, NN, preferred_element_type=F32)
    count = rows.shape[0] // 2
    ctf, noise = rows[0:count], rows[count:]
    return (noise * ctf * ctf).astype(BF16)


def shift_x(real, imag, cosine, sine):
    rc, rs, ic, si = real * cosine, real * sine, imag * cosine, imag * sine
    return (rc - si, real, rc + si), (ic + rs, imag, ic - rs)


def unpack(parts, wide_ref):
    size = parts[0].shape[0]
    whole = size * len(parts)
    for spot, part in enumerate(parts):
        for tile in range(WIDE // 128):
            start = whole * tile + size * spot
            wide_ref[start : start + size, :] = part[:, 128 * tile : 128 * (tile + 1)].astype(F32)

    def chunk(row, first, count):
        tiles = [
            wide_ref[pl.ds(whole * tile + 8 * first + row, count, stride=8), :] for tile in range(QUART // 128)
        ]
        return jnp.concatenate(tiles, axis=1)

    def codes(first, count):
        return wide_ref[pl.ds(whole * (QUART // 128) + 8 * first, count, stride=8), :]

    return chunk, codes


def swap_lanes(row, step, flag):
    lane = lax.broadcasted_iota(jnp.int32, row.shape, 1)
    width = row.shape[1]
    other = jnp.where((lane & step) == 0, pltpu.roll(row, width - step, 1), pltpu.roll(row, step, 1))
    return jnp.where(flag == 1, other, row)


def quarter_kernel(place, own_ref, side_ref, q0_ref, q1_ref, q2_ref, q3_ref, wide_ref):
    outs = (q0_ref, q1_ref, q2_ref, q3_ref)
    count = 2 * own_ref.shape[0] // 8
    chunk, codes = unpack((own_ref, side_ref), wide_ref)
    meta = codes(0, count)
    both = jnp.concatenate([meta, meta], axis=0).astype(BF16)
    for k in range(4):
        part = place[0] ^ k
        outs[k][:, 0:QUART] = jnp.concatenate([chunk(part, 0, count), chunk(part + 4, 0, count)], axis=0).astype(BF16)
        outs[k][:, QUART:WIDE] = both


def score_kernel(
    place, own_ref, side_ref, far_ref, corner_ref, turned_ref, power_ref, tables_ref, column_ref,
    q0_ref, q1_ref, q2_ref, q3_ref, stats_ref, wide_ref,
):
    outs = (q0_ref, q1_ref, q2_ref, q3_ref)
    count = 4 * own_ref.shape[0] // 8
    half = count // 2
    refs = power_ref.shape[0]
    chunk, codes = unpack((own_ref, side_ref, far_ref, corner_ref), wide_ref)
    meta = codes(0, count)
    picks = table_picks(meta[:, 0:1], meta[:, 1:2])
    cos_x, sin_x = phases_x(QUART)
    cross = jnp.zeros((3 * refs, 3 * count), F32)
    self_term = jnp.zeros((refs, count), F32)
    for j in range(4):
        at = slice(j * QUART, (j + 1) * QUART)
        for c, parts in enumerate(shift_x(chunk(j, 0, count), chunk(j + 4, 0, count), cos_x, sin_x)):
            new = jnp.concatenate(parts, axis=0).astype(BF16)
            cross += lax.dot_general(turned_ref[c, :, at], new, NT, preferred_element_type=F32)
        ctf_power = ctf_power_rows(picks, tables_ref[:, at])
        self_term += lax.dot_general(power_ref[:, at], ctf_power, NT, preferred_element_type=F32)
        part = place[0] ^ j
        late = jnp.concatenate([chunk(part, half, half), chunk(part + 4, half, half)], axis=0).astype(BF16)
        for side in range(2):
            outs[j][side * count : (side + 1) * count, 5 * refs : 5 * refs + QUART // 2] = late[
                :, side * QUART // 2 : (side + 1) * QUART // 2
            ]

    base = column_ref[:, 0:count] - 0.5 * self_term
    base_pair = jnp.concatenate([base, base], axis=1)
    turned_codes = meta.T
    centre_x, centre_y = turned_codes[2:3, :], turned_codes[3:4, :]

    def offset_term(a, b):
        off_x = centre_x + (2.0 * a - 2.0)
        off_y = centre_y + (2.0 * b - 2.0)
        return (off_x * off_x + off_y * off_y) / (2.0 * TRANS_VAR)

    pairs, singles = [], []
    for b in range(3):
        value = cross[b * refs : (b + 1) * refs]
        pairs.append(
            value[:, 0 : 2 * count] + base_pair - jnp.concatenate([offset_term(0, b), offset_term(1, b)], axis=1)
        )
        singles.append(value[:, 2 * count :] + base - offset_term(2, b))
    top_pair = jnp.max(jnp.maximum(jnp.maximum(pairs[0], pairs[1]), pairs[2]), axis=0, keepdims=True)
    top = jnp.max(jnp.maximum(jnp.maximum(singles[0], singles[1]), singles[2]), axis=0, keepdims=True)
    top = jnp.maximum(top, jnp.maximum(top_pair[:, 0:count], top_pair[:, count:]))
    top_pair = jnp.concatenate([top, top], axis=1)
    pairs = [jnp.exp(value - top_pair) for value in pairs]
    singles = [jnp.exp(value - top) for value in singles]
    mass_pair = jnp.sum(pairs[0] + pairs[1] + pairs[2], axis=0, keepdims=True)
    mass = jnp.sum(singles[0] + singles[1] + singles[2], axis=0, keepdims=True)
    mass = mass + mass_pair[:, 0:count] + mass_pair[:, count:]
    total = top + jnp.log(mass)
    row = jnp.concatenate([total, top], axis=1)
    row = swap_lanes(swap_lanes(row, half, place[2]), half // 2, place[3])
    stats_ref[...] = jnp.broadcast_to(row, stats_ref.shape)
    last = jnp.concatenate(singles[0:2], axis=1)
    notes = jnp.concatenate([meta[half:, 0:count], jnp.zeros((refs - half, count), F32)], axis=0)
    ends = jnp.concatenate([singles[2], notes], axis=1), jnp.concatenate([notes, singles[2]], axis=1)
    for k in range(4):
        for b in range(3):
            outs[k][:, b * refs : (b + 1) * refs] = pairs[b].astype(BF16)
        outs[k][:, 3 * refs : 4 * refs] = last.astype(BF16)
        outs[k][:, 4 * refs : 5 * refs] = ends[k % 2].astype(BF16)


def final_kernel(
    place, e0_ref, e1_ref, e2_ref, e3_ref, q0_ref, q1_ref, q2_ref, q3_ref, stats_ref, tables_ref,
    data_ref, weight_ref, evidence_ref, post_ref, sum_ref, *, scale,
):
    dom, orient, y_hi, z_lo, mine = place[0], place[1], place[2], place[3], place[4]
    early = (e0_ref, e1_ref, e2_ref, e3_ref)
    boxes = (q0_ref, q1_ref, q2_ref, q3_ref)
    doms = 4
    count = q0_ref.shape[0] // 2
    half = count // 2
    refs = sum_ref.shape[0]
    pair = 2 * count
    orients = stats_ref.shape[0] // doms
    lane = lax.broadcasted_iota(jnp.int32, (1, pair), 1)
    left = lane < count
    upper = (lax.broadcasted_iota(jnp.int32, (orients, pair), 0) & 8) != 0
    factors, groups, foci = [], [], []
    for k in range(doms):
        start = dom ^ k ^ (2 * y_hi)
        table = jnp.where(
            upper,
            stats_ref[pl.ds(start ^ 2, orients, stride=doms), :],
            stats_ref[pl.ds(start, orients, stride=doms), :],
        )
        top = jnp.max(table, axis=0, keepdims=True)
        evidence = top + jnp.log(jnp.sum(jnp.exp(table - top), axis=0, keepdims=True))
        own = stats_ref[pl.ds(orient * doms + (dom ^ k), 1), :]
        factor = jnp.exp(pltpu.roll(own, count, 1) - evidence)
        factor = swap_lanes(swap_lanes(factor, half, y_hi), half // 2, z_lo)
        factors.append(jnp.where(left, factor, pltpu.roll(factor, count, 1)))
        if k == 0:
            evidence_ref[0] = jnp.sum(jnp.where(lane == mine, evidence, 0.0))
        notes = boxes[k][0:half, 4 * refs : 5 * refs].astype(F32)
        first = early[k][0:half, QUART:WIDE].astype(F32)
        spot = count if k % 2 == 0 else 0
        groups += [first[:, 0:1], notes[:, spot : spot + 1]]
        foci += [first[:, 1:2], notes[:, spot + 1 : spot + 2]]

    def fill(pieces, spot):
        total = jnp.zeros((refs, pair), F32)
        for b in range(3):
            post = pieces[b].astype(BF16)
            post_ref[b * refs : (b + 1) * refs, spot : spot + pair] = post
            total = total + post.astype(F32)
        return total

    def block(k, number):
        return boxes[k][:, number * refs : (number + 1) * refs].astype(F32) * factors[k]

    totals = []
    for k in range(doms):
        total = fill([block(k, b) for b in range(3)], k * pair)
        totals.append(total + pltpu.roll(total, count, 1))
    for k in range(0, doms, 2):
        even, odd = block(k, 3), block(k + 1, 3)
        pieces = [
            jnp.where(left, even, pltpu.roll(odd, count, 1)),
            jnp.where(left, pltpu.roll(even, count, 1), odd),
            jnp.where(left, block(k, 4), block(k + 1, 4)),
        ]
        total = fill(pieces, (doms + k // 2) * pair) + jnp.where(left, totals[k], totals[k + 1])
        sum_ref[:, k * count : (k + 2) * count] = total.astype(BF16)

    width = 512
    cos_x, sin_x = phases_x(width)
    picks = table_picks(jnp.concatenate(groups, axis=0), jnp.concatenate(foci, axis=0))
    cos_rows, sin_rows = phases_y(dom * QUART, QUART // 128)
    cos_rows, sin_rows = cos_rows * scale, sin_rows * scale
    for n in range(QUART // width):
        at = slice(n * width, (n + 1) * width)
        wide_at = pl.ds(pl.multiple_of(dom * QUART + n * width, width), width)
        reals, imags = [], []
        side = 2 * n * width // QUART
        late_at = slice(5 * refs + n * width - side * QUART // 2, 5 * refs + (n + 1) * width - side * QUART // 2)
        for k in range(doms):
            late = boxes[k][side * count : (side + 1) * count, late_at].astype(F32)
            soon = early[k][:, at].astype(F32)
            real = jnp.concatenate([soon[0:half], late[0:half]], axis=0)
            imag = jnp.concatenate([soon[half:], late[half:]], axis=0)
            new_real, new_imag = shift_x(real, imag, cos_x, sin_x)
            reals.append([part.astype(BF16) for part in new_real])
            imags.append([part.astype(BF16) for part in new_imag])

        def stack(parts):
            first = [parts[k][a] for k in range(doms) for a in range(2)]
            return jnp.concatenate(first + [parts[k][2] for k in range(doms)], axis=0)

        sums_real = lax.dot_general(post_ref[...], stack(reals), NN, preferred_element_type=F32)
        sums_imag = lax.dot_general(post_ref[...], stack(imags), NN, preferred_element_type=F32)
        r0, r1, r2 = (sums_real[b * refs : (b + 1) * refs] for b in range(3))
        i0, i1, i2 = (sums_imag[b * refs : (b + 1) * refs] for b in range(3))
        lines = [n * (width // 128) + tile for tile in range(width // 128)]
        cos_y = jnp.concatenate([cos_rows[line : line + 1] for line in lines], axis=1)
        sin_y = jnp.concatenate([sin_rows[line : line + 1] for line in lines], axis=1)
        both = (
            r1 * scale + (r0 + r2) * cos_y + (i2 - i0) * sin_y,
            i1 * scale + (i0 + i2) * cos_y + (r0 - r2) * sin_y,
        )
        for tile in range(width // 128):
            for c in range(2):
                first = 2 * (n * (width // 128) + tile) + c
                data_ref[pl.ds(first, refs, stride=2 * (QUART // 128)), :] = both[c][:, 128 * tile : 128 * (tile + 1)]
        ctf_power = ctf_power_rows(picks, tables_ref[:, wide_at])
        weight_ref[:, at] = lax.dot_general(sum_ref[...], ctf_power, NN, preferred_element_type=F32) * scale


def on_device(images, offsets, groups, defocus, refs, log_prior, noise_inv, ctf_table):
    count_refs = refs.shape[0]
    size = {name: lax.axis_size(name) for name in AXES}
    orients = size["x"] * size["yh"] * size["zh"] * size["zl"]
    devices = orients * size["yl"] * size["c"]
    scale = 25.0 * (count_refs * orients) / devices
    at = {name: lax.axis_index(name) for name in AXES}
    dom = at["yl"] * size["c"] + at["c"]
    orient = ((at["x"] * size["yh"] + at["yh"]) * size["zh"] + at["zh"]) * size["zl"] + at["zl"]
    mine = ((at["yh"] * size["zl"] + at["zl"]) * size["x"] + at["x"]) * size["zh"] + at["zh"]
    place = jnp.stack([dom, orient, at["yh"], at["zl"], mine]).astype(jnp.int32)

    smem = pl.BlockSpec(memory_space=pltpu.SMEM)
    vmem = pl.BlockSpec(memory_space=pltpu.VMEM)
    hbm = pl.BlockSpec(memory_space=pltpu.HBM)
    shape = jax.ShapeDtypeStruct
    line = 8 * size["x"] * size["zh"]
    payload = pl.pallas_call(
        prep_kernel,
        in_specs=[smem] * 3 + [hbm] * 3,
        out_specs=vmem,
        out_shape=shape((line, WIDE), BF16),
        scratch_shapes=[
            pltpu.VMEM((1, 2, PIX), BF16),
            pltpu.VMEM((GROUPS, PIX), F32),
            pltpu.VMEM((8, PIX), F32),
            pltpu.SemaphoreType.DMA((3,)),
        ],
        compiler_params=params(VMEM_ALL),
        name="prep",
    )(jnp.transpose(offsets, (0, 2, 1))[0], groups, defocus, images, noise_inv, ctf_table)
    flip = [(i, 3 - i) for i in range(4)]
    own = lax.all_to_all(payload, ("x", "zh"), 0, 0, tiled=True)
    side = lax.ppermute(own, "zl", [(0, 1), (1, 0)])
    far = lax.ppermute(own, ("yh", "yl"), flip)

    flat = refs.reshape(count_refs, 2 * PIX)
    tables = pl.pallas_call(
        tables_kernel,
        in_specs=[vmem] * 2,
        out_specs=vmem,
        out_shape=shape((TABLE_ROWS, PIX), BF16),
        compiler_params=params(VMEM_LIMIT // 3),
        name="tables",
    )(ctf_table, noise_inv)
    side, _, flat = lax.optimization_barrier((side, far, flat))
    corner = lax.ppermute(side, ("yh", "yl"), flip)

    early = pl.pallas_call(
        quarter_kernel,
        in_specs=[smem] + [vmem] * 2,
        out_specs=[vmem] * 4,
        out_shape=[shape((orients, WIDE), BF16)] * 4,
        scratch_shapes=[pltpu.VMEM((4 * orients * (WIDE // 128), 128), F32)],
        compiler_params=params(VMEM_LIMIT // 3),
        name="quarters",
    )(place, own, side)

    def share(parts):
        moves = [[(d, d ^ k) for d in range(4)] for k in range(4)]
        return parts[0:1] + [lax.ppermute(parts[k], ("yl", "c"), moves[k]) for k in range(1, 4)]

    early = list(early)
    flat, early[0] = lax.optimization_barrier((flat, early[0]))
    turned, power, column = pl.pallas_call(
        refs_kernel,
        in_specs=[vmem] * 2,
        out_specs=[vmem] * 3,
        out_shape=[
            shape((2, 3 * count_refs, PIX), BF16),
            shape((count_refs, PIX), BF16),
            shape((count_refs, 128), F32),
        ],
        scratch_shapes=[pltpu.VMEM((PIX // 128, 128), F32)] * 2,
        compiler_params=params(),
        cost_estimate=pl.CostEstimate(flops=8 * count_refs * PIX, bytes_accessed=10 << 20, transcendentals=0),
        name="turn_refs",
    )(flat, log_prior[None, :])
    early = share(early)

    box = (2 * orients, 5 * count_refs + QUART // 2)
    *boxes, stats = pl.pallas_call(
        score_kernel,
        in_specs=[smem] + [vmem] * 8,
        out_specs=[vmem] * 5,
        out_shape=[shape(box, BF16)] * 4 + [shape((devices, 2 * orients), F32)],
        scratch_shapes=[pltpu.VMEM((8 * orients * (WIDE // 128), 128), F32)],
        compiler_params=params(),
        cost_estimate=pl.CostEstimate(
            flops=18 * orients * count_refs * 2 * PIX, bytes_accessed=10 << 20, transcendentals=0
        ),
        name="score",
    )(place, own, side, far, corner, turned, power, tables, column)

    early, boxes, stats = lax.optimization_barrier((early, list(boxes), stats))
    boxes = share(boxes)
    stats_all = lax.all_to_all(stats, AXES, 0, 0, tiled=True)

    data, weight, evidence = pl.pallas_call(
        functools.partial(final_kernel, scale=scale),
        in_specs=[smem] + [vmem] * 10,
        out_specs=[vmem, vmem, smem],
        scratch_shapes=[
            pltpu.VMEM((3 * count_refs, 12 * orients), BF16),
            pltpu.VMEM((count_refs, 4 * orients), BF16),
        ],
        out_shape=[
            shape((2 * count_refs * (QUART // 128), 128), F32),
            shape((count_refs, QUART), F32),
            shape((1,), F32),
        ],
        compiler_params=params(),
        name="insert",
    )(place, *early, *boxes, stats_all, tables)
    data = jnp.transpose(data.reshape(count_refs, QUART // 128, 2, 128), (0, 2, 1, 3))
    return data.reshape(count_refs, 2, QUART), weight, evidence


def solution(mesh):
    fine = Mesh(mesh.devices.reshape(4, 2, 4, 2, 2, 2), AXES)
    orient = AXES[0:4]
    dom = AXES[4:6]
    return jax.shard_map(
        on_device,
        mesh=fine,
        in_specs=(
            P(AXES, None, None),
            P(AXES, None, None),
            P(AXES),
            P(AXES),
            P(orient, None, None),
            P(orient),
            P(),
            P(),
        ),
        out_specs=(P(orient, None, dom), P(orient, dom), P(AXES)),
        check_vma=False,
    )
```

```python
import functools
import math

import jax
import jax.numpy as jnp
from jax import lax
from jax.experimental import pallas as pl
from jax.experimental.pallas import tpu as pltpu
from jax.sharding import Mesh
from jax.sharding import PartitionSpec as P

SIDE = 64
PIX = SIDE * SIDE
QUART = PIX // 4
META = 128
WIDE = QUART + META
DEFS = 64
GROUPS = 8
TWO_PI = 2.0 * math.pi
TRANS_VAR = 8.0
F32 = jnp.float32
BF16 = jnp.bfloat16
NT = (((1,), (1,)), ((), ()))
NN = (((1,), (0,)), ((), ()))
AXES = ("x", "yh", "zh", "zl", "yl", "c")
TABLE_ROWS = 3 * DEFS + 4 * GROUPS
VMEM_LIMIT = 24 * 1024 * 1024
VMEM_ALL = 61 * 1024 * 1024


def phases(step):
    freq = (step + SIDE // 2 & SIDE - 1) - SIDE // 2
    angle = (2 * freq & SIDE - 1).astype(F32) * (TWO_PI / SIDE)
    return jnp.cos(angle), jnp.sin(angle)


def phases_x(width):
    cosine, sine = phases(lax.broadcasted_iota(jnp.int32, (8, 128), 1) & SIDE - 1)
    many = width // 128
    return jnp.concatenate([cosine[0:1]] * many, axis=1), jnp.concatenate([sine[0:1]] * many, axis=1)


def phases_y(first, rows):
    line = lax.broadcasted_iota(jnp.int32, (rows, 128), 0)
    lane = lax.broadcasted_iota(jnp.int32, (rows, 128), 1)
    return phases((first + 128 * line + lane) // SIDE)


def params(limit=VMEM_LIMIT):
    return pltpu.CompilerParams(vmem_limit_bytes=limit)


def prep_kernel(
    offsets, groups, defocus, image_hbm, noise_hbm, ctf_hbm, out_ref, image_ref, noise_ref, ctf_ref, sems
):
    group, focus, centre_x, centre_y = groups[0], defocus[0], offsets[0, 4], offsets[1, 4]
    start = pl.multiple_of(focus // 8 * 8, 8)
    copies = [
        pltpu.make_async_copy(ctf_hbm.at[pl.ds(start, 8)], ctf_ref, sems.at[0]),
        pltpu.make_async_copy(noise_hbm, noise_ref, sems.at[1]),
        pltpu.make_async_copy(image_hbm, image_ref, sems.at[2]),
    ]
    for copy in copies:
        copy.start()
    lane = lax.broadcasted_iota(jnp.int32, (4, QUART), 1)
    row = lax.broadcasted_iota(jnp.int32, (4, QUART), 0)
    freq_x = ((lane & 63) + 32 & 63) - 32
    freq_y = ((row * (QUART // SIDE) + (lane >> 6)) + 32 & 63) - 32
    angle = ((freq_x * centre_x + freq_y * centre_y) & 63).astype(F32) * (TWO_PI / SIDE)
    cosine = jnp.cos(angle)
    sine = jnp.sin(angle)
    spot = lax.broadcasted_iota(jnp.int32, (8, META), 1)
    meta = jnp.where(
        spot == 0,
        group,
        jnp.where(spot == 1, focus, jnp.where(spot == 2, centre_x, jnp.where(spot == 3, centre_y, 0))),
    ).astype(F32)
    for copy in copies:
        copy.wait()
    rows = lax.broadcasted_iota(jnp.int32, (8, PIX), 0)
    noise = jnp.sum(jnp.where(rows == group, noise_ref[...], 0.0), axis=0, keepdims=True)
    ctf = jnp.sum(jnp.where(rows == focus % 8, ctf_ref[...], 0.0), axis=0, keepdims=True)
    weighted = (image_ref[0].astype(F32) * (noise * ctf)).astype(BF16).astype(F32)
    real = jnp.concatenate([weighted[0:1, j * QUART : (j + 1) * QUART] for j in range(4)], axis=0)
    imag = jnp.concatenate([weighted[1:2, j * QUART : (j + 1) * QUART] for j in range(4)], axis=0)
    body = jnp.concatenate([real * cosine + imag * sine, imag * cosine - real * sine], axis=0)
    one = jnp.concatenate([body, meta], axis=1)
    pair = jnp.concatenate([one, one], axis=0).astype(BF16)
    for k in range(out_ref.shape[0] // 16):
        out_ref[16 * k : 16 * (k + 1), :] = pair


def tables_kernel(ctf_ref, noise_ref, tables_ref):
    def split(table):
        first = table.astype(BF16).astype(F32)
        second = (table - first).astype(BF16).astype(F32)
        return [first, second, table - first - second]

    noise = split(noise_ref[...])
    rows = split(ctf_ref[...]) + noise + [jnp.zeros_like(noise[0])]
    tables_ref[...] = jnp.concatenate(rows, axis=0).astype(BF16)


def refs_kernel(flat_ref, prior_ref, turned_ref, power_ref, column_ref, cos_ref, sin_ref):
    count = flat_ref.shape[0]
    width = 256
    cos_ref[...], sin_ref[...] = phases_y(0, PIX // 128)

    def body(step, carry):
        at = pl.ds(pl.multiple_of(step * width, width), width)
        low = flat_ref[:, at]
        high = flat_ref[:, pl.ds(pl.multiple_of(PIX + step * width, width), width)]
        real = low.astype(F32)
        imag = high.astype(F32)
        lines = [pl.ds(step * (width // 128) + k, 1) for k in range(width // 128)]
        cosine = jnp.concatenate([cos_ref[line, :] for line in lines], axis=1)
        sine = jnp.concatenate([sin_ref[line, :] for line in lines], axis=1)
        rc, rs, ic, si = real * cosine, real * sine, imag * cosine, imag * sine
        turned_ref[0, 0:count, at] = (rc + si).astype(BF16)
        turned_ref[1, 0:count, at] = (ic - rs).astype(BF16)
        turned_ref[0, count : 2 * count, at] = low
        turned_ref[1, count : 2 * count, at] = high
        turned_ref[0, 2 * count : 3 * count, at] = (rc - si).astype(BF16)
        turned_ref[1, 2 * count : 3 * count, at] = (ic + rs).astype(BF16)
        power_ref[:, at] = (real * real + imag * imag).astype(BF16)
        return carry

    lax.fori_loop(0, PIX // width, body, 0)
    line = lax.broadcasted_iota(jnp.int32, (count, count), 0)
    lane = lax.broadcasted_iota(jnp.int32, (count, count), 1)
    column = jnp.sum(jnp.where(lane == line, prior_ref[...], 0.0), axis=1, keepdims=True)
    column_ref[...] = jnp.broadcast_to(column, column_ref.shape)


def table_picks(group, focus):
    spot = lax.broadcasted_iota(jnp.int32, (group.shape[0], TABLE_ROWS), 1)
    ctf = (spot < 3 * DEFS) & (spot % DEFS == focus.astype(jnp.int32))
    noise = (spot >= 3 * DEFS) & (spot < 3 * (DEFS + GROUPS)) & (spot % GROUPS == group.astype(jnp.int32))
    return jnp.concatenate([ctf.astype(F32), noise.astype(F32)], axis=0).astype(BF16)


def ctf_power_rows(picks, tables):
    rows = lax.dot_general(picks, tables, NN, preferred_element_type=F32)
    count = rows.shape[0] // 2
    ctf, noise = rows[0:count], rows[count:]
    return (noise * ctf * ctf).astype(BF16)


def shift_x(real, imag, cosine, sine):
    rc, rs, ic, si = real * cosine, real * sine, imag * cosine, imag * sine
    return (rc - si, real, rc + si), (ic + rs, imag, ic - rs)


def unpack(parts, wide_ref):
    size = parts[0].shape[0]
    whole = size * len(parts)
    for spot, part in enumerate(parts):
        for tile in range(WIDE // 128):
            start = whole * tile + size * spot
            wide_ref[start : start + size, :] = part[:, 128 * tile : 128 * (tile + 1)].astype(F32)

    def chunk(row, first, count):
        tiles = [
            wide_ref[pl.ds(whole * tile + 8 * first + row, count, stride=8), :] for tile in range(QUART // 128)
        ]
        return jnp.concatenate(tiles, axis=1)

    def codes(first, count):
        return wide_ref[pl.ds(whole * (QUART // 128) + 8 * first, count, stride=8), :]

    return chunk, codes


def swap_lanes(row, step, flag):
    lane = lax.broadcasted_iota(jnp.int32, row.shape, 1)
    width = row.shape[1]
    other = jnp.where((lane & step) == 0, pltpu.roll(row, width - step, 1), pltpu.roll(row, step, 1))
    return jnp.where(flag == 1, other, row)


def quarter_kernel(place, own_ref, side_ref, flat_ref, q0_ref, q1_ref, q2_ref, q3_ref, wide_ref):
    outs = (q0_ref, q1_ref, q2_ref, q3_ref)
    count = 2 * own_ref.shape[0] // 8
    chunk, codes = unpack((own_ref, side_ref), wide_ref)
    meta = codes(0, count)
    both = jnp.concatenate([meta, meta], axis=0).astype(BF16)
    for k in range(4):
        part = place[0] ^ k
        outs[k][:, 0:QUART] = jnp.concatenate([chunk(part, 0, count), chunk(part + 4, 0, count)], axis=0).astype(BF16)
        outs[k][:, QUART:WIDE] = both


def score_kernel(
    place, own_ref, side_ref, far_ref, corner_ref, turned_ref, power_ref, tables_ref, column_ref,
    q0_ref, q1_ref, q2_ref, q3_ref, stats_ref, wide_ref,
):
    outs = (q0_ref, q1_ref, q2_ref, q3_ref)
    count = 4 * own_ref.shape[0] // 8
    half = count // 2
    refs = power_ref.shape[0]
    chunk, codes = unpack((own_ref, side_ref, far_ref, corner_ref), wide_ref)
    meta = codes(0, count)
    picks = table_picks(meta[:, 0:1], meta[:, 1:2])
    cos_x, sin_x = phases_x(QUART)
    cross = jnp.zeros((3 * refs, 3 * count), F32)
    self_term = jnp.zeros((refs, count), F32)
    for j in range(4):
        at = slice(j * QUART, (j + 1) * QUART)
        ctf_power = ctf_power_rows(picks, tables_ref[:, at])
        self_term += lax.dot_general(power_ref[:, at], ctf_power, NT, preferred_element_type=F32)
    for j in range(4):
        at = slice(j * QUART, (j + 1) * QUART)
        for c, parts in enumerate(shift_x(chunk(j, 0, count), chunk(j + 4, 0, count), cos_x, sin_x)):
            new = jnp.concatenate(parts, axis=0).astype(BF16)
            cross += lax.dot_general(turned_ref[c, :, at], new, NT, preferred_element_type=F32)
        part = place[0] ^ j
        late = jnp.concatenate([chunk(part, half, half), chunk(part + 4, half, half)], axis=0).astype(BF16)
        for side in range(2):
            outs[j][side * count : (side + 1) * count, 5 * refs : 5 * refs + QUART // 2] = late[
                :, side * QUART // 2 : (side + 1) * QUART // 2
            ]

    base = column_ref[:, 0:count] - 0.5 * self_term
    base_pair = jnp.concatenate([base, base], axis=1)
    turned_codes = meta.T
    centre_x, centre_y = turned_codes[2:3, :], turned_codes[3:4, :]

    def offset_term(a, b):
        off_x = centre_x + (2.0 * a - 2.0)
        off_y = centre_y + (2.0 * b - 2.0)
        return (off_x * off_x + off_y * off_y) / (2.0 * TRANS_VAR)

    pairs, singles = [], []
    for b in range(3):
        value = cross[b * refs : (b + 1) * refs]
        pairs.append(
            value[:, 0 : 2 * count] + base_pair - jnp.concatenate([offset_term(0, b), offset_term(1, b)], axis=1)
        )
        singles.append(value[:, 2 * count :] + base - offset_term(2, b))
    top_pair = jnp.max(jnp.maximum(jnp.maximum(pairs[0], pairs[1]), pairs[2]), axis=0, keepdims=True)
    top = jnp.max(jnp.maximum(jnp.maximum(singles[0], singles[1]), singles[2]), axis=0, keepdims=True)
    top = jnp.maximum(top, jnp.maximum(top_pair[:, 0:count], top_pair[:, count:]))
    top_pair = jnp.concatenate([top, top], axis=1)
    pairs = [jnp.exp(value - top_pair) for value in pairs]
    singles = [jnp.exp(value - top) for value in singles]
    mass_pair = jnp.sum(pairs[0] + pairs[1] + pairs[2], axis=0, keepdims=True)
    mass = jnp.sum(singles[0] + singles[1] + singles[2], axis=0, keepdims=True)
    mass = mass + mass_pair[:, 0:count] + mass_pair[:, count:]
    total = top + jnp.log(mass)
    row = jnp.concatenate([total, top], axis=1)
    row = swap_lanes(swap_lanes(row, half, place[2]), half // 2, place[3])
    stats_ref[...] = jnp.broadcast_to(row, stats_ref.shape)
    last = jnp.concatenate(singles[0:2], axis=1)
    notes = jnp.concatenate([meta[half:, 0:count], jnp.zeros((refs - half, count), F32)], axis=0)
    ends = jnp.concatenate([singles[2], notes], axis=1), jnp.concatenate([notes, singles[2]], axis=1)
    for k in range(4):
        for b in range(3):
            outs[k][:, b * refs : (b + 1) * refs] = pairs[b].astype(BF16)
        outs[k][:, 3 * refs : 4 * refs] = last.astype(BF16)
        outs[k][:, 4 * refs : 5 * refs] = ends[k % 2].astype(BF16)


def final_kernel(
    place, e0_ref, e1_ref, e2_ref, e3_ref, q0_ref, q1_ref, q2_ref, q3_ref, stats_ref, tables_ref,
    data_ref, weight_ref, evidence_ref, post_ref, sum_ref, power_ref, *, scale,
):
    dom, orient, y_hi, z_lo, mine = place[0], place[1], place[2], place[3], place[4]
    early = (e0_ref, e1_ref, e2_ref, e3_ref)
    boxes = (q0_ref, q1_ref, q2_ref, q3_ref)
    doms = 4
    count = q0_ref.shape[0] // 2
    half = count // 2
    refs = sum_ref.shape[0]
    pair = 2 * count
    orients = stats_ref.shape[0] // doms
    lane = lax.broadcasted_iota(jnp.int32, (1, pair), 1)
    left = lane < count
    upper = (lax.broadcasted_iota(jnp.int32, (orients, pair), 0) & 8) != 0
    factors, groups, foci = [], [], []
    for k in range(doms):
        start = dom ^ k ^ (2 * y_hi)
        table = jnp.where(
            upper,
            stats_ref[pl.ds(start ^ 2, orients, stride=doms), :],
            stats_ref[pl.ds(start, orients, stride=doms), :],
        )
        top = jnp.max(table, axis=0, keepdims=True)
        evidence = top + jnp.log(jnp.sum(jnp.exp(table - top), axis=0, keepdims=True))
        own = stats_ref[pl.ds(orient * doms + (dom ^ k), 1), :]
        factor = jnp.exp(pltpu.roll(own, count, 1) - evidence)
        factor = swap_lanes(swap_lanes(factor, half, y_hi), half // 2, z_lo)
        factors.append(jnp.where(left, factor, pltpu.roll(factor, count, 1)))
        if k == 0:
            evidence_ref[0] = jnp.sum(jnp.where(lane == mine, evidence, 0.0))
        notes = boxes[k][0:half, 4 * refs : 5 * refs].astype(F32)
        first = early[k][0:half, QUART:WIDE].astype(F32)
        spot = count if k % 2 == 0 else 0
        groups += [first[:, 0:1], notes[:, spot : spot + 1]]
        foci += [first[:, 1:2], notes[:, spot + 1 : spot + 2]]

    picks = table_picks(jnp.concatenate(groups, axis=0), jnp.concatenate(foci, axis=0))
    for n in range(4):
        at = slice(n * QUART // 4, (n + 1) * QUART // 4)
        start = pl.multiple_of(dom * QUART + n * QUART // 4, QUART // 4)
        power_ref[:, at] = ctf_power_rows(picks, tables_ref[:, pl.ds(start, QUART // 4)])

    def fill(pieces, spot):
        total = jnp.zeros((refs, pair), F32)
        for b in range(3):
            post = pieces[b].astype(BF16)
            post_ref[b * refs : (b + 1) * refs, spot : spot + pair] = post
            total = total + post.astype(F32)
        return total

    def block(k, number):
        return boxes[k][:, number * refs : (number + 1) * refs].astype(F32) * factors[k]

    totals = []
    for k in range(doms):
        total = fill([block(k, b) for b in range(3)], k * pair)
        totals.append(total + pltpu.roll(total, count, 1))
    for k in range(0, doms, 2):
        even, odd = block(k, 3), block(k + 1, 3)
        pieces = [
            jnp.where(left, even, pltpu.roll(odd, count, 1)),
            jnp.where(left, pltpu.roll(even, count, 1), odd),
            jnp.where(left, block(k, 4), block(k + 1, 4)),
        ]
        total = fill(pieces, (doms + k // 2) * pair) + jnp.where(left, totals[k], totals[k + 1])
        sum_ref[:, k * count : (k + 2) * count] = total.astype(BF16)

    width = 512
    cos_x, sin_x = phases_x(width)
    cos_rows, sin_rows = phases_y(dom * QUART, QUART // 128)
    cos_rows, sin_rows = cos_rows * scale, sin_rows * scale
    for n in range(QUART // width):
        at = slice(n * width, (n + 1) * width)
        reals, imags = [], []
        side = 2 * n * width // QUART
        late_at = slice(5 * refs + n * width - side * QUART // 2, 5 * refs + (n + 1) * width - side * QUART // 2)
        for k in range(doms):
            late = boxes[k][side * count : (side + 1) * count, late_at].astype(F32)
            soon = early[k][:, at].astype(F32)
            real = jnp.concatenate([soon[0:half], late[0:half]], axis=0)
            imag = jnp.concatenate([soon[half:], late[half:]], axis=0)
            new_real, new_imag = shift_x(real, imag, cos_x, sin_x)
            reals.append([part.astype(BF16) for part in new_real])
            imags.append([part.astype(BF16) for part in new_imag])

        def stack(parts):
            first = [parts[k][a] for k in range(doms) for a in range(2)]
            return jnp.concatenate(first + [parts[k][2] for k in range(doms)], axis=0)

        sums_real = lax.dot_general(post_ref[...], stack(reals), NN, preferred_element_type=F32)
        sums_imag = lax.dot_general(post_ref[...], stack(imags), NN, preferred_element_type=F32)
        r0, r1, r2 = (sums_real[b * refs : (b + 1) * refs] for b in range(3))
        i0, i1, i2 = (sums_imag[b * refs : (b + 1) * refs] for b in range(3))
        lines = [n * (width // 128) + tile for tile in range(width // 128)]
        cos_y = jnp.concatenate([cos_rows[line : line + 1] for line in lines], axis=1)
        sin_y = jnp.concatenate([sin_rows[line : line + 1] for line in lines], axis=1)
        both = (
            r1 * scale + (r0 + r2) * cos_y + (i2 - i0) * sin_y,
            i1 * scale + (i0 + i2) * cos_y + (r0 - r2) * sin_y,
        )
        for tile in range(width // 128):
            for c in range(2):
                first = 2 * (n * (width // 128) + tile) + c
                data_ref[pl.ds(first, refs, stride=2 * (QUART // 128)), :] = both[c][:, 128 * tile : 128 * (tile + 1)]
        weight_ref[:, at] = lax.dot_general(sum_ref[...], power_ref[:, at], NN, preferred_element_type=F32) * scale


def on_device(images, offsets, groups, defocus, refs, log_prior, noise_inv, ctf_table):
    count_refs = refs.shape[0]
    size = {name: lax.axis_size(name) for name in AXES}
    orients = size["x"] * size["yh"] * size["zh"] * size["zl"]
    devices = orients * size["yl"] * size["c"]
    scale = 25.0 * (count_refs * orients) / devices
    at = {name: lax.axis_index(name) for name in AXES}
    dom = at["yl"] * size["c"] + at["c"]
    orient = ((at["x"] * size["yh"] + at["yh"]) * size["zh"] + at["zh"]) * size["zl"] + at["zl"]
    mine = ((at["yh"] * size["zl"] + at["zl"]) * size["x"] + at["x"]) * size["zh"] + at["zh"]
    place = jnp.stack([dom, orient, at["yh"], at["zl"], mine]).astype(jnp.int32)

    smem = pl.BlockSpec(memory_space=pltpu.SMEM)
    vmem = pl.BlockSpec(memory_space=pltpu.VMEM)
    hbm = pl.BlockSpec(memory_space=pltpu.HBM)
    shape = jax.ShapeDtypeStruct
    line = 8 * size["x"] * size["zh"]
    payload = pl.pallas_call(
        prep_kernel,
        in_specs=[smem] * 3 + [hbm] * 3,
        out_specs=vmem,
        out_shape=shape((line, WIDE), BF16),
        scratch_shapes=[
            pltpu.VMEM((1, 2, PIX), BF16),
            pltpu.VMEM((GROUPS, PIX), F32),
            pltpu.VMEM((8, PIX), F32),
            pltpu.SemaphoreType.DMA((3,)),
        ],
        compiler_params=params(VMEM_ALL),
        name="prep",
    )(jnp.transpose(offsets, (0, 2, 1))[0], groups, defocus, images, noise_inv, ctf_table)
    flip = [(i, 3 - i) for i in range(4)]
    own = lax.all_to_all(payload, ("x", "zh"), 0, 0, tiled=True)
    side = lax.ppermute(own, "zl", [(0, 1), (1, 0)])
    far = lax.ppermute(own, ("yh", "yl"), flip)

    flat = refs.reshape(count_refs, 2 * PIX)
    flat, ctf_late, noise_late = lax.optimization_barrier((flat, ctf_table, noise_inv))
    tables = pl.pallas_call(
        tables_kernel,
        in_specs=[vmem] * 2,
        out_specs=vmem,
        out_shape=shape((TABLE_ROWS, PIX), BF16),
        compiler_params=params(VMEM_LIMIT // 3),
        name="tables",
    )(ctf_late, noise_late)
    side, _, flat, tables = lax.optimization_barrier((side, far, flat, tables))
    corner = lax.ppermute(side, ("yh", "yl"), flip)

    early = pl.pallas_call(
        quarter_kernel,
        in_specs=[smem] + [vmem] * 3,
        out_specs=[vmem] * 4,
        out_shape=[shape((orients, WIDE), BF16)] * 4,
        scratch_shapes=[pltpu.VMEM((4 * orients * (WIDE // 128), 128), F32)],
        compiler_params=params(VMEM_LIMIT // 3),
        name="quarters",
    )(place, own, side, flat)

    def share(parts):
        moves = [[(d, d ^ k) for d in range(4)] for k in range(4)]
        return parts[0:1] + [lax.ppermute(parts[k], ("yl", "c"), moves[k]) for k in range(1, 4)]

    early = list(early)
    flat, early[0] = lax.optimization_barrier((flat, early[0]))
    turned, power, column = pl.pallas_call(
        refs_kernel,
        in_specs=[vmem] * 2,
        out_specs=[vmem] * 3,
        out_shape=[
            shape((2, 3 * count_refs, PIX), BF16),
            shape((count_refs, PIX), BF16),
            shape((count_refs, 128), F32),
        ],
        scratch_shapes=[pltpu.VMEM((PIX // 128, 128), F32)] * 2,
        compiler_params=params(),
        cost_estimate=pl.CostEstimate(flops=8 * count_refs * PIX, bytes_accessed=10 << 20, transcendentals=0),
        name="turn_refs",
    )(flat, log_prior[None, :])
    early = share(early)

    box = (2 * orients, 5 * count_refs + QUART // 2)
    *boxes, stats = pl.pallas_call(
        score_kernel,
        in_specs=[smem] + [vmem] * 8,
        out_specs=[vmem] * 5,
        out_shape=[shape(box, BF16)] * 4 + [shape((devices, 2 * orients), F32)],
        scratch_shapes=[pltpu.VMEM((8 * orients * (WIDE // 128), 128), F32)],
        compiler_params=params(),
        cost_estimate=pl.CostEstimate(
            flops=18 * orients * count_refs * 2 * PIX, bytes_accessed=10 << 20, transcendentals=0
        ),
        name="score",
    )(place, own, side, far, corner, turned, power, tables, column)

    early, boxes, stats = lax.optimization_barrier((early, list(boxes), stats))
    boxes = share(boxes)
    stats_all = lax.all_to_all(stats, AXES, 0, 0, tiled=True)

    data, weight, evidence = pl.pallas_call(
        functools.partial(final_kernel, scale=scale),
        in_specs=[smem] + [vmem] * 10,
        out_specs=[vmem, vmem, smem],
        scratch_shapes=[
            pltpu.VMEM((3 * count_refs, 12 * orients), BF16),
            pltpu.VMEM((count_refs, 4 * orients), BF16),
            pltpu.VMEM((4 * orients, QUART), BF16),
        ],
        out_shape=[
            shape((2 * count_refs * (QUART // 128), 128), F32),
            shape((count_refs, QUART), F32),
            shape((1,), F32),
        ],
        compiler_params=params(),
        name="insert",
    )(place, *early, *boxes, stats_all, tables)
    data = jnp.transpose(data.reshape(count_refs, QUART // 128, 2, 128), (0, 2, 1, 3))
    return data.reshape(count_refs, 2, QUART), weight, evidence


def solution(mesh):
    fine = Mesh(mesh.devices.reshape(4, 2, 4, 2, 2, 2), AXES)
    orient = AXES[0:4]
    dom = AXES[4:6]
    return jax.shard_map(
        on_device,
        mesh=fine,
        in_specs=(
            P(AXES, None, None),
            P(AXES, None, None),
            P(AXES),
            P(AXES),
            P(orient, None, None),
            P(orient),
            P(),
            P(),
        ),
        out_specs=(P(orient, None, dom), P(orient, dom), P(AXES)),
        check_vma=False,
    )
```

```python
import functools
import math

import jax
import jax.numpy as jnp
from jax import lax
from jax.experimental import pallas as pl
from jax.experimental.pallas import tpu as pltpu
from jax.sharding import Mesh
from jax.sharding import PartitionSpec as P

SIDE = 64
PIX = SIDE * SIDE
QUART = PIX // 4
META = 128
WIDE = QUART + META
DEFS = 64
GROUPS = 8
TWO_PI = 2.0 * math.pi
TRANS_VAR = 8.0
F32 = jnp.float32
BF16 = jnp.bfloat16
NT = (((1,), (1,)), ((), ()))
NN = (((1,), (0,)), ((), ()))
AXES = ("x", "yh", "zh", "zl", "yl", "c")
TABLE_ROWS = 3 * DEFS + 4 * GROUPS
VMEM_LIMIT = 24 * 1024 * 1024
VMEM_ALL = 61 * 1024 * 1024


def phases(step):
    freq = (step + SIDE // 2 & SIDE - 1) - SIDE // 2
    angle = (2 * freq & SIDE - 1).astype(F32) * (TWO_PI / SIDE)
    return jnp.cos(angle), jnp.sin(angle)


def phases_x(width):
    cosine, sine = phases(lax.broadcasted_iota(jnp.int32, (8, 128), 1) & SIDE - 1)
    many = width // 128
    return jnp.concatenate([cosine[0:1]] * many, axis=1), jnp.concatenate([sine[0:1]] * many, axis=1)


def phases_y(first, rows):
    line = lax.broadcasted_iota(jnp.int32, (rows, 128), 0)
    lane = lax.broadcasted_iota(jnp.int32, (rows, 128), 1)
    return phases((first + 128 * line + lane) // SIDE)


def params(limit=VMEM_LIMIT):
    return pltpu.CompilerParams(vmem_limit_bytes=limit)


def prep_kernel(
    offsets, groups, defocus, image_hbm, noise_hbm, ctf_hbm, out_ref, image_ref, noise_ref, ctf_ref, sems
):
    group, focus, centre_x, centre_y = groups[0], defocus[0], offsets[0, 4], offsets[1, 4]
    start = pl.multiple_of(focus // 8 * 8, 8)
    copies = [
        pltpu.make_async_copy(ctf_hbm.at[pl.ds(start, 8)], ctf_ref, sems.at[0]),
        pltpu.make_async_copy(noise_hbm, noise_ref, sems.at[1]),
        pltpu.make_async_copy(image_hbm, image_ref, sems.at[2]),
    ]
    for copy in copies:
        copy.start()
    lane = lax.broadcasted_iota(jnp.int32, (4, QUART), 1)
    row = lax.broadcasted_iota(jnp.int32, (4, QUART), 0)
    freq_x = ((lane & 63) + 32 & 63) - 32
    freq_y = ((row * (QUART // SIDE) + (lane >> 6)) + 32 & 63) - 32
    angle = ((freq_x * centre_x + freq_y * centre_y) & 63).astype(F32) * (TWO_PI / SIDE)
    cosine = jnp.cos(angle)
    sine = jnp.sin(angle)
    spot = lax.broadcasted_iota(jnp.int32, (8, META), 1)
    meta = jnp.where(
        spot == 0,
        group,
        jnp.where(spot == 1, focus, jnp.where(spot == 2, centre_x, jnp.where(spot == 3, centre_y, 0))),
    ).astype(F32)
    for copy in copies:
        copy.wait()
    rows = lax.broadcasted_iota(jnp.int32, (8, PIX), 0)
    noise = jnp.sum(jnp.where(rows == group, noise_ref[...], 0.0), axis=0, keepdims=True)
    ctf = jnp.sum(jnp.where(rows == focus % 8, ctf_ref[...], 0.0), axis=0, keepdims=True)
    weighted = (image_ref[0].astype(F32) * (noise * ctf)).astype(BF16).astype(F32)
    real = jnp.concatenate([weighted[0:1, j * QUART : (j + 1) * QUART] for j in range(4)], axis=0)
    imag = jnp.concatenate([weighted[1:2, j * QUART : (j + 1) * QUART] for j in range(4)], axis=0)
    body = jnp.concatenate([real * cosine + imag * sine, imag * cosine - real * sine], axis=0)
    one = jnp.concatenate([body, meta], axis=1)
    pair = jnp.concatenate([one, one], axis=0).astype(BF16)
    for k in range(out_ref.shape[0] // 16):
        out_ref[16 * k : 16 * (k + 1), :] = pair


def tables_kernel(ctf_ref, noise_ref, tables_ref):
    def split(table):
        first = table.astype(BF16).astype(F32)
        second = (table - first).astype(BF16).astype(F32)
        return [first, second, table - first - second]

    noise = split(noise_ref[...])
    rows = split(ctf_ref[...]) + noise + [jnp.zeros_like(noise[0])]
    tables_ref[...] = jnp.concatenate(rows, axis=0).astype(BF16)


def refs_kernel(flat_ref, prior_ref, turned_ref, power_ref, column_ref, cos_ref, sin_ref):
    count = flat_ref.shape[0]
    width = 256
    cos_ref[...], sin_ref[...] = phases_y(0, PIX // 128)

    def body(step, carry):
        at = pl.ds(pl.multiple_of(step * width, width), width)
        low = flat_ref[:, at]
        high = flat_ref[:, pl.ds(pl.multiple_of(PIX + step * width, width), width)]
        real = low.astype(F32)
        imag = high.astype(F32)
        lines = [pl.ds(step * (width // 128) + k, 1) for k in range(width // 128)]
        cosine = jnp.concatenate([cos_ref[line, :] for line in lines], axis=1)
        sine = jnp.concatenate([sin_ref[line, :] for line in lines], axis=1)
        rc, rs, ic, si = real * cosine, real * sine, imag * cosine, imag * sine
        turned_ref[0, 0:count, at] = (rc + si).astype(BF16)
        turned_ref[1, 0:count, at] = (ic - rs).astype(BF16)
        turned_ref[0, count : 2 * count, at] = low
        turned_ref[1, count : 2 * count, at] = high
        turned_ref[0, 2 * count : 3 * count, at] = (rc - si).astype(BF16)
        turned_ref[1, 2 * count : 3 * count, at] = (ic + rs).astype(BF16)
        power_ref[:, at] = (real * real + imag * imag).astype(BF16)
        return carry

    lax.fori_loop(0, PIX // width, body, 0)
    line = lax.broadcasted_iota(jnp.int32, (count, count), 0)
    lane = lax.broadcasted_iota(jnp.int32, (count, count), 1)
    column = jnp.sum(jnp.where(lane == line, prior_ref[...], 0.0), axis=1, keepdims=True)
    column_ref[...] = jnp.broadcast_to(column, column_ref.shape)


def table_picks(group, focus):
    spot = lax.broadcasted_iota(jnp.int32, (group.shape[0], TABLE_ROWS), 1)
    ctf = (spot < 3 * DEFS) & (spot % DEFS == focus.astype(jnp.int32))
    noise = (spot >= 3 * DEFS) & (spot < 3 * (DEFS + GROUPS)) & (spot % GROUPS == group.astype(jnp.int32))
    return jnp.concatenate([ctf.astype(F32), noise.astype(F32)], axis=0).astype(BF16)


def ctf_power_rows(picks, tables):
    rows = lax.dot_general(picks, tables, NN, preferred_element_type=F32)
    count = rows.shape[0] // 2
    ctf, noise = rows[0:count], rows[count:]
    return (noise * ctf * ctf).astype(BF16)


def shift_x(real, imag, cosine, sine):
    rc, rs, ic, si = real * cosine, real * sine, imag * cosine, imag * sine
    return (rc - si, real, rc + si), (ic + rs, imag, ic - rs)


def unpack(parts, wide_ref):
    size = parts[0].shape[0]
    whole = size * len(parts)
    for spot, part in enumerate(parts):
        for tile in range(WIDE // 128):
            start = whole * tile + size * spot
            wide_ref[start : start + size, :] = part[:, 128 * tile : 128 * (tile + 1)].astype(F32)

    def chunk(row, first, count):
        tiles = [
            wide_ref[pl.ds(whole * tile + 8 * first + row, count, stride=8), :] for tile in range(QUART // 128)
        ]
        return jnp.concatenate(tiles, axis=1)

    def codes(first, count):
        return wide_ref[pl.ds(whole * (QUART // 128) + 8 * first, count, stride=8), :]

    return chunk, codes


def swap_lanes(row, step, flag):
    lane = lax.broadcasted_iota(jnp.int32, row.shape, 1)
    width = row.shape[1]
    other = jnp.where((lane & step) == 0, pltpu.roll(row, width - step, 1), pltpu.roll(row, step, 1))
    return jnp.where(flag == 1, other, row)


def quarter_kernel(place, own_ref, side_ref, flat_ref, q0_ref, q1_ref, q2_ref, q3_ref, wide_ref):
    outs = (q0_ref, q1_ref, q2_ref, q3_ref)
    count = 2 * own_ref.shape[0] // 8
    chunk, codes = unpack((own_ref, side_ref), wide_ref)
    meta = codes(0, count)
    both = jnp.concatenate([meta, meta], axis=0).astype(BF16)
    for k in range(4):
        part = place[0] ^ k
        outs[k][:, 0:QUART] = jnp.concatenate([chunk(part, 0, count), chunk(part + 4, 0, count)], axis=0).astype(BF16)
        outs[k][:, QUART:WIDE] = both


def score_kernel(
    place, own_ref, side_ref, far_ref, corner_ref, turned_ref, power_ref, tables_ref, column_ref,
    q0_ref, q1_ref, q2_ref, q3_ref, stats_ref, wide_ref,
):
    outs = (q0_ref, q1_ref, q2_ref, q3_ref)
    count = 4 * own_ref.shape[0] // 8
    half = count // 2
    refs = power_ref.shape[0]
    chunk, codes = unpack((own_ref, side_ref, far_ref, corner_ref), wide_ref)
    meta = codes(0, count)
    picks = table_picks(meta[:, 0:1], meta[:, 1:2])
    cos_x, sin_x = phases_x(QUART)
    cross = jnp.zeros((3 * refs, 3 * count), F32)
    self_term = jnp.zeros((refs, count), F32)
    for j in range(4):
        at = slice(j * QUART, (j + 1) * QUART)
        ctf_power = ctf_power_rows(picks, tables_ref[:, at])
        self_term += lax.dot_general(power_ref[:, at], ctf_power, NT, preferred_element_type=F32)
    for j in range(4):
        at = slice(j * QUART, (j + 1) * QUART)
        for c, parts in enumerate(shift_x(chunk(j, 0, count), chunk(j + 4, 0, count), cos_x, sin_x)):
            new = jnp.concatenate(parts, axis=0).astype(BF16)
            cross += lax.dot_general(turned_ref[c, :, at], new, NT, preferred_element_type=F32)
        part = place[0] ^ j
        late = jnp.concatenate([chunk(part, half, half), chunk(part + 4, half, half)], axis=0).astype(BF16)
        for side in range(2):
            outs[j][side * count : (side + 1) * count, 5 * refs : 5 * refs + QUART // 2] = late[
                :, side * QUART // 2 : (side + 1) * QUART // 2
            ]

    base = column_ref[:, 0:count] - 0.5 * self_term
    base_pair = jnp.concatenate([base, base], axis=1)
    turned_codes = meta.T
    centre_x, centre_y = turned_codes[2:3, :], turned_codes[3:4, :]

    def offset_term(a, b):
        off_x = centre_x + (2.0 * a - 2.0)
        off_y = centre_y + (2.0 * b - 2.0)
        return (off_x * off_x + off_y * off_y) / (2.0 * TRANS_VAR)

    pairs, singles = [], []
    for b in range(3):
        value = cross[b * refs : (b + 1) * refs]
        pairs.append(
            value[:, 0 : 2 * count] + base_pair - jnp.concatenate([offset_term(0, b), offset_term(1, b)], axis=1)
        )
        singles.append(value[:, 2 * count :] + base - offset_term(2, b))
    top_pair = jnp.max(jnp.maximum(jnp.maximum(pairs[0], pairs[1]), pairs[2]), axis=0, keepdims=True)
    top = jnp.max(jnp.maximum(jnp.maximum(singles[0], singles[1]), singles[2]), axis=0, keepdims=True)
    top = jnp.maximum(top, jnp.maximum(top_pair[:, 0:count], top_pair[:, count:]))
    top_pair = jnp.concatenate([top, top], axis=1)
    pairs = [jnp.exp(value - top_pair) for value in pairs]
    singles = [jnp.exp(value - top) for value in singles]
    mass_pair = jnp.sum(pairs[0] + pairs[1] + pairs[2], axis=0, keepdims=True)
    mass = jnp.sum(singles[0] + singles[1] + singles[2], axis=0, keepdims=True)
    mass = mass + mass_pair[:, 0:count] + mass_pair[:, count:]
    total = top + jnp.log(mass)
    row = jnp.concatenate([total, top], axis=1)
    row = swap_lanes(swap_lanes(row, half, place[2]), half // 2, place[3])
    stats_ref[...] = jnp.broadcast_to(row, stats_ref.shape)
    last = jnp.concatenate(singles[0:2], axis=1)
    notes = jnp.concatenate([meta[half:, 0:count], jnp.zeros((refs - half, count), F32)], axis=0)
    ends = jnp.concatenate([singles[2], notes], axis=1), jnp.concatenate([notes, singles[2]], axis=1)
    for k in range(4):
        for b in range(3):
            outs[k][:, b * refs : (b + 1) * refs] = pairs[b].astype(BF16)
        outs[k][:, 3 * refs : 4 * refs] = last.astype(BF16)
        outs[k][:, 4 * refs : 5 * refs] = ends[k % 2].astype(BF16)


def final_kernel(
    place, e0_ref, e1_ref, e2_ref, e3_ref, q0_ref, q1_ref, q2_ref, q3_ref, stats_ref, tables_ref,
    data_hbm, weight_hbm, evidence_ref, post_ref, sum_ref, power_ref, data_ref, weight_ref, sems, *, scale,
):
    dom, orient, y_hi, z_lo, mine = place[0], place[1], place[2], place[3], place[4]
    early = (e0_ref, e1_ref, e2_ref, e3_ref)
    boxes = (q0_ref, q1_ref, q2_ref, q3_ref)
    doms = 4
    count = q0_ref.shape[0] // 2
    half = count // 2
    refs = sum_ref.shape[0]
    pair = 2 * count
    orients = stats_ref.shape[0] // doms
    lane = lax.broadcasted_iota(jnp.int32, (1, pair), 1)
    left = lane < count
    upper = (lax.broadcasted_iota(jnp.int32, (orients, pair), 0) & 8) != 0
    factors, groups, foci = [], [], []
    for k in range(doms):
        start = dom ^ k ^ (2 * y_hi)
        table = jnp.where(
            upper,
            stats_ref[pl.ds(start ^ 2, orients, stride=doms), :],
            stats_ref[pl.ds(start, orients, stride=doms), :],
        )
        top = jnp.max(table, axis=0, keepdims=True)
        evidence = top + jnp.log(jnp.sum(jnp.exp(table - top), axis=0, keepdims=True))
        own = stats_ref[pl.ds(orient * doms + (dom ^ k), 1), :]
        factor = jnp.exp(pltpu.roll(own, count, 1) - evidence)
        factor = swap_lanes(swap_lanes(factor, half, y_hi), half // 2, z_lo)
        factors.append(jnp.where(left, factor, pltpu.roll(factor, count, 1)))
        if k == 0:
            evidence_ref[0] = jnp.sum(jnp.where(lane == mine, evidence, 0.0))
        notes = boxes[k][0:half, 4 * refs : 5 * refs].astype(F32)
        first = early[k][0:half, QUART:WIDE].astype(F32)
        spot = count if k % 2 == 0 else 0
        groups += [first[:, 0:1], notes[:, spot : spot + 1]]
        foci += [first[:, 1:2], notes[:, spot + 1 : spot + 2]]

    picks = table_picks(jnp.concatenate(groups, axis=0), jnp.concatenate(foci, axis=0))
    for n in range(4):
        at = slice(n * QUART // 4, (n + 1) * QUART // 4)
        start = pl.multiple_of(dom * QUART + n * QUART // 4, QUART // 4)
        power_ref[:, at] = ctf_power_rows(picks, tables_ref[:, pl.ds(start, QUART // 4)])

    def fill(pieces, spot):
        total = jnp.zeros((refs, pair), F32)
        for b in range(3):
            post = pieces[b].astype(BF16)
            post_ref[b * refs : (b + 1) * refs, spot : spot + pair] = post
            total = total + post.astype(F32)
        return total

    def block(k, number):
        return boxes[k][:, number * refs : (number + 1) * refs].astype(F32) * factors[k]

    totals = []
    for k in range(doms):
        total = fill([block(k, b) for b in range(3)], k * pair)
        totals.append(total + pltpu.roll(total, count, 1))
    for k in range(0, doms, 2):
        even, odd = block(k, 3), block(k + 1, 3)
        pieces = [
            jnp.where(left, even, pltpu.roll(odd, count, 1)),
            jnp.where(left, pltpu.roll(even, count, 1), odd),
            jnp.where(left, block(k, 4), block(k + 1, 4)),
        ]
        total = fill(pieces, (doms + k // 2) * pair) + jnp.where(left, totals[k], totals[k + 1])
        sum_ref[:, k * count : (k + 2) * count] = total.astype(BF16)

    weight_ref[...] = lax.dot_general(sum_ref[...], power_ref[...], NN, preferred_element_type=F32) * scale
    copies = [pltpu.make_async_copy(weight_ref, weight_hbm, sems.at[2])]
    copies[0].start()
    width = 512
    cos_x, sin_x = phases_x(width)
    cos_rows, sin_rows = phases_y(dom * QUART, QUART // 128)
    cos_rows, sin_rows = cos_rows * scale, sin_rows * scale
    for n in range(QUART // width):
        at = slice(n * width, (n + 1) * width)
        reals, imags = [], []
        side = 2 * n * width // QUART
        late_at = slice(5 * refs + n * width - side * QUART // 2, 5 * refs + (n + 1) * width - side * QUART // 2)
        for k in range(doms):
            late = boxes[k][side * count : (side + 1) * count, late_at].astype(F32)
            soon = early[k][:, at].astype(F32)
            real = jnp.concatenate([soon[0:half], late[0:half]], axis=0)
            imag = jnp.concatenate([soon[half:], late[half:]], axis=0)
            new_real, new_imag = shift_x(real, imag, cos_x, sin_x)
            reals.append([part.astype(BF16) for part in new_real])
            imags.append([part.astype(BF16) for part in new_imag])

        def stack(parts):
            first = [parts[k][a] for k in range(doms) for a in range(2)]
            return jnp.concatenate(first + [parts[k][2] for k in range(doms)], axis=0)

        sums_real = lax.dot_general(post_ref[...], stack(reals), NN, preferred_element_type=F32)
        sums_imag = lax.dot_general(post_ref[...], stack(imags), NN, preferred_element_type=F32)
        r0, r1, r2 = (sums_real[b * refs : (b + 1) * refs] for b in range(3))
        i0, i1, i2 = (sums_imag[b * refs : (b + 1) * refs] for b in range(3))
        lines = [n * (width // 128) + tile for tile in range(width // 128)]
        cos_y = jnp.concatenate([cos_rows[line : line + 1] for line in lines], axis=1)
        sin_y = jnp.concatenate([sin_rows[line : line + 1] for line in lines], axis=1)
        both = (
            r1 * scale + (r0 + r2) * cos_y + (i2 - i0) * sin_y,
            i1 * scale + (i0 + i2) * cos_y + (r0 - r2) * sin_y,
        )
        lines = 2 * width // 128
        for tile in range(width // 128):
            for c in range(2):
                data_ref[n, pl.ds(2 * tile + c, refs, stride=lines), :] = both[c][:, 128 * tile : 128 * (tile + 1)]
        copy = pltpu.make_async_copy(
            data_ref.at[n].reshape(refs, lines, 128), data_hbm.at[:, n * lines : (n + 1) * lines], sems.at[n]
        )
        copy.start()
        copies.append(copy)
    for copy in copies:
        copy.wait()


def on_device(images, offsets, groups, defocus, refs, log_prior, noise_inv, ctf_table):
    count_refs = refs.shape[0]
    size = {name: lax.axis_size(name) for name in AXES}
    orients = size["x"] * size["yh"] * size["zh"] * size["zl"]
    devices = orients * size["yl"] * size["c"]
    scale = 25.0 * (count_refs * orients) / devices
    at = {name: lax.axis_index(name) for name in AXES}
    dom = at["yl"] * size["c"] + at["c"]
    orient = ((at["x"] * size["yh"] + at["yh"]) * size["zh"] + at["zh"]) * size["zl"] + at["zl"]
    mine = ((at["yh"] * size["zl"] + at["zl"]) * size["x"] + at["x"]) * size["zh"] + at["zh"]
    place = jnp.stack([dom, orient, at["yh"], at["zl"], mine]).astype(jnp.int32)

    smem = pl.BlockSpec(memory_space=pltpu.SMEM)
    vmem = pl.BlockSpec(memory_space=pltpu.VMEM)
    hbm = pl.BlockSpec(memory_space=pltpu.HBM)
    shape = jax.ShapeDtypeStruct
    line = 8 * size["x"] * size["zh"]
    payload = pl.pallas_call(
        prep_kernel,
        in_specs=[smem] * 3 + [hbm] * 3,
        out_specs=vmem,
        out_shape=shape((line, WIDE), BF16),
        scratch_shapes=[
            pltpu.VMEM((1, 2, PIX), BF16),
            pltpu.VMEM((GROUPS, PIX), F32),
            pltpu.VMEM((8, PIX), F32),
            pltpu.SemaphoreType.DMA((3,)),
        ],
        compiler_params=params(VMEM_ALL),
        name="prep",
    )(jnp.transpose(offsets, (0, 2, 1))[0], groups, defocus, images, noise_inv, ctf_table)
    flip = [(i, 3 - i) for i in range(4)]
    own = lax.all_to_all(payload, ("x", "zh"), 0, 0, tiled=True)
    side = lax.ppermute(own, "zl", [(0, 1), (1, 0)])
    far = lax.ppermute(own, ("yh", "yl"), flip)

    flat = refs.reshape(count_refs, 2 * PIX)
    flat, ctf_late, noise_late = lax.optimization_barrier((flat, ctf_table, noise_inv))
    tables = pl.pallas_call(
        tables_kernel,
        in_specs=[vmem] * 2,
        out_specs=vmem,
        out_shape=shape((TABLE_ROWS, PIX), BF16),
        compiler_params=params(VMEM_LIMIT // 3),
        name="tables",
    )(ctf_late, noise_late)
    side, _, flat, tables = lax.optimization_barrier((side, far, flat, tables))
    corner = lax.ppermute(side, ("yh", "yl"), flip)

    early = pl.pallas_call(
        quarter_kernel,
        in_specs=[smem] + [vmem] * 3,
        out_specs=[vmem] * 4,
        out_shape=[shape((orients, WIDE), BF16)] * 4,
        scratch_shapes=[pltpu.VMEM((4 * orients * (WIDE // 128), 128), F32)],
        compiler_params=params(VMEM_LIMIT // 3),
        name="quarters",
    )(place, own, side, flat)

    def share(parts):
        moves = [[(d, d ^ k) for d in range(4)] for k in range(4)]
        return parts[0:1] + [lax.ppermute(parts[k], ("yl", "c"), moves[k]) for k in range(1, 4)]

    early = list(early)
    flat, early[0] = lax.optimization_barrier((flat, early[0]))
    turned, power, column = pl.pallas_call(
        refs_kernel,
        in_specs=[vmem] * 2,
        out_specs=[vmem] * 3,
        out_shape=[
            shape((2, 3 * count_refs, PIX), BF16),
            shape((count_refs, PIX), BF16),
            shape((count_refs, 128), F32),
        ],
        scratch_shapes=[pltpu.VMEM((PIX // 128, 128), F32)] * 2,
        compiler_params=params(),
        cost_estimate=pl.CostEstimate(flops=8 * count_refs * PIX, bytes_accessed=10 << 20, transcendentals=0),
        name="turn_refs",
    )(flat, log_prior[None, :])
    early = share(early)

    box = (2 * orients, 5 * count_refs + QUART // 2)
    *boxes, stats = pl.pallas_call(
        score_kernel,
        in_specs=[smem] + [vmem] * 8,
        out_specs=[vmem] * 5,
        out_shape=[shape(box, BF16)] * 4 + [shape((devices, 2 * orients), F32)],
        scratch_shapes=[pltpu.VMEM((8 * orients * (WIDE // 128), 128), F32)],
        compiler_params=params(),
        cost_estimate=pl.CostEstimate(
            flops=18 * orients * count_refs * 2 * PIX, bytes_accessed=10 << 20, transcendentals=0
        ),
        name="score",
    )(place, own, side, far, corner, turned, power, tables, column)

    boxes = list(boxes)
    early, stats = lax.optimization_barrier((early, stats))
    boxes = share(boxes)
    stats_all = lax.all_to_all(stats, AXES, 0, 0, tiled=True)

    data, weight, evidence = pl.pallas_call(
        functools.partial(final_kernel, scale=scale),
        in_specs=[smem] + [vmem] * 10,
        out_specs=[hbm, hbm, smem],
        scratch_shapes=[
            pltpu.VMEM((3 * count_refs, 12 * orients), BF16),
            pltpu.VMEM((count_refs, 4 * orients), BF16),
            pltpu.VMEM((4 * orients, QUART), BF16),
            pltpu.VMEM((2, count_refs * (QUART // 128), 128), F32),
            pltpu.VMEM((count_refs, QUART), F32),
            pltpu.SemaphoreType.DMA((3,)),
        ],
        out_shape=[
            shape((count_refs, 2 * (QUART // 128), 128), F32),
            shape((count_refs, QUART), F32),
            shape((1,), F32),
        ],
        compiler_params=params(),
        name="insert",
    )(place, *early, *boxes, stats_all, tables)
    data = jnp.transpose(data.reshape(count_refs, QUART // 128, 2, 128), (0, 2, 1, 3))
    return data.reshape(count_refs, 2, QUART), weight, evidence


def solution(mesh):
    fine = Mesh(mesh.devices.reshape(4, 2, 4, 2, 2, 2), AXES)
    orient = AXES[0:4]
    dom = AXES[4:6]
    return jax.shard_map(
        on_device,
        mesh=fine,
        in_specs=(
            P(AXES, None, None),
            P(AXES, None, None),
            P(AXES),
            P(AXES),
            P(orient, None, None),
            P(orient),
            P(),
            P(),
        ),
        out_specs=(P(orient, None, dom), P(orient, dom), P(AXES)),
        check_vma=False,
    )
```

```python
import functools
import math

import jax
import jax.numpy as jnp
from jax import lax
from jax.experimental import pallas as pl
from jax.experimental.pallas import tpu as pltpu
from jax.sharding import Mesh
from jax.sharding import PartitionSpec as P

SIDE = 64
PIX = SIDE * SIDE
QUART = PIX // 4
META = 128
WIDE = QUART + META
DEFS = 64
GROUPS = 8
TWO_PI = 2.0 * math.pi
TRANS_VAR = 8.0
F32 = jnp.float32
BF16 = jnp.bfloat16
NT = (((1,), (1,)), ((), ()))
NN = (((1,), (0,)), ((), ()))
AXES = ("x", "yh", "zh", "zl", "yl", "c")
TABLE_ROWS = 3 * DEFS + 4 * GROUPS
VMEM_LIMIT = 24 * 1024 * 1024
VMEM_ALL = 61 * 1024 * 1024


def phases(step):
    freq = (step + SIDE // 2 & SIDE - 1) - SIDE // 2
    angle = (2 * freq & SIDE - 1).astype(F32) * (TWO_PI / SIDE)
    return jnp.cos(angle), jnp.sin(angle)


def phases_x(width):
    cosine, sine = phases(lax.broadcasted_iota(jnp.int32, (8, 128), 1) & SIDE - 1)
    many = width // 128
    return jnp.concatenate([cosine[0:1]] * many, axis=1), jnp.concatenate([sine[0:1]] * many, axis=1)


def phases_y(first, rows):
    line = lax.broadcasted_iota(jnp.int32, (rows, 128), 0)
    lane = lax.broadcasted_iota(jnp.int32, (rows, 128), 1)
    return phases((first + 128 * line + lane) // SIDE)


def params(limit=VMEM_LIMIT):
    return pltpu.CompilerParams(vmem_limit_bytes=limit)


def prep_kernel(
    offsets, groups, defocus, image_hbm, noise_hbm, ctf_hbm, out_ref, image_ref, noise_ref, ctf_ref, sems
):
    group, focus, centre_x, centre_y = groups[0], defocus[0], offsets[0, 4], offsets[1, 4]
    start = pl.multiple_of(focus // 8 * 8, 8)
    copies = [
        pltpu.make_async_copy(ctf_hbm.at[pl.ds(start, 8)], ctf_ref, sems.at[0]),
        pltpu.make_async_copy(noise_hbm, noise_ref, sems.at[1]),
        pltpu.make_async_copy(image_hbm, image_ref, sems.at[2]),
    ]
    for copy in copies:
        copy.start()
    lane = lax.broadcasted_iota(jnp.int32, (4, QUART), 1)
    row = lax.broadcasted_iota(jnp.int32, (4, QUART), 0)
    freq_x = ((lane & 63) + 32 & 63) - 32
    freq_y = ((row * (QUART // SIDE) + (lane >> 6)) + 32 & 63) - 32
    angle = ((freq_x * centre_x + freq_y * centre_y) & 63).astype(F32) * (TWO_PI / SIDE)
    cosine = jnp.cos(angle)
    sine = jnp.sin(angle)
    spot = lax.broadcasted_iota(jnp.int32, (8, META), 1)
    meta = jnp.where(
        spot == 0,
        group,
        jnp.where(spot == 1, focus, jnp.where(spot == 2, centre_x, jnp.where(spot == 3, centre_y, 0))),
    ).astype(F32)
    for copy in copies:
        copy.wait()
    rows = lax.broadcasted_iota(jnp.int32, (8, PIX), 0)
    noise = jnp.sum(jnp.where(rows == group, noise_ref[...], 0.0), axis=0, keepdims=True)
    ctf = jnp.sum(jnp.where(rows == focus % 8, ctf_ref[...], 0.0), axis=0, keepdims=True)
    weighted = (image_ref[0].astype(F32) * (noise * ctf)).astype(BF16).astype(F32)
    real = jnp.concatenate([weighted[0:1, j * QUART : (j + 1) * QUART] for j in range(4)], axis=0)
    imag = jnp.concatenate([weighted[1:2, j * QUART : (j + 1) * QUART] for j in range(4)], axis=0)
    body = jnp.concatenate([real * cosine + imag * sine, imag * cosine - real * sine], axis=0)
    one = jnp.concatenate([body, meta], axis=1)
    pair = jnp.concatenate([one, one], axis=0).astype(BF16)
    for k in range(out_ref.shape[0] // 16):
        out_ref[16 * k : 16 * (k + 1), :] = pair


def tables_kernel(ctf_ref, noise_ref, tables_ref):
    def split(table):
        first = table.astype(BF16).astype(F32)
        second = (table - first).astype(BF16).astype(F32)
        return [first, second, table - first - second]

    noise = split(noise_ref[...])
    rows = split(ctf_ref[...]) + noise + [jnp.zeros_like(noise[0])]
    tables_ref[...] = jnp.concatenate(rows, axis=0).astype(BF16)


def refs_kernel(flat_ref, prior_ref, turned_ref, power_ref, column_ref, cos_ref, sin_ref):
    count = flat_ref.shape[0]
    width = 256
    cos_ref[...], sin_ref[...] = phases_y(0, PIX // 128)

    def body(step, carry):
        at = pl.ds(pl.multiple_of(step * width, width), width)
        low = flat_ref[:, at]
        high = flat_ref[:, pl.ds(pl.multiple_of(PIX + step * width, width), width)]
        real = low.astype(F32)
        imag = high.astype(F32)
        lines = [pl.ds(step * (width // 128) + k, 1) for k in range(width // 128)]
        cosine = jnp.concatenate([cos_ref[line, :] for line in lines], axis=1)
        sine = jnp.concatenate([sin_ref[line, :] for line in lines], axis=1)
        rc, rs, ic, si = real * cosine, real * sine, imag * cosine, imag * sine
        turned_ref[0, 0:count, at] = (rc + si).astype(BF16)
        turned_ref[1, 0:count, at] = (ic - rs).astype(BF16)
        turned_ref[0, count : 2 * count, at] = low
        turned_ref[1, count : 2 * count, at] = high
        turned_ref[0, 2 * count : 3 * count, at] = (rc - si).astype(BF16)
        turned_ref[1, 2 * count : 3 * count, at] = (ic + rs).astype(BF16)
        power_ref[:, at] = (real * real + imag * imag).astype(BF16)
        return carry

    lax.fori_loop(0, PIX // width, body, 0)
    line = lax.broadcasted_iota(jnp.int32, (count, count), 0)
    lane = lax.broadcasted_iota(jnp.int32, (count, count), 1)
    column = jnp.sum(jnp.where(lane == line, prior_ref[...], 0.0), axis=1, keepdims=True)
    column_ref[...] = jnp.broadcast_to(column, column_ref.shape)


def table_picks(group, focus):
    spot = lax.broadcasted_iota(jnp.int32, (group.shape[0], TABLE_ROWS), 1)
    ctf = (spot < 3 * DEFS) & (spot % DEFS == focus.astype(jnp.int32))
    noise = (spot >= 3 * DEFS) & (spot < 3 * (DEFS + GROUPS)) & (spot % GROUPS == group.astype(jnp.int32))
    return jnp.concatenate([ctf.astype(F32), noise.astype(F32)], axis=0).astype(BF16)


def ctf_power_rows(picks, tables):
    rows = lax.dot_general(picks, tables, NN, preferred_element_type=F32)
    count = rows.shape[0] // 2
    ctf, noise = rows[0:count], rows[count:]
    return (noise * ctf * ctf).astype(BF16)


def shift_x(real, imag, cosine, sine):
    rc, rs, ic, si = real * cosine, real * sine, imag * cosine, imag * sine
    return (rc - si, real, rc + si), (ic + rs, imag, ic - rs)


def unpack(parts, wide_ref):
    size = parts[0].shape[0]
    whole = size * len(parts)
    for spot, part in enumerate(parts):
        for tile in range(WIDE // 128):
            start = whole * tile + size * spot
            wide_ref[start : start + size, :] = part[:, 128 * tile : 128 * (tile + 1)].astype(F32)

    def chunk(row, first, count):
        tiles = [
            wide_ref[pl.ds(whole * tile + 8 * first + row, count, stride=8), :] for tile in range(QUART // 128)
        ]
        return jnp.concatenate(tiles, axis=1)

    def codes(first, count):
        return wide_ref[pl.ds(whole * (QUART // 128) + 8 * first, count, stride=8), :]

    return chunk, codes


def swap_lanes(row, step, flag):
    lane = lax.broadcasted_iota(jnp.int32, row.shape, 1)
    width = row.shape[1]
    other = jnp.where((lane & step) == 0, pltpu.roll(row, width - step, 1), pltpu.roll(row, step, 1))
    return jnp.where(flag == 1, other, row)


def quarter_kernel(place, own_ref, side_ref, flat_ref, q0_ref, q2_ref, q3_ref, wide_ref):
    outs = {0: q0_ref, 2: q2_ref, 3: q3_ref}
    count = 2 * own_ref.shape[0] // 8
    chunk, codes = unpack((own_ref, side_ref), wide_ref)
    meta = codes(0, count)
    both = jnp.concatenate([meta, meta], axis=0).astype(BF16)
    for k in outs:
        part = place[0] ^ k
        outs[k][:, 0:QUART] = jnp.concatenate([chunk(part, 0, count), chunk(part + 4, 0, count)], axis=0).astype(BF16)
        outs[k][:, QUART:WIDE] = both


def score_kernel(
    place, own_ref, side_ref, far_ref, corner_ref, turned_ref, power_ref, tables_ref, column_ref,
    q0_ref, q1_ref, q2_ref, q3_ref, stats_ref, wide_ref,
):
    outs = (q0_ref, q1_ref, q2_ref, q3_ref)
    count = 4 * own_ref.shape[0] // 8
    half = count // 2
    refs = power_ref.shape[0]
    chunk, codes = unpack((own_ref, side_ref, far_ref, corner_ref), wide_ref)
    meta = codes(0, count)
    picks = table_picks(meta[:, 0:1], meta[:, 1:2])
    cos_x, sin_x = phases_x(QUART)
    cross = jnp.zeros((3 * refs, 3 * count), F32)
    self_term = jnp.zeros((refs, count), F32)
    for j in range(4):
        at = slice(j * QUART, (j + 1) * QUART)
        ctf_power = ctf_power_rows(picks, tables_ref[:, at])
        self_term += lax.dot_general(power_ref[:, at], ctf_power, NT, preferred_element_type=F32)
    for j in range(4):
        at = slice(j * QUART, (j + 1) * QUART)
        for c, parts in enumerate(shift_x(chunk(j, 0, count), chunk(j + 4, 0, count), cos_x, sin_x)):
            new = jnp.concatenate(parts, axis=0).astype(BF16)
            cross += lax.dot_general(turned_ref[c, :, at], new, NT, preferred_element_type=F32)
        part = place[0] ^ j
        late = jnp.concatenate([chunk(part, half, half), chunk(part + 4, half, half)], axis=0).astype(BF16)
        for side in range(2):
            outs[j][side * count : (side + 1) * count, 5 * refs : 5 * refs + QUART // 2] = late[
                :, side * QUART // 2 : (side + 1) * QUART // 2
            ]
    part = place[0] ^ 1
    soon = jnp.concatenate([chunk(part, 0, half), chunk(part + 4, 0, half)], axis=0).astype(BF16)
    base = 5 * refs + QUART // 2
    for side in range(2):
        rows = slice(side * count, (side + 1) * count)
        q1_ref[rows, base : base + QUART // 2] = soon[:, side * QUART // 2 : (side + 1) * QUART // 2]
        q1_ref[rows, base + QUART // 2 : base + QUART // 2 + META] = meta.astype(BF16)

    base = column_ref[:, 0:count] - 0.5 * self_term
    base_pair = jnp.concatenate([base, base], axis=1)
    turned_codes = meta.T
    centre_x, centre_y = turned_codes[2:3, :], turned_codes[3:4, :]

    def offset_term(a, b):
        off_x = centre_x + (2.0 * a - 2.0)
        off_y = centre_y + (2.0 * b - 2.0)
        return (off_x * off_x + off_y * off_y) / (2.0 * TRANS_VAR)

    pairs, singles = [], []
    for b in range(3):
        value = cross[b * refs : (b + 1) * refs]
        pairs.append(
            value[:, 0 : 2 * count] + base_pair - jnp.concatenate([offset_term(0, b), offset_term(1, b)], axis=1)
        )
        singles.append(value[:, 2 * count :] + base - offset_term(2, b))
    top_pair = jnp.max(jnp.maximum(jnp.maximum(pairs[0], pairs[1]), pairs[2]), axis=0, keepdims=True)
    top = jnp.max(jnp.maximum(jnp.maximum(singles[0], singles[1]), singles[2]), axis=0, keepdims=True)
    top = jnp.maximum(top, jnp.maximum(top_pair[:, 0:count], top_pair[:, count:]))
    top_pair = jnp.concatenate([top, top], axis=1)
    pairs = [jnp.exp(value - top_pair) for value in pairs]
    singles = [jnp.exp(value - top) for value in singles]
    mass_pair = jnp.sum(pairs[0] + pairs[1] + pairs[2], axis=0, keepdims=True)
    mass = jnp.sum(singles[0] + singles[1] + singles[2], axis=0, keepdims=True)
    mass = mass + mass_pair[:, 0:count] + mass_pair[:, count:]
    total = top + jnp.log(mass)
    row = jnp.concatenate([total, top], axis=1)
    row = swap_lanes(swap_lanes(row, half, place[2]), half // 2, place[3])
    stats_ref[...] = jnp.broadcast_to(row, stats_ref.shape)
    last = jnp.concatenate(singles[0:2], axis=1)
    notes = jnp.concatenate([meta[half:, 0:count], jnp.zeros((refs - half, count), F32)], axis=0)
    ends = jnp.concatenate([singles[2], notes], axis=1), jnp.concatenate([notes, singles[2]], axis=1)
    for k in range(4):
        for b in range(3):
            outs[k][:, b * refs : (b + 1) * refs] = pairs[b].astype(BF16)
        outs[k][:, 3 * refs : 4 * refs] = last.astype(BF16)
        outs[k][:, 4 * refs : 5 * refs] = ends[k % 2].astype(BF16)


def final_kernel(
    place, e0_ref, e2_ref, e3_ref, q0_ref, q1_ref, q2_ref, q3_ref, stats_ref, tables_ref,
    data_hbm, weight_hbm, evidence_ref, post_ref, sum_ref, power_ref, data_ref, weight_ref, sems, *, scale,
):
    dom, orient, y_hi, z_lo, mine = place[0], place[1], place[2], place[3], place[4]
    early = {0: e0_ref, 2: e2_ref, 3: e3_ref}
    boxes = (q0_ref, q1_ref, q2_ref, q3_ref)
    doms = 4
    count = q0_ref.shape[0] // 2
    half = count // 2
    refs = sum_ref.shape[0]
    tail = 5 * refs + QUART // 2
    pair = 2 * count
    orients = stats_ref.shape[0] // doms
    lane = lax.broadcasted_iota(jnp.int32, (1, pair), 1)
    left = lane < count
    upper = (lax.broadcasted_iota(jnp.int32, (orients, pair), 0) & 8) != 0
    factors, groups, foci = [], [], []
    for k in range(doms):
        start = dom ^ k ^ (2 * y_hi)
        table = jnp.where(
            upper,
            stats_ref[pl.ds(start ^ 2, orients, stride=doms), :],
            stats_ref[pl.ds(start, orients, stride=doms), :],
        )
        top = jnp.max(table, axis=0, keepdims=True)
        evidence = top + jnp.log(jnp.sum(jnp.exp(table - top), axis=0, keepdims=True))
        own = stats_ref[pl.ds(orient * doms + (dom ^ k), 1), :]
        factor = jnp.exp(pltpu.roll(own, count, 1) - evidence)
        factor = swap_lanes(swap_lanes(factor, half, y_hi), half // 2, z_lo)
        factors.append(jnp.where(left, factor, pltpu.roll(factor, count, 1)))
        if k == 0:
            evidence_ref[0] = jnp.sum(jnp.where(lane == mine, evidence, 0.0))
        notes = boxes[k][0:half, 4 * refs : 5 * refs].astype(F32)
        if k in early:
            first = early[k][0:half, QUART:WIDE].astype(F32)
        else:
            first = boxes[k][0:half, tail + QUART // 2 : tail + QUART // 2 + META].astype(F32)
        spot = count if k % 2 == 0 else 0
        groups += [first[:, 0:1], notes[:, spot : spot + 1]]
        foci += [first[:, 1:2], notes[:, spot + 1 : spot + 2]]

    picks = table_picks(jnp.concatenate(groups, axis=0), jnp.concatenate(foci, axis=0))
    for n in range(4):
        at = slice(n * QUART // 4, (n + 1) * QUART // 4)
        start = pl.multiple_of(dom * QUART + n * QUART // 4, QUART // 4)
        power_ref[:, at] = ctf_power_rows(picks, tables_ref[:, pl.ds(start, QUART // 4)])

    def fill(pieces, spot):
        total = jnp.zeros((refs, pair), F32)
        for b in range(3):
            post = pieces[b].astype(BF16)
            post_ref[b * refs : (b + 1) * refs, spot : spot + pair] = post
            total = total + post.astype(F32)
        return total

    def block(k, number):
        return boxes[k][:, number * refs : (number + 1) * refs].astype(F32) * factors[k]

    totals = []
    for k in range(doms):
        total = fill([block(k, b) for b in range(3)], k * pair)
        totals.append(total + pltpu.roll(total, count, 1))
    for k in range(0, doms, 2):
        even, odd = block(k, 3), block(k + 1, 3)
        pieces = [
            jnp.where(left, even, pltpu.roll(odd, count, 1)),
            jnp.where(left, pltpu.roll(even, count, 1), odd),
            jnp.where(left, block(k, 4), block(k + 1, 4)),
        ]
        total = fill(pieces, (doms + k // 2) * pair) + jnp.where(left, totals[k], totals[k + 1])
        sum_ref[:, k * count : (k + 2) * count] = total.astype(BF16)

    weight_ref[...] = lax.dot_general(sum_ref[...], power_ref[...], NN, preferred_element_type=F32) * scale
    copies = [pltpu.make_async_copy(weight_ref, weight_hbm, sems.at[2])]
    copies[0].start()
    width = 512
    cos_x, sin_x = phases_x(width)
    cos_rows, sin_rows = phases_y(dom * QUART, QUART // 128)
    cos_rows, sin_rows = cos_rows * scale, sin_rows * scale
    for n in range(QUART // width):
        at = slice(n * width, (n + 1) * width)
        reals, imags = [], []
        side = 2 * n * width // QUART
        late_at = slice(5 * refs + n * width - side * QUART // 2, 5 * refs + (n + 1) * width - side * QUART // 2)
        for k in range(doms):
            late = boxes[k][side * count : (side + 1) * count, late_at].astype(F32)
            if k in early:
                soon = early[k][:, at].astype(F32)
            else:
                start = tail + n * width - side * QUART // 2
                soon = boxes[k][side * count : (side + 1) * count, start : start + width].astype(F32)
            real = jnp.concatenate([soon[0:half], late[0:half]], axis=0)
            imag = jnp.concatenate([soon[half:], late[half:]], axis=0)
            new_real, new_imag = shift_x(real, imag, cos_x, sin_x)
            reals.append([part.astype(BF16) for part in new_real])
            imags.append([part.astype(BF16) for part in new_imag])

        def stack(parts):
            first = [parts[k][a] for k in range(doms) for a in range(2)]
            return jnp.concatenate(first + [parts[k][2] for k in range(doms)], axis=0)

        sums_real = lax.dot_general(post_ref[...], stack(reals), NN, preferred_element_type=F32)
        sums_imag = lax.dot_general(post_ref[...], stack(imags), NN, preferred_element_type=F32)
        r0, r1, r2 = (sums_real[b * refs : (b + 1) * refs] for b in range(3))
        i0, i1, i2 = (sums_imag[b * refs : (b + 1) * refs] for b in range(3))
        lines = [n * (width // 128) + tile for tile in range(width // 128)]
        cos_y = jnp.concatenate([cos_rows[line : line + 1] for line in lines], axis=1)
        sin_y = jnp.concatenate([sin_rows[line : line + 1] for line in lines], axis=1)
        both = (
            r1 * scale + (r0 + r2) * cos_y + (i2 - i0) * sin_y,
            i1 * scale + (i0 + i2) * cos_y + (r0 - r2) * sin_y,
        )
        lines = 2 * width // 128
        for tile in range(width // 128):
            for c in range(2):
                data_ref[n, pl.ds(2 * tile + c, refs, stride=lines), :] = both[c][:, 128 * tile : 128 * (tile + 1)]
        copy = pltpu.make_async_copy(
            data_ref.at[n].reshape(refs, lines, 128), data_hbm.at[:, n * lines : (n + 1) * lines], sems.at[n]
        )
        copy.start()
        copies.append(copy)
    for copy in copies:
        copy.wait()


def on_device(images, offsets, groups, defocus, refs, log_prior, noise_inv, ctf_table):
    count_refs = refs.shape[0]
    size = {name: lax.axis_size(name) for name in AXES}
    orients = size["x"] * size["yh"] * size["zh"] * size["zl"]
    devices = orients * size["yl"] * size["c"]
    scale = 25.0 * (count_refs * orients) / devices
    at = {name: lax.axis_index(name) for name in AXES}
    dom = at["yl"] * size["c"] + at["c"]
    orient = ((at["x"] * size["yh"] + at["yh"]) * size["zh"] + at["zh"]) * size["zl"] + at["zl"]
    mine = ((at["yh"] * size["zl"] + at["zl"]) * size["x"] + at["x"]) * size["zh"] + at["zh"]
    place = jnp.stack([dom, orient, at["yh"], at["zl"], mine]).astype(jnp.int32)

    smem = pl.BlockSpec(memory_space=pltpu.SMEM)
    vmem = pl.BlockSpec(memory_space=pltpu.VMEM)
    hbm = pl.BlockSpec(memory_space=pltpu.HBM)
    shape = jax.ShapeDtypeStruct
    line = 8 * size["x"] * size["zh"]
    payload = pl.pallas_call(
        prep_kernel,
        in_specs=[smem] * 3 + [hbm] * 3,
        out_specs=vmem,
        out_shape=shape((line, WIDE), BF16),
        scratch_shapes=[
            pltpu.VMEM((1, 2, PIX), BF16),
            pltpu.VMEM((GROUPS, PIX), F32),
            pltpu.VMEM((8, PIX), F32),
            pltpu.SemaphoreType.DMA((3,)),
        ],
        compiler_params=params(VMEM_ALL),
        name="prep",
    )(jnp.transpose(offsets, (0, 2, 1))[0], groups, defocus, images, noise_inv, ctf_table)
    flip = [(i, 3 - i) for i in range(4)]
    own = lax.all_to_all(payload, ("x", "zh"), 0, 0, tiled=True)
    side = lax.ppermute(own, "zl", [(0, 1), (1, 0)])
    far = lax.ppermute(own, ("yh", "yl"), flip)

    flat = refs.reshape(count_refs, 2 * PIX)
    flat, ctf_late, noise_late = lax.optimization_barrier((flat, ctf_table, noise_inv))
    tables = pl.pallas_call(
        tables_kernel,
        in_specs=[vmem] * 2,
        out_specs=vmem,
        out_shape=shape((TABLE_ROWS, PIX), BF16),
        compiler_params=params(VMEM_LIMIT // 3),
        name="tables",
    )(ctf_late, noise_late)
    side, _, flat, tables = lax.optimization_barrier((side, far, flat, tables))
    corner = lax.ppermute(side, ("yh", "yl"), flip)

    early = pl.pallas_call(
        quarter_kernel,
        in_specs=[smem] + [vmem] * 3,
        out_specs=[vmem] * 3,
        out_shape=[shape((orients, WIDE), BF16)] * 3,
        scratch_shapes=[pltpu.VMEM((4 * orients * (WIDE // 128), 128), F32)],
        compiler_params=params(VMEM_LIMIT // 3),
        name="quarters",
    )(place, own, side, flat)

    def share(parts):
        moves = [[(d, d ^ k) for d in range(4)] for k in range(4)]
        return {k: lax.ppermute(part, ("yl", "c"), moves[k]) if k else part for k, part in parts.items()}

    early = dict(zip((0, 2, 3), early))
    flat, early[0] = lax.optimization_barrier((flat, early[0]))
    turned, power, column = pl.pallas_call(
        refs_kernel,
        in_specs=[vmem] * 2,
        out_specs=[vmem] * 3,
        out_shape=[
            shape((2, 3 * count_refs, PIX), BF16),
            shape((count_refs, PIX), BF16),
            shape((count_refs, 128), F32),
        ],
        scratch_shapes=[pltpu.VMEM((PIX // 128, 128), F32)] * 2,
        compiler_params=params(),
        cost_estimate=pl.CostEstimate(flops=8 * count_refs * PIX, bytes_accessed=10 << 20, transcendentals=0),
        name="turn_refs",
    )(flat, log_prior[None, :])
    early = share(early)

    box = (2 * orients, 5 * count_refs + QUART // 2)
    *boxes, stats = pl.pallas_call(
        score_kernel,
        in_specs=[smem] + [vmem] * 8,
        out_specs=[vmem] * 5,
        out_shape=[shape((box[0], box[1] + (k == 1) * (QUART // 2 + META)), BF16) for k in range(4)]
        + [shape((devices, 2 * orients), F32)],
        scratch_shapes=[pltpu.VMEM((8 * orients * (WIDE // 128), 128), F32)],
        compiler_params=params(),
        cost_estimate=pl.CostEstimate(
            flops=18 * orients * count_refs * 2 * PIX, bytes_accessed=10 << 20, transcendentals=0
        ),
        name="score",
    )(place, own, side, far, corner, turned, power, tables, column)

    boxes = dict(enumerate(boxes))
    early, boxes, stats = lax.optimization_barrier((early, boxes, stats))
    boxes = share(boxes)
    stats_all = lax.all_to_all(stats, AXES, 0, 0, tiled=True)

    data, weight, evidence = pl.pallas_call(
        functools.partial(final_kernel, scale=scale),
        in_specs=[smem] + [vmem] * 9,
        out_specs=[hbm, hbm, smem],
        scratch_shapes=[
            pltpu.VMEM((3 * count_refs, 12 * orients), BF16),
            pltpu.VMEM((count_refs, 4 * orients), BF16),
            pltpu.VMEM((4 * orients, QUART), BF16),
            pltpu.VMEM((2, count_refs * (QUART // 128), 128), F32),
            pltpu.VMEM((count_refs, QUART), F32),
            pltpu.SemaphoreType.DMA((3,)),
        ],
        out_shape=[
            shape((count_refs, 2 * (QUART // 128), 128), F32),
            shape((count_refs, QUART), F32),
            shape((1,), F32),
        ],
        compiler_params=params(),
        name="insert",
    )(place, *(early[k] for k in (0, 2, 3)), *(boxes[k] for k in range(4)), stats_all, tables)
    data = jnp.transpose(data.reshape(count_refs, QUART // 128, 2, 128), (0, 2, 1, 3))
    return data.reshape(count_refs, 2, QUART), weight, evidence


def solution(mesh):
    fine = Mesh(mesh.devices.reshape(4, 2, 4, 2, 2, 2), AXES)
    orient = AXES[0:4]
    dom = AXES[4:6]
    return jax.shard_map(
        on_device,
        mesh=fine,
        in_specs=(
            P(AXES, None, None),
            P(AXES, None, None),
            P(AXES),
            P(AXES),
            P(orient, None, None),
            P(orient),
            P(),
            P(),
        ),
        out_specs=(P(orient, None, dom), P(orient, dom), P(AXES)),
        check_vma=False,
    )
```

```python
import functools
import math

import jax
import jax.numpy as jnp
from jax import lax
from jax.experimental import pallas as pl
from jax.experimental.pallas import tpu as pltpu
from jax.sharding import Mesh
from jax.sharding import PartitionSpec as P

SIDE = 64
PIX = SIDE * SIDE
QUART = PIX // 4
META = 128
WIDE = QUART + META
DEFS = 64
GROUPS = 8
TWO_PI = 2.0 * math.pi
TRANS_VAR = 8.0
F32 = jnp.float32
BF16 = jnp.bfloat16
NT = (((1,), (1,)), ((), ()))
NN = (((1,), (0,)), ((), ()))
AXES = ("x", "yh", "zh", "zl", "yl", "c")
TABLE_ROWS = 3 * DEFS + 4 * GROUPS
VMEM_LIMIT = 24 * 1024 * 1024
VMEM_ALL = 61 * 1024 * 1024


def phases(step):
    freq = (step + SIDE // 2 & SIDE - 1) - SIDE // 2
    angle = (2 * freq & SIDE - 1).astype(F32) * (TWO_PI / SIDE)
    return jnp.cos(angle), jnp.sin(angle)


def phases_x(width):
    cosine, sine = phases(lax.broadcasted_iota(jnp.int32, (8, 128), 1) & SIDE - 1)
    many = width // 128
    return jnp.concatenate([cosine[0:1]] * many, axis=1), jnp.concatenate([sine[0:1]] * many, axis=1)


def phases_y(first, rows):
    line = lax.broadcasted_iota(jnp.int32, (rows, 128), 0)
    lane = lax.broadcasted_iota(jnp.int32, (rows, 128), 1)
    return phases((first + 128 * line + lane) // SIDE)


def params(limit=VMEM_LIMIT):
    return pltpu.CompilerParams(vmem_limit_bytes=limit)


def prep_kernel(
    offsets, groups, defocus, image_hbm, noise_hbm, ctf_hbm, out_ref, image_ref, noise_ref, ctf_ref, sems
):
    group, focus, centre_x, centre_y = groups[0], defocus[0], offsets[0, 4], offsets[1, 4]
    start = pl.multiple_of(focus // 8 * 8, 8)
    copies = [
        pltpu.make_async_copy(ctf_hbm.at[pl.ds(start, 8)], ctf_ref, sems.at[0]),
        pltpu.make_async_copy(noise_hbm, noise_ref, sems.at[1]),
        pltpu.make_async_copy(image_hbm, image_ref, sems.at[2]),
    ]
    for copy in copies:
        copy.start()
    lane = lax.broadcasted_iota(jnp.int32, (4, QUART), 1)
    row = lax.broadcasted_iota(jnp.int32, (4, QUART), 0)
    freq_x = ((lane & 63) + 32 & 63) - 32
    freq_y = ((row * (QUART // SIDE) + (lane >> 6)) + 32 & 63) - 32
    angle = ((freq_x * centre_x + freq_y * centre_y) & 63).astype(F32) * (TWO_PI / SIDE)
    cosine = jnp.cos(angle)
    sine = jnp.sin(angle)
    spot = lax.broadcasted_iota(jnp.int32, (8, META), 1)
    meta = jnp.where(
        spot == 0,
        group,
        jnp.where(spot == 1, focus, jnp.where(spot == 2, centre_x, jnp.where(spot == 3, centre_y, 0))),
    ).astype(F32)
    for copy in copies:
        copy.wait()
    rows = lax.broadcasted_iota(jnp.int32, (8, PIX), 0)
    noise = jnp.sum(jnp.where(rows == group, noise_ref[...], 0.0), axis=0, keepdims=True)
    ctf = jnp.sum(jnp.where(rows == focus % 8, ctf_ref[...], 0.0), axis=0, keepdims=True)
    weighted = (image_ref[0].astype(F32) * (noise * ctf)).astype(BF16).astype(F32)
    real = jnp.concatenate([weighted[0:1, j * QUART : (j + 1) * QUART] for j in range(4)], axis=0)
    imag = jnp.concatenate([weighted[1:2, j * QUART : (j + 1) * QUART] for j in range(4)], axis=0)
    body = jnp.concatenate([real * cosine + imag * sine, imag * cosine - real * sine], axis=0)
    one = jnp.concatenate([body, meta], axis=1)
    pair = jnp.concatenate([one, one], axis=0).astype(BF16)
    for k in range(out_ref.shape[0] // 16):
        out_ref[16 * k : 16 * (k + 1), :] = pair


def tables_kernel(ctf_ref, noise_ref, tables_ref):
    def split(table):
        first = table.astype(BF16).astype(F32)
        second = (table - first).astype(BF16).astype(F32)
        return [first, second, table - first - second]

    noise = split(noise_ref[...])
    rows = split(ctf_ref[...]) + noise + [jnp.zeros_like(noise[0])]
    tables_ref[...] = jnp.concatenate(rows, axis=0).astype(BF16)


def refs_kernel(flat_ref, prior_ref, turned_ref, power_ref, column_ref, cos_ref, sin_ref):
    count = flat_ref.shape[0]
    width = 256
    cos_ref[...], sin_ref[...] = phases_y(0, PIX // 128)

    def body(step, carry):
        at = pl.ds(pl.multiple_of(step * width, width), width)
        low = flat_ref[:, at]
        high = flat_ref[:, pl.ds(pl.multiple_of(PIX + step * width, width), width)]
        real = low.astype(F32)
        imag = high.astype(F32)
        lines = [pl.ds(step * (width // 128) + k, 1) for k in range(width // 128)]
        cosine = jnp.concatenate([cos_ref[line, :] for line in lines], axis=1)
        sine = jnp.concatenate([sin_ref[line, :] for line in lines], axis=1)
        rc, rs, ic, si = real * cosine, real * sine, imag * cosine, imag * sine
        turned_ref[0, 0:count, at] = (rc + si).astype(BF16)
        turned_ref[1, 0:count, at] = (ic - rs).astype(BF16)
        turned_ref[0, count : 2 * count, at] = low
        turned_ref[1, count : 2 * count, at] = high
        turned_ref[0, 2 * count : 3 * count, at] = (rc - si).astype(BF16)
        turned_ref[1, 2 * count : 3 * count, at] = (ic + rs).astype(BF16)
        power_ref[:, at] = (real * real + imag * imag).astype(BF16)
        return carry

    lax.fori_loop(0, PIX // width, body, 0)
    line = lax.broadcasted_iota(jnp.int32, (count, count), 0)
    lane = lax.broadcasted_iota(jnp.int32, (count, count), 1)
    column = jnp.sum(jnp.where(lane == line, prior_ref[...], 0.0), axis=1, keepdims=True)
    column_ref[...] = jnp.broadcast_to(column, column_ref.shape)


def table_picks(group, focus):
    spot = lax.broadcasted_iota(jnp.int32, (group.shape[0], TABLE_ROWS), 1)
    ctf = (spot < 3 * DEFS) & (spot % DEFS == focus.astype(jnp.int32))
    noise = (spot >= 3 * DEFS) & (spot < 3 * (DEFS + GROUPS)) & (spot % GROUPS == group.astype(jnp.int32))
    return jnp.concatenate([ctf.astype(F32), noise.astype(F32)], axis=0).astype(BF16)


def ctf_power_rows(picks, tables):
    rows = lax.dot_general(picks, tables, NN, preferred_element_type=F32)
    count = rows.shape[0] // 2
    ctf, noise = rows[0:count], rows[count:]
    return (noise * ctf * ctf).astype(BF16)


def shift_x(real, imag, cosine, sine):
    rc, rs, ic, si = real * cosine, real * sine, imag * cosine, imag * sine
    return (rc - si, real, rc + si), (ic + rs, imag, ic - rs)


def unpack(parts, wide_ref):
    size = parts[0].shape[0]
    whole = size * len(parts)
    for spot, part in enumerate(parts):
        for tile in range(WIDE // 128):
            start = whole * tile + size * spot
            wide_ref[start : start + size, :] = part[:, 128 * tile : 128 * (tile + 1)].astype(F32)

    def chunk(row, first, count):
        tiles = [
            wide_ref[pl.ds(whole * tile + 8 * first + row, count, stride=8), :] for tile in range(QUART // 128)
        ]
        return jnp.concatenate(tiles, axis=1)

    def codes(first, count):
        return wide_ref[pl.ds(whole * (QUART // 128) + 8 * first, count, stride=8), :]

    return chunk, codes


def swap_lanes(row, step, flag):
    lane = lax.broadcasted_iota(jnp.int32, row.shape, 1)
    width = row.shape[1]
    other = jnp.where((lane & step) == 0, pltpu.roll(row, width - step, 1), pltpu.roll(row, step, 1))
    return jnp.where(flag == 1, other, row)


def quarter_kernel(place, own_ref, side_ref, flat_ref, q0_ref, q1_ref, q2_ref, q3_ref, wide_ref):
    outs = (q0_ref, q1_ref, q2_ref, q3_ref)
    count = 2 * own_ref.shape[0] // 8
    chunk, codes = unpack((own_ref, side_ref), wide_ref)
    meta = codes(0, count)
    both = jnp.concatenate([meta, meta], axis=0).astype(BF16)
    for k in range(4):
        part = place[0] ^ k
        outs[k][:, 0:QUART] = jnp.concatenate([chunk(part, 0, count), chunk(part + 4, 0, count)], axis=0).astype(BF16)
        outs[k][:, QUART:WIDE] = both


def score_kernel(
    place, own_ref, side_ref, far_ref, corner_ref, turned_ref, power_ref, tables_ref, column_ref,
    q0_ref, q1_ref, q2_ref, q3_ref, stats_ref, wide_ref,
):
    outs = (q0_ref, q1_ref, q2_ref, q3_ref)
    count = 4 * own_ref.shape[0] // 8
    half = count // 2
    refs = power_ref.shape[0]
    chunk, codes = unpack((own_ref, side_ref, far_ref, corner_ref), wide_ref)
    meta = codes(0, count)
    picks = table_picks(meta[:, 0:1], meta[:, 1:2])
    cos_x, sin_x = phases_x(QUART)
    cross = jnp.zeros((3 * refs, 3 * count), F32)
    self_term = jnp.zeros((refs, count), F32)
    for j in range(4):
        at = slice(j * QUART, (j + 1) * QUART)
        ctf_power = ctf_power_rows(picks, tables_ref[:, at])
        self_term += lax.dot_general(power_ref[:, at], ctf_power, NT, preferred_element_type=F32)
    for j in range(4):
        at = slice(j * QUART, (j + 1) * QUART)
        for c, parts in enumerate(shift_x(chunk(j, 0, count), chunk(j + 4, 0, count), cos_x, sin_x)):
            new = jnp.concatenate(parts, axis=0).astype(BF16)
            cross += lax.dot_general(turned_ref[c, :, at], new, NT, preferred_element_type=F32)
        part = place[0] ^ j
        late = jnp.concatenate([chunk(part, half, half), chunk(part + 4, half, half)], axis=0).astype(BF16)
        for side in range(2):
            outs[j][side * count : (side + 1) * count, 5 * refs : 5 * refs + QUART // 2] = late[
                :, side * QUART // 2 : (side + 1) * QUART // 2
            ]

    base = column_ref[:, 0:count] - 0.5 * self_term
    base_pair = jnp.concatenate([base, base], axis=1)
    turned_codes = meta.T
    centre_x, centre_y = turned_codes[2:3, :], turned_codes[3:4, :]

    def offset_term(a, b):
        off_x = centre_x + (2.0 * a - 2.0)
        off_y = centre_y + (2.0 * b - 2.0)
        return (off_x * off_x + off_y * off_y) / (2.0 * TRANS_VAR)

    pairs, singles = [], []
    for b in range(3):
        value = cross[b * refs : (b + 1) * refs]
        pairs.append(
            value[:, 0 : 2 * count] + base_pair - jnp.concatenate([offset_term(0, b), offset_term(1, b)], axis=1)
        )
        singles.append(value[:, 2 * count :] + base - offset_term(2, b))
    top_pair = jnp.max(jnp.maximum(jnp.maximum(pairs[0], pairs[1]), pairs[2]), axis=0, keepdims=True)
    top = jnp.max(jnp.maximum(jnp.maximum(singles[0], singles[1]), singles[2]), axis=0, keepdims=True)
    top = jnp.maximum(top, jnp.maximum(top_pair[:, 0:count], top_pair[:, count:]))
    top_pair = jnp.concatenate([top, top], axis=1)
    pairs = [jnp.exp(value - top_pair) for value in pairs]
    singles = [jnp.exp(value - top) for value in singles]
    mass_pair = jnp.sum(pairs[0] + pairs[1] + pairs[2], axis=0, keepdims=True)
    mass = jnp.sum(singles[0] + singles[1] + singles[2], axis=0, keepdims=True)
    mass = mass + mass_pair[:, 0:count] + mass_pair[:, count:]
    total = top + jnp.log(mass)
    row = jnp.concatenate([total, top], axis=1)
    row = swap_lanes(swap_lanes(row, half, place[2]), half // 2, place[3])
    stats_ref[...] = jnp.broadcast_to(row, stats_ref.shape)
    last = jnp.concatenate(singles[0:2], axis=1)
    notes = jnp.concatenate([meta[half:, 0:count], jnp.zeros((refs - half, count), F32)], axis=0)
    ends = jnp.concatenate([singles[2], notes], axis=1), jnp.concatenate([notes, singles[2]], axis=1)
    for k in range(4):
        for b in range(3):
            outs[k][:, b * refs : (b + 1) * refs] = pairs[b].astype(BF16)
        outs[k][:, 3 * refs : 4 * refs] = last.astype(BF16)
        outs[k][:, 4 * refs : 5 * refs] = ends[k % 2].astype(BF16)


def final_kernel(
    place, e0_ref, e1_ref, e2_ref, e3_ref, q0_ref, q1_ref, q2_ref, q3_ref, stats_ref, tables_ref,
    data_hbm, weight_hbm, evidence_ref, post_ref, sum_ref, power_ref, data_ref, weight_ref, sems, *, scale,
):
    dom, orient, y_hi, z_lo, mine = place[0], place[1], place[2], place[3], place[4]
    early = (e0_ref, e1_ref, e2_ref, e3_ref)
    boxes = (q0_ref, q1_ref, q2_ref, q3_ref)
    doms = 4
    count = q0_ref.shape[0] // 2
    half = count // 2
    refs = sum_ref.shape[0]
    pair = 2 * count
    orients = stats_ref.shape[0] // doms
    lane = lax.broadcasted_iota(jnp.int32, (1, pair), 1)
    left = lane < count
    upper = (lax.broadcasted_iota(jnp.int32, (orients, pair), 0) & 8) != 0
    factors, groups, foci = [], [], []
    for k in range(doms):
        start = dom ^ k ^ (2 * y_hi)
        table = jnp.where(
            upper,
            stats_ref[pl.ds(start ^ 2, orients, stride=doms), :],
            stats_ref[pl.ds(start, orients, stride=doms), :],
        )
        top = jnp.max(table, axis=0, keepdims=True)
        evidence = top + jnp.log(jnp.sum(jnp.exp(table - top), axis=0, keepdims=True))
        own = stats_ref[pl.ds(orient * doms + (dom ^ k), 1), :]
        factor = jnp.exp(pltpu.roll(own, count, 1) - evidence)
        factor = swap_lanes(swap_lanes(factor, half, y_hi), half // 2, z_lo)
        factors.append(jnp.where(left, factor, pltpu.roll(factor, count, 1)))
        if k == 0:
            evidence_ref[0] = jnp.sum(jnp.where(lane == mine, evidence, 0.0))
        notes = boxes[k][0:half, 4 * refs : 5 * refs].astype(F32)
        first = early[k][0:half, QUART:WIDE].astype(F32)
        spot = count if k % 2 == 0 else 0
        groups += [first[:, 0:1], notes[:, spot : spot + 1]]
        foci += [first[:, 1:2], notes[:, spot + 1 : spot + 2]]

    picks = table_picks(jnp.concatenate(groups, axis=0), jnp.concatenate(foci, axis=0))
    for n in range(4):
        at = slice(n * QUART // 4, (n + 1) * QUART // 4)
        start = pl.multiple_of(dom * QUART + n * QUART // 4, QUART // 4)
        power_ref[:, at] = ctf_power_rows(picks, tables_ref[:, pl.ds(start, QUART // 4)])

    def fill(pieces, spot):
        total = jnp.zeros((refs, pair), F32)
        for b in range(3):
            post = pieces[b].astype(BF16)
            post_ref[b * refs : (b + 1) * refs, spot : spot + pair] = post
            total = total + post.astype(F32)
        return total

    def block(k, number):
        return boxes[k][:, number * refs : (number + 1) * refs].astype(F32) * factors[k]

    totals = []
    for k in range(doms):
        total = fill([block(k, b) for b in range(3)], k * pair)
        totals.append(total + pltpu.roll(total, count, 1))
    for k in range(0, doms, 2):
        even, odd = block(k, 3), block(k + 1, 3)
        pieces = [
            jnp.where(left, even, pltpu.roll(odd, count, 1)),
            jnp.where(left, pltpu.roll(even, count, 1), odd),
            jnp.where(left, block(k, 4), block(k + 1, 4)),
        ]
        total = fill(pieces, (doms + k // 2) * pair) + jnp.where(left, totals[k], totals[k + 1])
        sum_ref[:, k * count : (k + 2) * count] = total.astype(BF16)

    weight_ref[...] = lax.dot_general(sum_ref[...], power_ref[...], NN, preferred_element_type=F32) * scale
    copies = [pltpu.make_async_copy(weight_ref, weight_hbm, sems.at[2])]
    copies[0].start()
    width = 512
    cos_x, sin_x = phases_x(width)
    cos_rows, sin_rows = phases_y(dom * QUART, QUART // 128)
    cos_rows, sin_rows = cos_rows * scale, sin_rows * scale
    for n in range(QUART // width):
        at = slice(n * width, (n + 1) * width)
        reals, imags = [], []
        side = 2 * n * width // QUART
        late_at = slice(5 * refs + n * width - side * QUART // 2, 5 * refs + (n + 1) * width - side * QUART // 2)
        for k in range(doms):
            late = boxes[k][side * count : (side + 1) * count, late_at].astype(F32)
            soon = early[k][:, at].astype(F32)
            real = jnp.concatenate([soon[0:half], late[0:half]], axis=0)
            imag = jnp.concatenate([soon[half:], late[half:]], axis=0)
            new_real, new_imag = shift_x(real, imag, cos_x, sin_x)
            reals.append([part.astype(BF16) for part in new_real])
            imags.append([part.astype(BF16) for part in new_imag])

        def stack(parts):
            first = [parts[k][a] for k in range(doms) for a in range(2)]
            return jnp.concatenate(first + [parts[k][2] for k in range(doms)], axis=0)

        sums_real = lax.dot_general(post_ref[...], stack(reals), NN, preferred_element_type=F32)
        sums_imag = lax.dot_general(post_ref[...], stack(imags), NN, preferred_element_type=F32)
        r0, r1, r2 = (sums_real[b * refs : (b + 1) * refs] for b in range(3))
        i0, i1, i2 = (sums_imag[b * refs : (b + 1) * refs] for b in range(3))
        lines = [n * (width // 128) + tile for tile in range(width // 128)]
        cos_y = jnp.concatenate([cos_rows[line : line + 1] for line in lines], axis=1)
        sin_y = jnp.concatenate([sin_rows[line : line + 1] for line in lines], axis=1)
        both = (
            r1 * scale + (r0 + r2) * cos_y + (i2 - i0) * sin_y,
            i1 * scale + (i0 + i2) * cos_y + (r0 - r2) * sin_y,
        )
        lines = 2 * width // 128
        for tile in range(width // 128):
            for c in range(2):
                data_ref[n, pl.ds(2 * tile + c, refs, stride=lines), :] = both[c][:, 128 * tile : 128 * (tile + 1)]
        copy = pltpu.make_async_copy(
            data_ref.at[n].reshape(refs, lines, 128), data_hbm.at[:, n * lines : (n + 1) * lines], sems.at[n]
        )
        copy.start()
        copies.append(copy)
    for copy in copies:
        copy.wait()


def on_device(images, offsets, groups, defocus, refs, log_prior, noise_inv, ctf_table):
    count_refs = refs.shape[0]
    size = {name: lax.axis_size(name) for name in AXES}
    orients = size["x"] * size["yh"] * size["zh"] * size["zl"]
    devices = orients * size["yl"] * size["c"]
    scale = 25.0 * (count_refs * orients) / devices
    at = {name: lax.axis_index(name) for name in AXES}
    dom = at["yl"] * size["c"] + at["c"]
    orient = ((at["x"] * size["yh"] + at["yh"]) * size["zh"] + at["zh"]) * size["zl"] + at["zl"]
    mine = ((at["yh"] * size["zl"] + at["zl"]) * size["x"] + at["x"]) * size["zh"] + at["zh"]
    place = jnp.stack([dom, orient, at["yh"], at["zl"], mine]).astype(jnp.int32)

    smem = pl.BlockSpec(memory_space=pltpu.SMEM)
    vmem = pl.BlockSpec(memory_space=pltpu.VMEM)
    hbm = pl.BlockSpec(memory_space=pltpu.HBM)
    shape = jax.ShapeDtypeStruct
    line = 8 * size["x"] * size["zh"]
    payload = pl.pallas_call(
        prep_kernel,
        in_specs=[smem] * 3 + [hbm] * 3,
        out_specs=vmem,
        out_shape=shape((line, WIDE), BF16),
        scratch_shapes=[
            pltpu.VMEM((1, 2, PIX), BF16),
            pltpu.VMEM((GROUPS, PIX), F32),
            pltpu.VMEM((8, PIX), F32),
            pltpu.SemaphoreType.DMA((3,)),
        ],
        compiler_params=params(VMEM_ALL),
        name="prep",
    )(jnp.transpose(offsets, (0, 2, 1))[0], groups, defocus, images, noise_inv, ctf_table)
    flip = [(i, 3 - i) for i in range(4)]
    own = lax.all_to_all(payload, ("x", "zh"), 0, 0, tiled=True)
    side = lax.ppermute(own, "zl", [(0, 1), (1, 0)])
    far = lax.ppermute(own, ("yh", "yl"), flip)

    flat = refs.reshape(count_refs, 2 * PIX)
    flat, ctf_late, noise_late = lax.optimization_barrier((flat, ctf_table, noise_inv))
    tables = pl.pallas_call(
        tables_kernel,
        in_specs=[vmem] * 2,
        out_specs=vmem,
        out_shape=shape((TABLE_ROWS, PIX), BF16),
        compiler_params=params(VMEM_LIMIT // 3),
        name="tables",
    )(ctf_late, noise_late)
    side, _, flat, tables = lax.optimization_barrier((side, far, flat, tables))
    corner = lax.ppermute(side, ("yh", "yl"), flip)

    early = pl.pallas_call(
        quarter_kernel,
        in_specs=[smem] + [vmem] * 3,
        out_specs=[vmem] * 4,
        out_shape=[shape((orients, WIDE), BF16)] * 4,
        scratch_shapes=[pltpu.VMEM((4 * orients * (WIDE // 128), 128), F32)],
        compiler_params=params(VMEM_LIMIT // 3),
        name="quarters",
    )(place, own, side, flat)

    def share(parts):
        moves = [[(d, d ^ k) for d in range(4)] for k in range(4)]
        sent = {k: lax.ppermute(parts[k], ("yl", "c"), moves[k]) for k in (2, 3, 1)}
        return parts[0:1] + [sent[k] for k in range(1, 4)]

    early = list(early)
    flat, early[0] = lax.optimization_barrier((flat, early[0]))
    turned, power, column = pl.pallas_call(
        refs_kernel,
        in_specs=[vmem] * 2,
        out_specs=[vmem] * 3,
        out_shape=[
            shape((2, 3 * count_refs, PIX), BF16),
            shape((count_refs, PIX), BF16),
            shape((count_refs, 128), F32),
        ],
        scratch_shapes=[pltpu.VMEM((PIX // 128, 128), F32)] * 2,
        compiler_params=params(),
        cost_estimate=pl.CostEstimate(flops=8 * count_refs * PIX, bytes_accessed=10 << 20, transcendentals=0),
        name="turn_refs",
    )(flat, log_prior[None, :])
    early = share(early)

    box = (2 * orients, 5 * count_refs + QUART // 2)
    *boxes, stats = pl.pallas_call(
        score_kernel,
        in_specs=[smem] + [vmem] * 8,
        out_specs=[vmem] * 5,
        out_shape=[shape(box, BF16)] * 4 + [shape((devices, 2 * orients), F32)],
        scratch_shapes=[pltpu.VMEM((8 * orients * (WIDE // 128), 128), F32)],
        compiler_params=params(),
        cost_estimate=pl.CostEstimate(
            flops=18 * orients * count_refs * 2 * PIX, bytes_accessed=10 << 20, transcendentals=0
        ),
        name="score",
    )(place, own, side, far, corner, turned, power, tables, column)

    boxes = list(boxes)
    early, stats = lax.optimization_barrier((early, stats))
    boxes = share(boxes)
    stats_all = lax.all_to_all(stats, AXES, 0, 0, tiled=True)

    data, weight, evidence = pl.pallas_call(
        functools.partial(final_kernel, scale=scale),
        in_specs=[smem] + [vmem] * 10,
        out_specs=[hbm, hbm, smem],
        scratch_shapes=[
            pltpu.VMEM((3 * count_refs, 12 * orients), BF16),
            pltpu.VMEM((count_refs, 4 * orients), BF16),
            pltpu.VMEM((4 * orients, QUART), BF16),
            pltpu.VMEM((2, count_refs * (QUART // 128), 128), F32),
            pltpu.VMEM((count_refs, QUART), F32),
            pltpu.SemaphoreType.DMA((3,)),
        ],
        out_shape=[
            shape((count_refs, 2 * (QUART // 128), 128), F32),
            shape((count_refs, QUART), F32),
            shape((1,), F32),
        ],
        compiler_params=params(),
        name="insert",
    )(place, *early, *boxes, stats_all, tables)
    data = jnp.transpose(data.reshape(count_refs, QUART // 128, 2, 128), (0, 2, 1, 3))
    return data.reshape(count_refs, 2, QUART), weight, evidence


def solution(mesh):
    fine = Mesh(mesh.devices.reshape(4, 2, 4, 2, 2, 2), AXES)
    orient = AXES[0:4]
    dom = AXES[4:6]
    return jax.shard_map(
        on_device,
        mesh=fine,
        in_specs=(
            P(AXES, None, None),
            P(AXES, None, None),
            P(AXES),
            P(AXES),
            P(orient, None, None),
            P(orient),
            P(),
            P(),
        ),
        out_specs=(P(orient, None, dom), P(orient, dom), P(AXES)),
        check_vma=False,
    )
```
